32 devices in a mesh: particle: 8 (over z, x), token: 4 (over y, core).
Axes of the slice: x: 2, y: 2, z: 4, core: 2. Of those that a mesh axis runs over, the one named last changes fastest.
Arguments:
- states: bfloat16 [16, 256, 768], P('particle', 'token'), may hold values from -6 to 6
- ancestors: int32 [16], P('particle'), may hold values from 0 to 15, as said below
- pair_bias: bfloat16 [16, 256, 256], P(None, 'token'), may hold values from -3 to 300, as said below
- key_mask: int32 [256], replicated, may hold values from 0 to 1, as said below
- gain_attn: float32 [768], replicated, may hold values from 0.1 to 1.9
- w_qkv: bfloat16 [768, 2304], replicated, may hold values from -0.21875 to 0.21875
- w_o: bfloat16 [768, 768], replicated, may hold values from -0.21875 to 0.21875
- gain_ff: float32 [768], replicated, may hold values from 0.1 to 1.9
- w_in: bfloat16 [2, 768, 1536], P(None, 'particle'), may hold values from -0.21875 to 0.21875
- w_out: bfloat16 [768, 1536], P('particle'), may hold values from -0.15625 to 0.15625
Outputs:
- new_states: bfloat16 [16, 256, 768], P('particle', 'token')
The draws below stay inside these ranges and needn't reach their ends.
Inputs may be any that keep to these rules, and one draw needn't show every extreme that they name: `ancestors`: any particle may be the ancestor of any number of particles. `pair_bias`: real values; rows of some heads may hold a few large entries. `key_mask`: 1 on a prefix of 128 or more tokens and 0 after it; the last token is always 0.
All inputs are finite; a program needn't handle non-finite values.
Results may differ from the reference program's by a relative error of at most 0.0085.
Values may be sent and summed in bfloat16 or wider, within the bound.
A program may use at most 64 MiB of HBM per device.

```python
import math
import jax
import jax.numpy as jnp
from jax import lax

D = 768
HEADS = 16
FF = 1536
PART_DEV = 2
LEN = 256
PARTICLES = 16


def draw_ancestors(key, part):
    key = jax.random.fold_in(key, 7)
    key_prev, key_common, key_which, key_any, key_coin = jax.random.split(key, 5)
    index = jnp.arange(PARTICLES, dtype=jnp.int32)
    groups = PARTICLES // PART_DEV
    device = index // PART_DEV
    previous = (device - 1) % groups * PART_DEV + jax.random.randint(key_prev, (PARTICLES,), 0, PART_DEV)
    previous = jnp.where(index == 0, PARTICLES - 1, previous)
    previous = jnp.where(index == PART_DEV, 0, previous)
    common = jax.random.randint(key_common, (4,), 0, PARTICLES)
    common_pick = common[jax.random.randint(key_which, (PARTICLES,), 0, 4)]
    anywhere = jax.random.randint(key_any, (PARTICLES,), 0, PARTICLES)
    coin = jax.random.randint(key_coin, (PARTICLES,), 0, 2)
    other = jnp.where(coin == 0, common_pick, anywhere)
    return jnp.where(index % PART_DEV == 0, previous, other).astype(jnp.int32)


def draw_pair_bias(key, part):
    key = jax.random.fold_in(key, 11)
    key_base = jax.random.fold_in(key, 0)
    base = jnp.clip(jax.random.normal(key_base, (HEADS, LEN, LEN), jnp.float32), -3.0, 3.0)
    return base.astype(jnp.bfloat16)


def draw_key_mask(key, part):
    key = jax.random.fold_in(key, 5)
    length = jax.random.randint(key, (), LEN // 2, LEN)
    return (jnp.arange(LEN) < length).astype(jnp.int32)


def levels(rng, dims, shards, least, top_value):
    level = 1.0
    for position, blocks in shards:
        heights = jax.random.uniform(jax.random.fold_in(jax.random.fold_in(rng, 6), position), (blocks,), jnp.float32, least / len(shards), top_value / len(shards))
        level = level * jnp.repeat(jnp.exp(heights), dims[position] // blocks).reshape((-1,) + (1,) * (len(dims) - 1 - position))
    return level


def normal_values(stream_key, shape, spread, bound, shards=(), kind=jnp.bfloat16):
    entries = jax.random.normal(stream_key, shape, jnp.float32) * spread
    if len(shards) > 0:
        entries = levels(stream_key, shape, shards, -0.22, 0.18) * entries
    return jnp.clip(entries, min=-bound, max=bound).astype(kind)


def setup_inputs(seed: int = 0) -> dict:
    seeds = jax.random.split(jax.random.key(seed), 11)
    states = normal_values(seeds[0], (PARTICLES, LEN, D), 1.0, 6.0, ((0, 8), (1, 4)))
    ancestors = draw_ancestors(jax.random.fold_in(seeds[10], 71), 0)
    pair_bias = draw_pair_bias(jax.random.fold_in(seeds[10], 71), 0)
    key_mask = draw_key_mask(jax.random.fold_in(seeds[10], 71), 0)
    gain_attn = jnp.clip(1.0 + 0.18 * jax.random.normal(seeds[4], (D,), jnp.float32), 0.1, 1.9)
    w_qkv = normal_values(seeds[5], (D, 3 * D), D ** -0.5, 0.21875)
    w_o = normal_values(seeds[6], (D, D), D ** -0.5, 0.21875)
    gain_ff = jnp.clip(1.0 + 0.18 * jax.random.normal(seeds[7], (D,), jnp.float32), 0.1, 1.9)
    w_in = normal_values(seeds[8], (2, D, FF), D ** -0.5, 0.21875, ((1, 8),))
    w_out = normal_values(seeds[9], (D, FF), FF ** -0.5, 0.15625, ((0, 8),))
    return dict(states=states, ancestors=ancestors, pair_bias=pair_bias, key_mask=key_mask, gain_attn=gain_attn, w_qkv=w_qkv, w_o=w_o, gain_ff=gain_ff, w_in=w_in, w_out=w_out)


def rms_norm(stream, gain_vec):
    return stream * lax.rsqrt(lax.optimization_barrier(jnp.mean(stream * stream, axis=-1, keepdims=True)) + 1e-05) * gain_vec

def one_particle(particle_state, pair_bias, key_mask, gain_attn, w_qkv, w_o, gain_ff, w_in, w_out):
    head_size = D // HEADS
    stream = particle_state.astype(jnp.float32)
    normed = rms_norm(stream, gain_attn).astype(jnp.bfloat16)
    projected = jnp.dot(normed, w_qkv, preferred_element_type=jnp.float32)
    queries = (projected[:, :D] * (1.0 / math.sqrt(head_size))).astype(jnp.bfloat16)
    keys = projected[:, D:2 * D].astype(jnp.bfloat16)
    values = projected[:, 2 * D:].astype(jnp.bfloat16)
    usable = (key_mask > 0)[None, :]
    query_heads = queries.reshape(LEN, HEADS, head_size).transpose(1, 0, 2)
    key_heads = keys.reshape(LEN, HEADS, head_size).transpose(1, 0, 2)
    value_heads = values.reshape(LEN, HEADS, head_size).transpose(1, 0, 2)

    def one_head(head_items):
        query_head, key_head, value_head, bias_head = head_items
        scores = jnp.dot(query_head, key_head.T, preferred_element_type=jnp.float32) + bias_head.astype(jnp.float32)
        row_max = lax.optimization_barrier(jnp.max(jnp.where(usable, scores, -1e+30), axis=1, keepdims=True))
        weights = jnp.where(usable, jnp.exp(scores - row_max), 0.0)
        row_total = lax.optimization_barrier(jnp.sum(weights, axis=1, keepdims=True))
        mixture = jnp.dot(weights.astype(jnp.bfloat16), value_head, preferred_element_type=jnp.float32)
        return mixture / row_total
    head_out = lax.map(one_head, (query_heads, key_heads, value_heads, pair_bias))
    attended = head_out.transpose(1, 0, 2).reshape(LEN, D).astype(jnp.bfloat16)
    stream = stream + jnp.dot(attended, w_o, preferred_element_type=jnp.float32)
    normed_ff = rms_norm(stream, gain_ff).astype(jnp.bfloat16)
    gate_term = jnp.dot(normed_ff, w_in[0], preferred_element_type=jnp.float32)
    up_term = jnp.dot(normed_ff, w_in[1], preferred_element_type=jnp.float32)
    hidden = (jax.nn.silu(gate_term) * up_term).astype(jnp.bfloat16)
    update = lax.dot_general(hidden, w_out, (((1,), (1,)), ((), ())), preferred_element_type=jnp.float32)
    return (stream + update).astype(jnp.bfloat16)

def reference(states, ancestors, pair_bias, key_mask, gain_attn, w_qkv, w_o, gain_ff, w_in, w_out):
    chosen = jnp.take(states, ancestors.astype(jnp.int32), axis=0)

    def run_one(particle_state):
        return one_particle(particle_state, pair_bias, key_mask, gain_attn, w_qkv, w_o, gain_ff, w_in, w_out)
    return lax.map(run_one, chosen)
```

```python
import math

import jax
import jax.numpy as jnp
from jax import lax
from jax.experimental import pallas as pl
from jax.experimental.pallas import tpu as pltpu
from jax.sharding import PartitionSpec as P

MESH = pl.DeviceIdType.MESH


def rms_norm(stream, gain_vec):
    return stream * lax.rsqrt(jnp.mean(stream * stream, axis=-1, keepdims=True) + 1e-05) * gain_vec


def attend_portion(running_sum, queries, key_part, value_part, pair_bias, key_mask):
    running, totals, summed = running_sum
    part_count, row_count, model_width = queries.shape
    head_count = pair_bias.shape[0]
    head_size = model_width // head_count
    number = key_part.shape[1]
    query_heads = queries.reshape(part_count, row_count, head_count, head_size)
    key_heads = key_part.reshape(part_count, number, head_count, head_size)
    value_heads = value_part.reshape(part_count, number, head_count, head_size)
    scores = jnp.einsum(
        "prhe,pnhe->phrn", query_heads, key_heads, preferred_element_type=jnp.float32
    )
    bias_part = pair_bias.astype(jnp.float32)
    scores = scores + bias_part[None]
    usable = (key_mask > 0)[None, None, None, :]
    new_max = jnp.maximum(running, jnp.max(jnp.where(usable, scores, -1e30), axis=3))
    weights = jnp.where(usable, jnp.exp(scores - new_max[..., None]), 0.0)
    totals = jnp.sum(weights, axis=3)
    summed = jnp.einsum(
        "phrn,pnhe->phre",
        weights.astype(jnp.bfloat16),
        value_heads,
        preferred_element_type=jnp.float32,
    )
    return (new_max, totals, summed)


def run_block(states, pair_bias, key_mask, gain_attn, w_qkv, w_o, gain_ff, w_in, w_out):
    part_count, row_count, model_width = states.shape
    head_count = pair_bias.shape[0]
    head_size = model_width // head_count
    score_scale = 1.0 / math.sqrt(head_size)
    stream = states.astype(jnp.float32)
    normed = rms_norm(stream, gain_attn).astype(jnp.bfloat16)
    start_carry = (
        jnp.full((part_count, head_count, row_count), -1e30, jnp.float32),
        jnp.zeros((part_count, head_count, row_count), jnp.float32),
        jnp.zeros((part_count, head_count, row_count, head_size), jnp.float32),
    )
    queries = (
        jnp.einsum(
            "prd,de->pre", normed, w_qkv[:, :model_width], preferred_element_type=jnp.float32
        )
        * score_scale
    ).astype(jnp.bfloat16)
    normed_all = lax.all_gather(normed, "token", axis=1, tiled=True)
    projected = jnp.einsum(
        "prd,de->pre", normed_all, w_qkv[:, model_width:], preferred_element_type=jnp.float32
    ).astype(jnp.bfloat16)
    portion = (projected[..., :model_width], projected[..., model_width:])
    running, totals, summed = attend_portion(
        start_carry, queries, portion[0], portion[1], pair_bias, key_mask
    )
    attended = (
        (summed / totals[..., None])
        .transpose(0, 2, 1, 3)
        .reshape(part_count, row_count, model_width)
        .astype(jnp.bfloat16)
    )
    stream = stream + jnp.einsum("prd,de->pre", attended, w_o, preferred_element_type=jnp.float32)
    normed_ff = rms_norm(stream, gain_ff).astype(jnp.bfloat16)
    normed_ff = lax.all_gather(normed_ff, "token", axis=1, tiled=True)
    gate_sum = jnp.einsum("prd,df->prf", normed_ff, w_in[0], preferred_element_type=jnp.float32)
    up_sum = jnp.einsum("prd,df->prf", normed_ff, w_in[1], preferred_element_type=jnp.float32)
    hidden = (jax.nn.silu(gate_sum) * up_sum).astype(jnp.bfloat16)
    update = jnp.einsum(
        "prf,nf->prn", hidden, w_out, preferred_element_type=jnp.float32
    ).astype(jnp.bfloat16)
    update = lax.psum_scatter(update, "token", scatter_dimension=1, tiled=True)
    return (stream + update.astype(jnp.float32)).astype(jnp.bfloat16)


def select_rows(ancestors, portion):
    number = portion.shape[0]
    indices = lax.iota(jnp.int32, number)
    onehot = (ancestors[:, None] == indices[None, :]).astype(jnp.bfloat16)
    return jnp.einsum("jp,prd->jrd", onehot, portion, preferred_element_type=jnp.float32)


def body(states, ancestors, pair_bias, key_mask, gain_attn, w_qkv, w_o, gain_ff, w_in, w_out):
    chosen = select_rows(ancestors, lax.all_gather(states, "particle", axis=0, tiled=True)).astype(
        jnp.bfloat16
    )
    units = w_out.shape[1] // lax.axis_size("token")
    first = lax.axis_index("token") * units
    w_in = lax.all_gather(
        lax.dynamic_slice_in_dim(w_in, first, units, 2), "particle", axis=1, tiled=True
    )
    w_out = lax.all_gather(
        lax.dynamic_slice_in_dim(w_out, first, units, 1), "particle", axis=0, tiled=True
    )
    return run_block(chosen, pair_bias, key_mask, gain_attn, w_qkv, w_o, gain_ff, w_in, w_out)


def block_kernel(
    states_ref, ancestors_ref, bias_hbm, mask_ref, gain_attn_ref, w_qkv_hbm, w_o_hbm, gain_ff_ref,
    w_in_hbm, w_out_hbm, out_ref,
    states_all, w_in_all, w_out_all, w_qkv, w_o, bias, normed_all, kv_all, ff_all,
    core_out, core_in, row_out, row_in,
    local_sem, recv_sem, right_sem, left_sem, across_sem, gather_recv, gather_row, gather_core,
    core_send, core_recv, row_send, row_recv,
):
    per, rows, width = states_ref.shape
    groups = lax.axis_size("particle")
    lines = groups // 2
    cells = lax.axis_size("token")
    spans = cells // 2
    units = w_in_all.shape[-1]
    head_count = bias.shape[0] // rows
    head_size = width // head_count
    me = lax.axis_index("particle")
    spot = lax.axis_index("token")
    line, side = me // 2, me % 2
    span, core = spot // 2, spot % 2
    across = (line * 2 + 1 - side, spot)
    above, below = (me + 2, spot), (me - 2, spot)
    other_core = (me, span * 2 + 1 - core)

    def span_peer(step):
        return lax.rem(span + step, spans)

    barrier = pltpu.get_barrier_semaphore()

    def greet(device):
        pl.semaphore_signal(barrier, inc=1, device_id=device, device_id_type=MESH)

    greet(across)
    greet(other_core)
    for step in range(1, spans):
        greet((me, span_peer(step) * 2 + core))

    @pl.when(line > 0)
    def _():
        greet(below)

    @pl.when(line < lines - 1)
    def _():
        greet(above)

    first = pl.multiple_of(spot * units, 128)
    locals_ = [
        pltpu.make_async_copy(states_ref, states_all.at[pl.ds(me * per, per)], local_sem.at[0]),
        pltpu.make_async_copy(
            w_in_hbm.at[:, :, pl.ds(first, units)], w_in_all.at[me], local_sem.at[1]
        ),
        pltpu.make_async_copy(
            w_out_hbm.at[:, pl.ds(first, units)], w_out_all.at[me], local_sem.at[2]
        ),
        pltpu.make_async_copy(w_qkv_hbm, w_qkv, local_sem.at[3]),
        pltpu.make_async_copy(bias_hbm, bias, local_sem.at[4]),
        pltpu.make_async_copy(w_o_hbm, w_o, local_sem.at[5]),
    ]
    for copy in locals_:
        copy.start()
    locals_[0].wait()
    pl.semaphore_wait(
        barrier,
        2 + spans - 1 + jnp.where(line > 0, 1, 0) + jnp.where(line < lines - 1, 1, 0),
    )

    views = (
        lambda k: states_all.at[pl.ds(k * per, per)],
        lambda k: w_in_all.at[k],
        lambda k: w_out_all.at[k],
    )

    def remote(kind, source, sems, device):
        k = source * 2 + side
        return pltpu.make_async_remote_copy(
            src_ref=views[kind](k),
            dst_ref=views[kind](k),
            send_sem=sems.at[kind, source],
            recv_sem=recv_sem.at[kind, k],
            device_id=device,
            device_id_type=MESH,
        )

    def arrived(kind, k):
        pltpu.make_async_remote_copy(
            src_ref=views[kind](k),
            dst_ref=views[kind](k),
            send_sem=across_sem.at[kind, 0],
            recv_sem=recv_sem.at[kind, k],
            device_id=across,
            device_id_type=MESH,
        ).wait_recv()

    def relay(kind, step):
        low, high = line - step, line + step

        @pl.when(low >= 0)
        def _():
            if step > 0:
                arrived(kind, low * 2 + side)

            @pl.when(line < lines - 1)
            def _():
                remote(kind, low, right_sem, above).start()

        @pl.when(high < lines)
        def _():
            if step > 0:
                arrived(kind, high * 2 + side)

            @pl.when(line > 0)
            def _():
                remote(kind, high, left_sem, below).start()

        @pl.when(low >= 0)
        def _():
            remote(kind, low, across_sem, across).start()

        if step > 0:

            @pl.when(high < lines)
            def _():
                remote(kind, high, across_sem, across).start()

    def finish(kind):
        for source in range(lines):
            arrived(kind, source * 2 + 1 - side)

    def drain(kind):
        for source in range(lines):
            remote(kind, source, across_sem, across).wait_send()

            @pl.when(jnp.logical_and(line < lines - 1, source <= line))
            def _():
                remote(kind, source, right_sem, above).wait_send()

            @pl.when(jnp.logical_and(line > 0, source >= line))
            def _():
                remote(kind, source, left_sem, below).wait_send()

    def slot_copy(which, buf, slot, send, device):
        return pltpu.make_async_remote_copy(
            src_ref=buf.at[slot],
            dst_ref=buf.at[slot],
            send_sem=send,
            recv_sem=gather_recv.at[which, slot],
            device_id=device,
            device_id_type=MESH,
        )

    def token_sends(which, buf):
        copies = [
            slot_copy(
                which, buf, spot, gather_row.at[which, step], (me, span_peer(step) * 2 + core)
            )
            for step in range(1, spans)
        ]
        copies.append(slot_copy(which, buf, spot, gather_core.at[which, 0], other_core))
        for copy in copies:
            copy.start()
        return copies

    def token_forward(which, buf):
        copies = []
        for step in range(1, spans):
            slot = span_peer(step) * 2 + core
            copy = slot_copy(which, buf, slot, gather_core.at[which, step], other_core)
            copy.wait_recv()
            copy.start()
            copies.append(copy)
        for step in range(spans):
            slot = span_peer(step) * 2 + 1 - core
            slot_copy(which, buf, slot, gather_core.at[which, 0], other_core).wait_recv()
        return copies

    def norm(stream, gain):
        mean = jnp.mean(stream * stream, axis=-1, keepdims=True)
        return (stream * lax.rsqrt(mean + 1e-05) * gain).astype(jnp.bfloat16)

    def dot(a, b):
        return jnp.dot(a, b, preferred_element_type=jnp.float32)

    def dot_t(a, b):
        return lax.dot_general(
            a, b, (((1,), (1,)), ((), ())), preferred_element_type=jnp.float32
        )

    relay(0, 0)
    locals_[1].wait()
    relay(0, 1)
    relay(1, 0)
    relay(0, 2) if lines > 2 else None
    for step in range(3, lines):
        relay(0, step)
    locals_[2].wait()
    relay(2, 0)
    finish(0)

    stream = jnp.concatenate(
        [states_all[ancestors_ref[j]].astype(jnp.float32) for j in range(per)], axis=0
    )
    normed = norm(stream, gain_attn_ref[...])
    normed_all[spot] = normed
    sent = token_sends(0, normed_all)
    if lines > 1:
        relay(1, 1)
    locals_[3].wait()
    scale = 1.0 / math.sqrt(head_size)
    queries = (dot(normed, w_qkv[:, :width]) * scale).astype(jnp.bfloat16)
    sent += token_forward(0, normed_all)
    if lines > 1:
        relay(2, 1)
    kv_all[...] = dot(
        normed_all[...].reshape(cells * per * rows, width), w_qkv[:, width:]
    ).astype(jnp.bfloat16)
    if lines > 2:
        relay(1, 2)
    locals_[4].wait()
    usable = mask_ref[...] > 0
    half = 8
    strip = half * head_size
    lane = lax.broadcasted_iota(jnp.int32, (half, 1, strip), 2)
    head = lax.broadcasted_iota(jnp.int32, (half, 1, strip), 0)
    mine = jnp.logical_and(lane >= head * head_size, lane < (head + 1) * head_size)
    mine_bf = mine.astype(jnp.float32).astype(jnp.bfloat16)
    mine_f = mine.astype(jnp.float32)
    mixed = []
    for j in range(per):
        strips = []
        for part in range(head_count // half):
            cols = slice(part * strip, (part + 1) * strip)
            q = queries[j * rows : (j + 1) * rows, cols]
            spread = (q[None] * mine_bf).reshape(half * rows, strip)

            def tokens_of(base):
                return jnp.concatenate(
                    [
                        kv_all[
                            (t * per + j) * rows : (t * per + j + 1) * rows,
                            base + part * strip : base + (part + 1) * strip,
                        ]
                        for t in range(cells)
                    ],
                    axis=0,
                )

            scores = dot_t(spread, tokens_of(0)) + bias[
                part * half * rows : (part + 1) * half * rows, :
            ].astype(jnp.float32)
            scores = jnp.where(usable, scores, -1e30)
            top = jnp.max(scores, axis=1, keepdims=True)
            weights = jnp.where(usable, jnp.exp(scores - top), 0.0)
            total = jnp.sum(weights, axis=1, keepdims=True)
            mix = dot(weights.astype(jnp.bfloat16), tokens_of(width)) / total
            strips.append(jnp.sum(mix.reshape(half, rows, strip) * mine_f, axis=0))
        mixed.append(jnp.concatenate(strips, axis=1))
    attended = jnp.concatenate(mixed, axis=0).astype(jnp.bfloat16)
    if lines > 2:
        relay(2, 2)
    locals_[5].wait()
    stream = stream + dot(attended, w_o[...])
    ff_all[spot] = norm(stream, gain_ff_ref[...])
    sent += token_sends(1, ff_all)
    for step in range(3, lines):
        relay(1, step)
        relay(2, step)
    sent += token_forward(1, ff_all)
    finish(1)
    normed_ff = ff_all[...].reshape(cells * per * rows, width)
    gate = dot(normed_ff, w_in_all[:, 0].reshape(width, units))
    up = dot(normed_ff, w_in_all[:, 1].reshape(width, units))
    hidden = (gate / (1.0 + jnp.exp(-gate)) * up).astype(jnp.bfloat16)
    finish(2)
    update = dot_t(hidden, w_out_all[...].reshape(width, units))
    update = update.reshape(spans, 2, per * rows, width)
    is_low = core == 0
    core_out[...] = jnp.where(is_low, update[:, 1], update[:, 0]).astype(jnp.bfloat16)
    copy = pltpu.make_async_remote_copy(
        src_ref=core_out,
        dst_ref=core_in,
        send_sem=core_send,
        recv_sem=core_recv,
        device_id=other_core,
        device_id_type=MESH,
    )
    copy.start()
    kept = jnp.where(is_low, update[:, 0], update[:, 1])
    copy.wait_recv()
    sent.append(copy)
    row_out[...] = (kept + core_in[...].astype(jnp.float32)).astype(jnp.bfloat16)
    rowed = []
    for step in range(1, spans):
        copy = pltpu.make_async_remote_copy(
            src_ref=row_out.at[span_peer(step)],
            dst_ref=row_in.at[step],
            send_sem=row_send.at[step],
            recv_sem=row_recv.at[step],
            device_id=(me, span_peer(step) * 2 + core),
            device_id_type=MESH,
        )
        copy.start()
        rowed.append(copy)
    stream = stream + row_out[span].astype(jnp.float32)
    for step, copy in enumerate(rowed, 1):
        copy.wait_recv()
        stream = stream + row_in[step].astype(jnp.float32)
    out_ref[...] = stream.astype(jnp.bfloat16).reshape(per, rows, width)
    for copy in sent + rowed:
        copy.wait_send()
    for kind in range(3):
        drain(kind)


def fused_body(
    states, ancestors, pair_bias, key_mask, gain_attn, w_qkv, w_o, gain_ff, w_in, w_out
):
    per, rows, width = states.shape
    groups, cells = lax.axis_size("particle"), lax.axis_size("token")
    lines, spans = groups // 2, cells // 2
    units = w_out.shape[1] // cells
    depth = w_in.shape[1]
    heads, _, keys = pair_bias.shape
    vmem = pl.BlockSpec(memory_space=pltpu.VMEM)
    smem = pl.BlockSpec(memory_space=pltpu.SMEM)
    hbm = pl.BlockSpec(memory_space=pl.ANY)
    dma = pltpu.SemaphoreType.DMA
    bf16 = jnp.bfloat16
    block = (per * rows, width)
    return pl.pallas_call(
        block_kernel,
        out_shape=jax.ShapeDtypeStruct(states.shape, bf16),
        in_specs=[vmem, smem, hbm, vmem, vmem, hbm, hbm, vmem, hbm, hbm],
        out_specs=vmem,
        scratch_shapes=[
            pltpu.VMEM((groups * per, rows, width), bf16),
            pltpu.VMEM((groups, 2, depth, units), bf16),
            pltpu.VMEM((groups, depth, units), bf16),
            pltpu.VMEM(w_qkv.shape, bf16),
            pltpu.VMEM(w_o.shape, bf16),
            pltpu.VMEM((heads * rows, keys), bf16),
            pltpu.VMEM((cells,) + block, bf16),
            pltpu.VMEM((cells * per * rows, 2 * width), bf16),
            pltpu.VMEM((cells,) + block, bf16),
            pltpu.VMEM((spans,) + block, bf16),
            pltpu.VMEM((spans,) + block, bf16),
            pltpu.VMEM((spans,) + block, bf16),
            pltpu.VMEM((spans,) + block, bf16),
            dma((6,)),
            dma((3, groups)),
            dma((3, lines)),
            dma((3, lines)),
            dma((3, lines)),
            dma((2, cells)),
            dma((2, spans)),
            dma((2, spans)),
            dma,
            dma,
            dma((spans,)),
            dma((spans,)),
        ],
        compiler_params=pltpu.CompilerParams(
            collective_id=0, has_side_effects=True, vmem_limit_bytes=56 * 1024 * 1024
        ),
    )(
        states,
        ancestors,
        pair_bias.reshape(heads * rows, keys),
        key_mask.reshape(1, keys),
        gain_attn.reshape(1, width),
        w_qkv,
        w_o,
        gain_ff.reshape(1, width),
        w_in,
        w_out,
    )


def either_body(states, ancestors, pair_bias, key_mask, gain_attn, w_qkv, w_o, gain_ff, w_in, w_out):
    tiles = w_in.shape[1] % 16 == 0 and (w_out.shape[1] // lax.axis_size("token")) % 128 == 0
    run = fused_body if tiles else body
    return run(
        states, ancestors, pair_bias, key_mask, gain_attn, w_qkv, w_o, gain_ff, w_in, w_out
    )


def solution(mesh):
    placed = (
        P("particle", "token", None),
        P("particle"),
        P(None, "token", None),
        P(),
        P(),
        P(),
        P(),
        P(),
        P(None, "particle", None),
        P("particle", None),
    )
    return jax.shard_map(
        either_body, mesh=mesh, in_specs=placed, out_specs=P("particle", "token", None), check_vma=False
    )
```

```python
import math

import jax
import jax.numpy as jnp
from jax import lax
from jax.experimental import pallas as pl
from jax.experimental.pallas import tpu as pltpu
from jax.sharding import PartitionSpec as P

MESH = pl.DeviceIdType.MESH


def rms_norm(stream, gain_vec):
    return stream * lax.rsqrt(jnp.mean(stream * stream, axis=-1, keepdims=True) + 1e-05) * gain_vec


def attend_portion(running_sum, queries, key_part, value_part, pair_bias, key_mask):
    running, totals, summed = running_sum
    part_count, row_count, model_width = queries.shape
    head_count = pair_bias.shape[0]
    head_size = model_width // head_count
    number = key_part.shape[1]
    query_heads = queries.reshape(part_count, row_count, head_count, head_size)
    key_heads = key_part.reshape(part_count, number, head_count, head_size)
    value_heads = value_part.reshape(part_count, number, head_count, head_size)
    scores = jnp.einsum(
        "prhe,pnhe->phrn", query_heads, key_heads, preferred_element_type=jnp.float32
    )
    bias_part = pair_bias.astype(jnp.float32)
    scores = scores + bias_part[None]
    usable = (key_mask > 0)[None, None, None, :]
    new_max = jnp.maximum(running, jnp.max(jnp.where(usable, scores, -1e30), axis=3))
    weights = jnp.where(usable, jnp.exp(scores - new_max[..., None]), 0.0)
    totals = jnp.sum(weights, axis=3)
    summed = jnp.einsum(
        "phrn,pnhe->phre",
        weights.astype(jnp.bfloat16),
        value_heads,
        preferred_element_type=jnp.float32,
    )
    return (new_max, totals, summed)


def run_block(states, pair_bias, key_mask, gain_attn, w_qkv, w_o, gain_ff, w_in, w_out):
    part_count, row_count, model_width = states.shape
    head_count = pair_bias.shape[0]
    head_size = model_width // head_count
    score_scale = 1.0 / math.sqrt(head_size)
    stream = states.astype(jnp.float32)
    normed = rms_norm(stream, gain_attn).astype(jnp.bfloat16)
    start_carry = (
        jnp.full((part_count, head_count, row_count), -1e30, jnp.float32),
        jnp.zeros((part_count, head_count, row_count), jnp.float32),
        jnp.zeros((part_count, head_count, row_count, head_size), jnp.float32),
    )
    queries = (
        jnp.einsum(
            "prd,de->pre", normed, w_qkv[:, :model_width], preferred_element_type=jnp.float32
        )
        * score_scale
    ).astype(jnp.bfloat16)
    normed_all = lax.all_gather(normed, "token", axis=1, tiled=True)
    projected = jnp.einsum(
        "prd,de->pre", normed_all, w_qkv[:, model_width:], preferred_element_type=jnp.float32
    ).astype(jnp.bfloat16)
    portion = (projected[..., :model_width], projected[..., model_width:])
    running, totals, summed = attend_portion(
        start_carry, queries, portion[0], portion[1], pair_bias, key_mask
    )
    attended = (
        (summed / totals[..., None])
        .transpose(0, 2, 1, 3)
        .reshape(part_count, row_count, model_width)
        .astype(jnp.bfloat16)
    )
    stream = stream + jnp.einsum("prd,de->pre", attended, w_o, preferred_element_type=jnp.float32)
    normed_ff = rms_norm(stream, gain_ff).astype(jnp.bfloat16)
    normed_ff = lax.all_gather(normed_ff, "token", axis=1, tiled=True)
    gate_sum = jnp.einsum("prd,df->prf", normed_ff, w_in[0], preferred_element_type=jnp.float32)
    up_sum = jnp.einsum("prd,df->prf", normed_ff, w_in[1], preferred_element_type=jnp.float32)
    hidden = (jax.nn.silu(gate_sum) * up_sum).astype(jnp.bfloat16)
    update = jnp.einsum(
        "prf,nf->prn", hidden, w_out, preferred_element_type=jnp.float32
    ).astype(jnp.bfloat16)
    update = lax.psum_scatter(update, "token", scatter_dimension=1, tiled=True)
    return (stream + update.astype(jnp.float32)).astype(jnp.bfloat16)


def select_rows(ancestors, portion):
    number = portion.shape[0]
    indices = lax.iota(jnp.int32, number)
    onehot = (ancestors[:, None] == indices[None, :]).astype(jnp.bfloat16)
    return jnp.einsum("jp,prd->jrd", onehot, portion, preferred_element_type=jnp.float32)


def body(states, ancestors, pair_bias, key_mask, gain_attn, w_qkv, w_o, gain_ff, w_in, w_out):
    chosen = select_rows(ancestors, lax.all_gather(states, "particle", axis=0, tiled=True)).astype(
        jnp.bfloat16
    )
    units = w_out.shape[1] // lax.axis_size("token")
    first = lax.axis_index("token") * units
    w_in = lax.all_gather(
        lax.dynamic_slice_in_dim(w_in, first, units, 2), "particle", axis=1, tiled=True
    )
    w_out = lax.all_gather(
        lax.dynamic_slice_in_dim(w_out, first, units, 1), "particle", axis=0, tiled=True
    )
    return run_block(chosen, pair_bias, key_mask, gain_attn, w_qkv, w_o, gain_ff, w_in, w_out)


def block_kernel(
    states_ref, ancestors_ref, bias_hbm, mask_ref, gain_attn_ref, w_qkv_hbm, w_o_hbm, gain_ff_ref,
    w_in_hbm, w_out_hbm, out_ref,
    states_all, w_in_all, w_out_all, w_qkv, w_o, bias, normed_all, kv_all, ff_all,
    core_out, core_in, row_out, row_in, wish_out, wish_in, pick_out, pick_in,
    local_sem, recv_sem, right_sem, left_sem, across_sem, gather_recv, gather_row, gather_core,
    core_send, core_recv, row_send, row_recv, wish_send, wish_recv, pick_send, pick_recv,
):
    per, rows, width = states_ref.shape
    groups = lax.axis_size("particle")
    lines = groups // 2
    cells = lax.axis_size("token")
    spans = cells // 2
    units = w_in_all.shape[-1]
    head_count = bias.shape[0] // rows
    head_size = width // head_count
    me = lax.axis_index("particle")
    spot = lax.axis_index("token")
    line, side = me // 2, me % 2
    span, core = spot // 2, spot % 2
    across = (line * 2 + 1 - side, spot)
    above, below = (me + 2, spot), (me - 2, spot)
    other_core = (me, span * 2 + 1 - core)

    def span_peer(step):
        return lax.rem(span + step, spans)

    barrier = pltpu.get_barrier_semaphore()

    def greet(device):
        pl.semaphore_signal(barrier, inc=1, device_id=device, device_id_type=MESH)

    greet(across)
    greet(other_core)
    for step in range(1, spans):
        greet((me, span_peer(step) * 2 + core))

    @pl.when(line > 0)
    def _():
        greet(below)

    @pl.when(line < lines - 1)
    def _():
        greet(above)

    first = pl.multiple_of(spot * units, 128)
    locals_ = [
        pltpu.make_async_copy(states_ref, states_all.at[pl.ds(me * per, per)], local_sem.at[0]),
        pltpu.make_async_copy(
            w_in_hbm.at[:, :, pl.ds(first, units)], w_in_all.at[me], local_sem.at[1]
        ),
        pltpu.make_async_copy(
            w_out_hbm.at[:, pl.ds(first, units)], w_out_all.at[me], local_sem.at[2]
        ),
        pltpu.make_async_copy(w_qkv_hbm, w_qkv, local_sem.at[3]),
        pltpu.make_async_copy(bias_hbm, bias, local_sem.at[4]),
        pltpu.make_async_copy(w_o_hbm, w_o, local_sem.at[5]),
    ]
    for copy in locals_:
        copy.start()
    locals_[0].wait()
    pl.semaphore_wait(
        barrier,
        2 + spans - 1 + jnp.where(line > 0, 1, 0) + jnp.where(line < lines - 1, 1, 0),
    )

    views = (
        lambda k: states_all.at[pl.ds(k * per, per)],
        lambda k: w_in_all.at[k],
        lambda k: w_out_all.at[k],
    )

    def remote(kind, source, sems, device):
        k = source * 2 + side
        return pltpu.make_async_remote_copy(
            src_ref=views[kind](k),
            dst_ref=views[kind](k),
            send_sem=sems.at[kind, source],
            recv_sem=recv_sem.at[kind, k],
            device_id=device,
            device_id_type=MESH,
        )

    def arrived(kind, k):
        pltpu.make_async_remote_copy(
            src_ref=views[kind](k),
            dst_ref=views[kind](k),
            send_sem=across_sem.at[kind, 0],
            recv_sem=recv_sem.at[kind, k],
            device_id=across,
            device_id_type=MESH,
        ).wait_recv()

    def relay(kind, step, along=True, cross=True):
        low, high = line - step, line + step

        @pl.when(low >= 0)
        def _():
            if step > 0:
                arrived(kind, low * 2 + side)

            @pl.when(jnp.logical_and(along, line < lines - 1))
            def _():
                remote(kind, low, right_sem, above).start()

        @pl.when(high < lines)
        def _():
            if step > 0:
                arrived(kind, high * 2 + side)

            @pl.when(jnp.logical_and(along, line > 0))
            def _():
                remote(kind, high, left_sem, below).start()

        if kind == 0 or not cross:
            return

        @pl.when(low >= 0)
        def _():
            remote(kind, low, across_sem, across).start()

        if step > 0:

            @pl.when(high < lines)
            def _():
                remote(kind, high, across_sem, across).start()

    def finish(kind):
        for source in range(lines):
            arrived(kind, source * 2 + 1 - side)

    def drain(kind):
        for source in range(lines):
            if kind > 0:
                remote(kind, source, across_sem, across).wait_send()

            @pl.when(jnp.logical_and(line < lines - 1, source <= line))
            def _():
                remote(kind, source, right_sem, above).wait_send()

            @pl.when(jnp.logical_and(line > 0, source >= line))
            def _():
                remote(kind, source, left_sem, below).wait_send()

    def slot_copy(which, buf, slot, send, device):
        return pltpu.make_async_remote_copy(
            src_ref=buf.at[slot],
            dst_ref=buf.at[slot],
            send_sem=send,
            recv_sem=gather_recv.at[which, slot],
            device_id=device,
            device_id_type=MESH,
        )

    def token_sends(which, buf):
        copies = [
            slot_copy(
                which, buf, spot, gather_row.at[which, step], (me, span_peer(step) * 2 + core)
            )
            for step in range(1, spans)
        ]
        copies.append(slot_copy(which, buf, spot, gather_core.at[which, 0], other_core))
        for copy in copies:
            copy.start()
        return copies

    def token_forward(which, buf):
        copies = []
        for step in range(1, spans):
            slot = span_peer(step) * 2 + core
            copy = slot_copy(which, buf, slot, gather_core.at[which, step], other_core)
            copy.wait_recv()
            copy.start()
            copies.append(copy)
        for step in range(spans):
            slot = span_peer(step) * 2 + 1 - core
            slot_copy(which, buf, slot, gather_core.at[which, 0], other_core).wait_recv()
        return copies

    def norm(stream, gain):
        mean = jnp.mean(stream * stream, axis=-1, keepdims=True)
        return (stream * lax.rsqrt(mean + 1e-05) * gain).astype(jnp.bfloat16)

    def dot(a, b):
        return jnp.dot(a, b, preferred_element_type=jnp.float32)

    def dot_t(a, b):
        return lax.dot_general(
            a, b, (((1,), (1,)), ((), ())), preferred_element_type=jnp.float32
        )

    for j in range(per):
        wish_out[j] = jnp.full(wish_out.shape[1:], ancestors_ref[j], jnp.int32)

    def to_across(source, target, send, recv):
        return pltpu.make_async_remote_copy(
            src_ref=source,
            dst_ref=target,
            send_sem=send,
            recv_sem=recv,
            device_id=across,
            device_id_type=MESH,
        )

    wish = to_across(wish_out, wish_in, wish_send, wish_recv)
    wish.start()
    relay(0, 0)
    locals_[1].wait()
    relay(1, 0, along=False)
    locals_[2].wait()
    relay(2, 0, along=False)
    for step in range(1, lines - 1):
        relay(0, step)
    relay(1, 0, cross=False)
    if lines > 1:
        relay(0, lines - 1)
    wish.wait_recv()

    def picked(wishes):
        found = [jnp.zeros((rows, width), jnp.float32) for _ in range(per)]
        for source in range(lines):
            for i in range(per):
                k = (source * 2 + side) * per + i
                held = states_all[k].astype(jnp.float32)
                for j in range(per):
                    found[j] = jnp.where(wishes[j][:1, :1] == k, held, found[j])
        return found

    for j, found in enumerate(picked([wish_in[j] for j in range(per)])):
        pick_out[j] = found.astype(jnp.bfloat16)
    pick = to_across(pick_out, pick_in, pick_send, pick_recv)
    pick.start()
    own = picked([wish_out[j] for j in range(per)])
    pick.wait_recv()
    stream = jnp.concatenate(
        [own[j] + pick_in[j].astype(jnp.float32) for j in range(per)], axis=0
    )
    normed = norm(stream, gain_attn_ref[...].reshape(1, width))
    normed_all[spot] = normed
    sent = token_sends(0, normed_all)
    locals_[3].wait()
    scale = 1.0 / math.sqrt(head_size)
    queries = (dot(normed, w_qkv[:, :width]) * scale).astype(jnp.bfloat16)
    sent += token_forward(0, normed_all)
    if lines > 1:
        relay(1, 1)
    kv_all[...] = dot(
        normed_all[...].reshape(cells * per * rows, width), w_qkv[:, width:]
    ).astype(jnp.bfloat16)
    for step in range(2, lines - 1):
        relay(1, step)
    relay(2, 0, cross=False)
    locals_[4].wait()
    usable = mask_ref[...].reshape(1, -1) > 0
    half = 8
    strip = half * head_size
    lane = lax.broadcasted_iota(jnp.int32, (half, 1, strip), 2)
    head = lax.broadcasted_iota(jnp.int32, (half, 1, strip), 0)
    mine = jnp.logical_and(lane >= head * head_size, lane < (head + 1) * head_size)
    mine_bf = mine.astype(jnp.float32).astype(jnp.bfloat16)
    mine_f = mine.astype(jnp.float32)
    mixed = []
    for j in range(per):
        strips = []
        for part in range(head_count // half):
            cols = slice(part * strip, (part + 1) * strip)
            q = queries[j * rows : (j + 1) * rows, cols]
            spread = (q[None] * mine_bf).reshape(half * rows, strip)

            def tokens_of(base):
                return jnp.concatenate(
                    [
                        kv_all[
                            (t * per + j) * rows : (t * per + j + 1) * rows,
                            base + part * strip : base + (part + 1) * strip,
                        ]
                        for t in range(cells)
                    ],
                    axis=0,
                )

            scores = dot_t(spread, tokens_of(0)) + bias[
                part * half * rows : (part + 1) * half * rows, :
            ].astype(jnp.float32)
            scores = jnp.where(usable, scores, -1e30)
            top = jnp.max(scores, axis=1, keepdims=True)
            weights = jnp.where(usable, jnp.exp(scores - top), 0.0)
            total = jnp.sum(weights, axis=1, keepdims=True)
            mix = dot(weights.astype(jnp.bfloat16), tokens_of(width)) / total
            strips.append(jnp.sum(mix.reshape(half, rows, strip) * mine_f, axis=0))
        mixed.append(jnp.concatenate(strips, axis=1))
        if j == 0 and lines > 1:
            if lines > 2:
                relay(1, lines - 1)
            relay(2, 1)
    attended = jnp.concatenate(mixed, axis=0).astype(jnp.bfloat16)
    for step in range(2, lines - 1):
        relay(2, step)
    locals_[5].wait()
    stream = stream + dot(attended, w_o[...])
    ff_all[spot] = norm(stream, gain_ff_ref[...].reshape(1, width))
    sent += token_sends(1, ff_all)
    if lines > 2:
        relay(2, lines - 1)
    sent += token_forward(1, ff_all)
    finish(1)
    normed_ff = ff_all[...].reshape(cells * per * rows, width)
    gate = dot(normed_ff, w_in_all[:, 0].reshape(width, units))
    up = dot(normed_ff, w_in_all[:, 1].reshape(width, units))
    hidden = (gate / (1.0 + jnp.exp(-gate)) * up).astype(jnp.bfloat16)
    finish(2)
    update = dot_t(hidden, w_out_all[...].reshape(width, units))
    update = update.reshape(spans, 2, per * rows, width)
    is_low = core == 0
    core_out[...] = jnp.where(is_low, update[:, 1], update[:, 0]).astype(jnp.bfloat16)
    copy = pltpu.make_async_remote_copy(
        src_ref=core_out,
        dst_ref=core_in,
        send_sem=core_send,
        recv_sem=core_recv,
        device_id=other_core,
        device_id_type=MESH,
    )
    copy.start()
    kept = jnp.where(is_low, update[:, 0], update[:, 1])
    copy.wait_recv()
    sent.append(copy)
    row_out[...] = (kept + core_in[...].astype(jnp.float32)).astype(jnp.bfloat16)
    rowed = []
    for step in range(1, spans):
        copy = pltpu.make_async_remote_copy(
            src_ref=row_out.at[span_peer(step)],
            dst_ref=row_in.at[step],
            send_sem=row_send.at[step],
            recv_sem=row_recv.at[step],
            device_id=(me, span_peer(step) * 2 + core),
            device_id_type=MESH,
        )
        copy.start()
        rowed.append(copy)
    stream = stream + row_out[span].astype(jnp.float32)
    for step, copy in enumerate(rowed, 1):
        copy.wait_recv()
        stream = stream + row_in[step].astype(jnp.float32)
    out_ref[...] = stream.astype(jnp.bfloat16).reshape(per, rows, width)
    for copy in sent + rowed + [wish, pick]:
        copy.wait_send()
    for kind in range(3):
        drain(kind)


def fused_body(
    states, ancestors, pair_bias, key_mask, gain_attn, w_qkv, w_o, gain_ff, w_in, w_out
):
    per, rows, width = states.shape
    groups, cells = lax.axis_size("particle"), lax.axis_size("token")
    lines, spans = groups // 2, cells // 2
    units = w_out.shape[1] // cells
    depth = w_in.shape[1]
    heads, _, keys = pair_bias.shape
    vmem = pl.BlockSpec(memory_space=pltpu.VMEM)
    smem = pl.BlockSpec(memory_space=pltpu.SMEM)
    hbm = pl.BlockSpec(memory_space=pl.ANY)
    dma = pltpu.SemaphoreType.DMA
    bf16 = jnp.bfloat16
    block = (per * rows, width)
    return pl.pallas_call(
        block_kernel,
        out_shape=jax.ShapeDtypeStruct(states.shape, bf16),
        in_specs=[vmem, smem, hbm, vmem, vmem, hbm, hbm, vmem, hbm, hbm],
        out_specs=vmem,
        scratch_shapes=[
            pltpu.VMEM((groups * per, rows, width), bf16),
            pltpu.VMEM((groups, 2, depth, units), bf16),
            pltpu.VMEM((groups, depth, units), bf16),
            pltpu.VMEM(w_qkv.shape, bf16),
            pltpu.VMEM(w_o.shape, bf16),
            pltpu.VMEM((heads * rows, keys), bf16),
            pltpu.VMEM((cells,) + block, bf16),
            pltpu.VMEM((cells * per * rows, 2 * width), bf16),
            pltpu.VMEM((cells,) + block, bf16),
            pltpu.VMEM((spans,) + block, bf16),
            pltpu.VMEM((spans,) + block, bf16),
            pltpu.VMEM((spans,) + block, bf16),
            pltpu.VMEM((spans,) + block, bf16),
            pltpu.VMEM((per, 8, 128), jnp.int32),
            pltpu.VMEM((per, 8, 128), jnp.int32),
            pltpu.VMEM((per, rows, width), bf16),
            pltpu.VMEM((per, rows, width), bf16),
            dma((6,)),
            dma((3, groups)),
            dma((3, lines)),
            dma((3, lines)),
            dma((3, lines)),
            dma((2, cells)),
            dma((2, spans)),
            dma((2, spans)),
            dma,
            dma,
            dma((spans,)),
            dma((spans,)),
            dma,
            dma,
            dma,
            dma,
        ],
        compiler_params=pltpu.CompilerParams(
            collective_id=0, has_side_effects=True, vmem_limit_bytes=56 * 1024 * 1024
        ),
    )(
        states,
        ancestors,
        pair_bias.reshape(heads * rows, keys),
        key_mask,
        gain_attn,
        w_qkv,
        w_o,
        gain_ff,
        w_in,
        w_out,
    )


def either_body(states, ancestors, pair_bias, key_mask, gain_attn, w_qkv, w_o, gain_ff, w_in, w_out):
    tiles = w_in.shape[1] % 16 == 0 and (w_out.shape[1] // lax.axis_size("token")) % 128 == 0
    run = fused_body if tiles else body
    return run(
        states, ancestors, pair_bias, key_mask, gain_attn, w_qkv, w_o, gain_ff, w_in, w_out
    )


def solution(mesh):
    placed = (
        P("particle", "token", None),
        P("particle"),
        P(None, "token", None),
        P(),
        P(),
        P(),
        P(),
        P(),
        P(None, "particle", None),
        P("particle", None),
    )
    return jax.shard_map(
        either_body, mesh=mesh, in_specs=placed, out_specs=P("particle", "token", None), check_vma=False
    )
```

```python
import math

import jax
import jax.numpy as jnp
from jax import lax
from jax.experimental import pallas as pl
from jax.experimental.pallas import tpu as pltpu
from jax.sharding import PartitionSpec as P

MESH = pl.DeviceIdType.MESH


def rms_norm(stream, gain_vec):
    return stream * lax.rsqrt(jnp.mean(stream * stream, axis=-1, keepdims=True) + 1e-05) * gain_vec


def attend_portion(running_sum, queries, key_part, value_part, pair_bias, key_mask):
    running, totals, summed = running_sum
    part_count, row_count, model_width = queries.shape
    head_count = pair_bias.shape[0]
    head_size = model_width // head_count
    number = key_part.shape[1]
    query_heads = queries.reshape(part_count, row_count, head_count, head_size)
    key_heads = key_part.reshape(part_count, number, head_count, head_size)
    value_heads = value_part.reshape(part_count, number, head_count, head_size)
    scores = jnp.einsum(
        "prhe,pnhe->phrn", query_heads, key_heads, preferred_element_type=jnp.float32
    )
    bias_part = pair_bias.astype(jnp.float32)
    scores = scores + bias_part[None]
    usable = (key_mask > 0)[None, None, None, :]
    new_max = jnp.maximum(running, jnp.max(jnp.where(usable, scores, -1e30), axis=3))
    weights = jnp.where(usable, jnp.exp(scores - new_max[..., None]), 0.0)
    totals = jnp.sum(weights, axis=3)
    summed = jnp.einsum(
        "phrn,pnhe->phre",
        weights.astype(jnp.bfloat16),
        value_heads,
        preferred_element_type=jnp.float32,
    )
    return (new_max, totals, summed)


def run_block(states, pair_bias, key_mask, gain_attn, w_qkv, w_o, gain_ff, w_in, w_out):
    part_count, row_count, model_width = states.shape
    head_count = pair_bias.shape[0]
    head_size = model_width // head_count
    score_scale = 1.0 / math.sqrt(head_size)
    stream = states.astype(jnp.float32)
    normed = rms_norm(stream, gain_attn).astype(jnp.bfloat16)
    start_carry = (
        jnp.full((part_count, head_count, row_count), -1e30, jnp.float32),
        jnp.zeros((part_count, head_count, row_count), jnp.float32),
        jnp.zeros((part_count, head_count, row_count, head_size), jnp.float32),
    )
    queries = (
        jnp.einsum(
            "prd,de->pre", normed, w_qkv[:, :model_width], preferred_element_type=jnp.float32
        )
        * score_scale
    ).astype(jnp.bfloat16)
    normed_all = lax.all_gather(normed, "token", axis=1, tiled=True)
    projected = jnp.einsum(
        "prd,de->pre", normed_all, w_qkv[:, model_width:], preferred_element_type=jnp.float32
    ).astype(jnp.bfloat16)
    portion = (projected[..., :model_width], projected[..., model_width:])
    running, totals, summed = attend_portion(
        start_carry, queries, portion[0], portion[1], pair_bias, key_mask
    )
    attended = (
        (summed / totals[..., None])
        .transpose(0, 2, 1, 3)
        .reshape(part_count, row_count, model_width)
        .astype(jnp.bfloat16)
    )
    stream = stream + jnp.einsum("prd,de->pre", attended, w_o, preferred_element_type=jnp.float32)
    normed_ff = rms_norm(stream, gain_ff).astype(jnp.bfloat16)
    normed_ff = lax.all_gather(normed_ff, "token", axis=1, tiled=True)
    gate_sum = jnp.einsum("prd,df->prf", normed_ff, w_in[0], preferred_element_type=jnp.float32)
    up_sum = jnp.einsum("prd,df->prf", normed_ff, w_in[1], preferred_element_type=jnp.float32)
    hidden = (jax.nn.silu(gate_sum) * up_sum).astype(jnp.bfloat16)
    update = jnp.einsum(
        "prf,nf->prn", hidden, w_out, preferred_element_type=jnp.float32
    ).astype(jnp.bfloat16)
    update = lax.psum_scatter(update, "token", scatter_dimension=1, tiled=True)
    return (stream + update.astype(jnp.float32)).astype(jnp.bfloat16)


def select_rows(ancestors, portion):
    number = portion.shape[0]
    indices = lax.iota(jnp.int32, number)
    onehot = (ancestors[:, None] == indices[None, :]).astype(jnp.bfloat16)
    return jnp.einsum("jp,prd->jrd", onehot, portion, preferred_element_type=jnp.float32)


def body(states, ancestors, pair_bias, key_mask, gain_attn, w_qkv, w_o, gain_ff, w_in, w_out):
    chosen = select_rows(ancestors, lax.all_gather(states, "particle", axis=0, tiled=True)).astype(
        jnp.bfloat16
    )
    units = w_out.shape[1] // lax.axis_size("token")
    first = lax.axis_index("token") * units
    w_in = lax.all_gather(
        lax.dynamic_slice_in_dim(w_in, first, units, 2), "particle", axis=1, tiled=True
    )
    w_out = lax.all_gather(
        lax.dynamic_slice_in_dim(w_out, first, units, 1), "particle", axis=0, tiled=True
    )
    return run_block(chosen, pair_bias, key_mask, gain_attn, w_qkv, w_o, gain_ff, w_in, w_out)


def block_kernel(
    states_ref, ancestors_ref, bias_hbm, mask_ref, gain_attn_ref, w_qkv_hbm, w_o_hbm, gain_ff_ref,
    w_in_hbm, w_out_hbm, out_ref,
    states_all, w_in_all, w_out_all, w_qkv, w_o, bias, normed_all, kv_all, ff_all,
    core_out, core_in, row_out, row_in,
    local_sem, recv_sem, right_sem, left_sem, across_sem, gather_recv, gather_row, gather_core,
    core_send, core_recv, row_send, row_recv,
):
    per, rows, width = states_ref.shape
    groups = lax.axis_size("particle")
    lines = groups // 2
    cells = lax.axis_size("token")
    spans = cells // 2
    units = w_in_all.shape[-1]
    head_count = bias.shape[0] // rows
    head_size = width // head_count
    me = lax.axis_index("particle")
    spot = lax.axis_index("token")
    line, side = me // 2, me % 2
    span, core = spot // 2, spot % 2
    across = (line * 2 + 1 - side, spot)
    above, below = (me + 2, spot), (me - 2, spot)
    other_core = (me, span * 2 + 1 - core)

    def span_peer(step):
        return lax.rem(span + step, spans)

    barrier = pltpu.get_barrier_semaphore()

    def greet(device):
        pl.semaphore_signal(barrier, inc=1, device_id=device, device_id_type=MESH)

    greet(across)
    greet(other_core)
    for step in range(1, spans):
        greet((me, span_peer(step) * 2 + core))

    @pl.when(line > 0)
    def _():
        greet(below)

    @pl.when(line < lines - 1)
    def _():
        greet(above)

    first = pl.multiple_of(spot * units, 128)
    locals_ = [
        pltpu.make_async_copy(states_ref, states_all.at[pl.ds(me * per, per)], local_sem.at[0]),
        pltpu.make_async_copy(
            w_in_hbm.at[:, :, pl.ds(first, units)], w_in_all.at[me], local_sem.at[1]
        ),
        pltpu.make_async_copy(
            w_out_hbm.at[:, pl.ds(first, units)], w_out_all.at[me], local_sem.at[2]
        ),
        pltpu.make_async_copy(w_qkv_hbm, w_qkv, local_sem.at[3]),
        pltpu.make_async_copy(bias_hbm, bias, local_sem.at[4]),
        pltpu.make_async_copy(w_o_hbm, w_o, local_sem.at[5]),
    ]
    for copy in locals_:
        copy.start()
    locals_[0].wait()
    pl.semaphore_wait(
        barrier,
        2 + spans - 1 + jnp.where(line > 0, 1, 0) + jnp.where(line < lines - 1, 1, 0),
    )

    views = (
        lambda k: states_all.at[pl.ds(k * per, per)],
        lambda k: w_in_all.at[k],
        lambda k: w_out_all.at[k],
    )

    def remote(kind, source, sems, device):
        k = source * 2 + side
        return pltpu.make_async_remote_copy(
            src_ref=views[kind](k),
            dst_ref=views[kind](k),
            send_sem=sems.at[kind, source],
            recv_sem=recv_sem.at[kind, k],
            device_id=device,
            device_id_type=MESH,
        )

    def arrived(kind, k):
        pltpu.make_async_remote_copy(
            src_ref=views[kind](k),
            dst_ref=views[kind](k),
            send_sem=across_sem.at[kind, 0],
            recv_sem=recv_sem.at[kind, k],
            device_id=across,
            device_id_type=MESH,
        ).wait_recv()

    def relay(kind, step, along=True, cross=True):
        low, high = line - step, line + step

        @pl.when(low >= 0)
        def _():
            if step > 0:
                arrived(kind, low * 2 + side)

            @pl.when(jnp.logical_and(along, line < lines - 1))
            def _():
                remote(kind, low, right_sem, above).start()

        @pl.when(high < lines)
        def _():
            if step > 0:
                arrived(kind, high * 2 + side)

            @pl.when(jnp.logical_and(along, line > 0))
            def _():
                remote(kind, high, left_sem, below).start()

        if not cross:
            return

        @pl.when(low >= 0)
        def _():
            remote(kind, low, across_sem, across).start()

        if step > 0:

            @pl.when(high < lines)
            def _():
                remote(kind, high, across_sem, across).start()

    def finish(kind):
        for source in range(lines):
            arrived(kind, source * 2 + 1 - side)

    def drain(kind):
        for source in range(lines):
            remote(kind, source, across_sem, across).wait_send()

            @pl.when(jnp.logical_and(line < lines - 1, source <= line))
            def _():
                remote(kind, source, right_sem, above).wait_send()

            @pl.when(jnp.logical_and(line > 0, source >= line))
            def _():
                remote(kind, source, left_sem, below).wait_send()

    def slot_copy(which, buf, j, slot, send, device):
        return pltpu.make_async_remote_copy(
            src_ref=buf.at[j, slot],
            dst_ref=buf.at[j, slot],
            send_sem=send,
            recv_sem=gather_recv.at[which, j, slot],
            device_id=device,
            device_id_type=MESH,
        )

    sent = []

    def token_sends(which, buf, j):
        for step in range(1, spans):
            device = (me, span_peer(step) * 2 + core)
            sent.append(slot_copy(which, buf, j, spot, gather_row.at[which, j, step], device))
            sent[-1].start()
        sent.append(slot_copy(which, buf, j, spot, gather_core.at[which, j, 0], other_core))
        sent[-1].start()

    def token_forward(which, buf, j):
        for step in range(1, spans):
            slot = span_peer(step) * 2 + core
            copy = slot_copy(which, buf, j, slot, gather_core.at[which, j, step], other_core)
            copy.wait_recv()
            copy.start()
            sent.append(copy)

    def token_finish(which, buf, j):
        for step in range(spans):
            slot = span_peer(step) * 2 + 1 - core
            slot_copy(
                which, buf, j, slot, gather_core.at[which, j, 0], other_core
            ).wait_recv()

    def norm(stream, gain):
        mean = jnp.mean(stream * stream, axis=-1, keepdims=True)
        return (stream * lax.rsqrt(mean + 1e-05) * gain).astype(jnp.bfloat16)

    def dot(a, b):
        return jnp.dot(a, b, preferred_element_type=jnp.float32)

    def dot_t(a, b):
        return lax.dot_general(
            a, b, (((1,), (1,)), ((), ())), preferred_element_type=jnp.float32
        )

    tokens = cells * rows
    last = lines - 1
    for step in range(lines):
        relay(0, step)
        if step == max(last - 1, 0):
            locals_[1].wait()
            relay(1, 0, cross=False)
    relay(1, 0, along=False)
    locals_[2].wait()
    finish(0)

    gain = gain_attn_ref[...].reshape(1, width)
    streams, normed = [], []
    for j in range(per):
        streams.append(states_all[ancestors_ref[j]].astype(jnp.float32))
        normed.append(norm(streams[j], gain))
        normed_all[j, spot] = normed[j]
        token_sends(0, normed_all, j)
    locals_[3].wait()
    scale = 1.0 / math.sqrt(head_size)
    queries = (dot(jnp.concatenate(normed, axis=0), w_qkv[:, :width]) * scale).astype(jnp.bfloat16)
    token_forward(0, normed_all, 0)
    if lines > 1:
        relay(1, 1)

    usable = mask_ref[...].reshape(1, -1) > 0
    half = 8
    strip = half * head_size
    lane = lax.broadcasted_iota(jnp.int32, (half, 1, strip), 2)
    head = lax.broadcasted_iota(jnp.int32, (half, 1, strip), 0)
    mine = jnp.logical_and(lane >= head * head_size, lane < (head + 1) * head_size)
    mine_f = mine.astype(jnp.float32)
    mine_bf = mine_f.astype(jnp.bfloat16)

    def make_keys(j):
        kv_all[j] = dot(normed_all[j].reshape(tokens, width), w_qkv[:, width:]).astype(
            jnp.bfloat16
        )

    def attend(j):
        strips = []
        for part in range(head_count // half):
            low, high = part * strip, (part + 1) * strip
            q = queries[j * rows : (j + 1) * rows, low:high]
            spread = (q[None] * mine_bf).reshape(half * rows, strip)
            scores = dot_t(spread, kv_all[j, :, low:high]) + bias[
                part * half * rows : (part + 1) * half * rows, :
            ].astype(jnp.float32)
            scores = jnp.where(usable, scores, -1e30)
            weights = jnp.exp(scores - jnp.max(scores, axis=1, keepdims=True))
            total = jnp.sum(weights, axis=1, keepdims=True)
            mix = dot(weights.astype(jnp.bfloat16), kv_all[j, :, width + low : width + high])
            mix = mix * (1.0 / total)
            strips.append(jnp.sum(mix.reshape(half, rows, strip) * mine_f, axis=0))
        return jnp.concatenate(strips, axis=1).astype(jnp.bfloat16)

    def close(j, attended):
        streams[j] = streams[j] + dot(attended, w_o[...])
        ff_all[j, spot] = norm(streams[j], gain_ff_ref[...].reshape(1, width))
        token_sends(1, ff_all, j)

    token_finish(0, normed_all, 0)
    make_keys(0)
    for j in range(1, per):
        token_forward(0, normed_all, j)
    for step in range(2, last):
        relay(1, step)
    relay(2, 0)
    locals_[4].wait()
    attended = attend(0)
    locals_[5].wait()
    close(0, attended)
    if lines > 2:
        relay(1, last)
    if lines > 1:
        relay(2, 1)
    for j in range(1, per):
        token_finish(0, normed_all, j)
        make_keys(j)
        attended = attend(j)
        token_forward(1, ff_all, j - 1)
        close(j, attended)
    for step in range(2, lines):
        relay(2, step)
    finish(1)

    is_low = core == 0
    kept, cored, rowed = [], [], []

    def to_core(j):
        return pltpu.make_async_remote_copy(
            src_ref=core_out.at[j],
            dst_ref=core_in.at[j],
            send_sem=core_send.at[j],
            recv_sem=core_recv.at[j],
            device_id=other_core,
            device_id_type=MESH,
        )

    def to_row(j, step):
        return pltpu.make_async_remote_copy(
            src_ref=row_out.at[j, span_peer(step)],
            dst_ref=row_in.at[j, step],
            send_sem=row_send.at[j, step],
            recv_sem=row_recv.at[j, step],
            device_id=(me, span_peer(step) * 2 + core),
            device_id_type=MESH,
        )

    def send_rows(j):
        cored[j].wait_recv()
        row_out[j] = (kept[j] + core_in[j].astype(jnp.float32)).astype(jnp.bfloat16)
        for step in range(1, spans):
            rowed.append(to_row(j, step))
            rowed[-1].start()

    for j in range(per):
        token_finish(1, ff_all, j)
        normed_ff = ff_all[j].reshape(tokens, width)
        gate = dot(normed_ff, w_in_all[:, 0].reshape(width, units))
        up = dot(normed_ff, w_in_all[:, 1].reshape(width, units))
        hidden = (gate / (1.0 + jnp.exp(-gate)) * up).astype(jnp.bfloat16)
        if j == 0:
            finish(2)
        if j + 1 == per - 1:
            token_forward(1, ff_all, per - 1)
        if j > 0:
            send_rows(j - 1)
        update = dot_t(hidden, w_out_all[...].reshape(width, units))
        update = update.reshape(spans, 2, rows, width)
        core_out[j] = jnp.where(is_low, update[:, 1], update[:, 0]).astype(jnp.bfloat16)
        cored.append(to_core(j))
        cored[j].start()
        kept.append(jnp.where(is_low, update[:, 0], update[:, 1]))
    send_rows(per - 1)
    for j in range(per):
        stream = streams[j] + row_out[j, span].astype(jnp.float32)
        for step in range(1, spans):
            to_row(j, step).wait_recv()
            stream = stream + row_in[j, step].astype(jnp.float32)
        out_ref[j] = stream.astype(jnp.bfloat16)
    for copy in sent + cored + rowed:
        copy.wait_send()
    for kind in range(3):
        drain(kind)


def fused_body(
    states, ancestors, pair_bias, key_mask, gain_attn, w_qkv, w_o, gain_ff, w_in, w_out
):
    per, rows, width = states.shape
    groups, cells = lax.axis_size("particle"), lax.axis_size("token")
    lines, spans = groups // 2, cells // 2
    units = w_out.shape[1] // cells
    depth = w_in.shape[1]
    heads, _, keys = pair_bias.shape
    vmem = pl.BlockSpec(memory_space=pltpu.VMEM)
    smem = pl.BlockSpec(memory_space=pltpu.SMEM)
    hbm = pl.BlockSpec(memory_space=pl.ANY)
    dma = pltpu.SemaphoreType.DMA
    bf16 = jnp.bfloat16
    block = (rows, width)
    return pl.pallas_call(
        block_kernel,
        out_shape=jax.ShapeDtypeStruct(states.shape, bf16),
        in_specs=[vmem, smem, hbm, vmem, vmem, hbm, hbm, vmem, hbm, hbm],
        out_specs=vmem,
        scratch_shapes=[
            pltpu.VMEM((groups * per, rows, width), bf16),
            pltpu.VMEM((groups, 2, depth, units), bf16),
            pltpu.VMEM((groups, depth, units), bf16),
            pltpu.VMEM(w_qkv.shape, bf16),
            pltpu.VMEM(w_o.shape, bf16),
            pltpu.VMEM((heads * rows, keys), bf16),
            pltpu.VMEM((per, cells) + block, bf16),
            pltpu.VMEM((per, cells * rows, 2 * width), bf16),
            pltpu.VMEM((per, cells) + block, bf16),
            pltpu.VMEM((per, spans) + block, bf16),
            pltpu.VMEM((per, spans) + block, bf16),
            pltpu.VMEM((per, spans) + block, bf16),
            pltpu.VMEM((per, spans) + block, bf16),
            dma((6,)),
            dma((3, groups)),
            dma((3, lines)),
            dma((3, lines)),
            dma((3, lines)),
            dma((2, per, cells)),
            dma((2, per, spans)),
            dma((2, per, spans)),
            dma((per,)),
            dma((per,)),
            dma((per, spans)),
            dma((per, spans)),
        ],
        compiler_params=pltpu.CompilerParams(
            collective_id=0, has_side_effects=True, vmem_limit_bytes=56 * 1024 * 1024
        ),
    )(
        states,
        ancestors,
        pair_bias.reshape(heads * rows, keys),
        key_mask,
        gain_attn,
        w_qkv,
        w_o,
        gain_ff,
        w_in,
        w_out,
    )


def either_body(states, ancestors, pair_bias, key_mask, gain_attn, w_qkv, w_o, gain_ff, w_in, w_out):
    tiles = w_in.shape[1] % 16 == 0 and (w_out.shape[1] // lax.axis_size("token")) % 128 == 0
    run = fused_body if tiles else body
    return run(
        states, ancestors, pair_bias, key_mask, gain_attn, w_qkv, w_o, gain_ff, w_in, w_out
    )


def solution(mesh):
    placed = (
        P("particle", "token", None),
        P("particle"),
        P(None, "token", None),
        P(),
        P(),
        P(),
        P(),
        P(),
        P(None, "particle", None),
        P("particle", None),
    )
    return jax.shard_map(
        either_body, mesh=mesh, in_specs=placed, out_specs=P("particle", "token", None), check_vma=False
    )
```

```python
import math

import jax
import jax.numpy as jnp
from jax import lax
from jax.experimental import pallas as pl
from jax.experimental.pallas import tpu as pltpu
from jax.sharding import PartitionSpec as P

MESH = pl.DeviceIdType.MESH


def rms_norm(stream, gain_vec):
    return stream * lax.rsqrt(jnp.mean(stream * stream, axis=-1, keepdims=True) + 1e-05) * gain_vec


def attend_portion(running_sum, queries, key_part, value_part, pair_bias, key_mask):
    running, totals, summed = running_sum
    part_count, row_count, model_width = queries.shape
    head_count = pair_bias.shape[0]
    head_size = model_width // head_count
    number = key_part.shape[1]
    query_heads = queries.reshape(part_count, row_count, head_count, head_size)
    key_heads = key_part.reshape(part_count, number, head_count, head_size)
    value_heads = value_part.reshape(part_count, number, head_count, head_size)
    scores = jnp.einsum(
        "prhe,pnhe->phrn", query_heads, key_heads, preferred_element_type=jnp.float32
    )
    bias_part = pair_bias.astype(jnp.float32)
    scores = scores + bias_part[None]
    usable = (key_mask > 0)[None, None, None, :]
    new_max = jnp.maximum(running, jnp.max(jnp.where(usable, scores, -1e30), axis=3))
    weights = jnp.where(usable, jnp.exp(scores - new_max[..., None]), 0.0)
    totals = jnp.sum(weights, axis=3)
    summed = jnp.einsum(
        "phrn,pnhe->phre",
        weights.astype(jnp.bfloat16),
        value_heads,
        preferred_element_type=jnp.float32,
    )
    return (new_max, totals, summed)


def run_block(states, pair_bias, key_mask, gain_attn, w_qkv, w_o, gain_ff, w_in, w_out):
    part_count, row_count, model_width = states.shape
    head_count = pair_bias.shape[0]
    head_size = model_width // head_count
    score_scale = 1.0 / math.sqrt(head_size)
    stream = states.astype(jnp.float32)
    normed = rms_norm(stream, gain_attn).astype(jnp.bfloat16)
    start_carry = (
        jnp.full((part_count, head_count, row_count), -1e30, jnp.float32),
        jnp.zeros((part_count, head_count, row_count), jnp.float32),
        jnp.zeros((part_count, head_count, row_count, head_size), jnp.float32),
    )
    queries = (
        jnp.einsum(
            "prd,de->pre", normed, w_qkv[:, :model_width], preferred_element_type=jnp.float32
        )
        * score_scale
    ).astype(jnp.bfloat16)
    normed_all = lax.all_gather(normed, "token", axis=1, tiled=True)
    projected = jnp.einsum(
        "prd,de->pre", normed_all, w_qkv[:, model_width:], preferred_element_type=jnp.float32
    ).astype(jnp.bfloat16)
    portion = (projected[..., :model_width], projected[..., model_width:])
    running, totals, summed = attend_portion(
        start_carry, queries, portion[0], portion[1], pair_bias, key_mask
    )
    attended = (
        (summed / totals[..., None])
        .transpose(0, 2, 1, 3)
        .reshape(part_count, row_count, model_width)
        .astype(jnp.bfloat16)
    )
    stream = stream + jnp.einsum("prd,de->pre", attended, w_o, preferred_element_type=jnp.float32)
    normed_ff = rms_norm(stream, gain_ff).astype(jnp.bfloat16)
    normed_ff = lax.all_gather(normed_ff, "token", axis=1, tiled=True)
    gate_sum = jnp.einsum("prd,df->prf", normed_ff, w_in[0], preferred_element_type=jnp.float32)
    up_sum = jnp.einsum("prd,df->prf", normed_ff, w_in[1], preferred_element_type=jnp.float32)
    hidden = (jax.nn.silu(gate_sum) * up_sum).astype(jnp.bfloat16)
    update = jnp.einsum(
        "prf,nf->prn", hidden, w_out, preferred_element_type=jnp.float32
    ).astype(jnp.bfloat16)
    update = lax.psum_scatter(update, "token", scatter_dimension=1, tiled=True)
    return (stream + update.astype(jnp.float32)).astype(jnp.bfloat16)


def select_rows(ancestors, portion):
    number = portion.shape[0]
    indices = lax.iota(jnp.int32, number)
    onehot = (ancestors[:, None] == indices[None, :]).astype(jnp.bfloat16)
    return jnp.einsum("jp,prd->jrd", onehot, portion, preferred_element_type=jnp.float32)


def body(states, ancestors, pair_bias, key_mask, gain_attn, w_qkv, w_o, gain_ff, w_in, w_out):
    chosen = select_rows(ancestors, lax.all_gather(states, "particle", axis=0, tiled=True)).astype(
        jnp.bfloat16
    )
    units = w_out.shape[1] // lax.axis_size("token")
    first = lax.axis_index("token") * units
    w_in = lax.all_gather(
        lax.dynamic_slice_in_dim(w_in, first, units, 2), "particle", axis=1, tiled=True
    )
    w_out = lax.all_gather(
        lax.dynamic_slice_in_dim(w_out, first, units, 1), "particle", axis=0, tiled=True
    )
    return run_block(chosen, pair_bias, key_mask, gain_attn, w_qkv, w_o, gain_ff, w_in, w_out)


def block_kernel(
    states_ref, ancestors_ref, bias_hbm, mask_ref, gain_attn_ref, w_qkv_hbm, w_o_hbm, gain_ff_ref,
    w_in_hbm, w_out_hbm, out_ref,
    states_all, w_in_all, w_out_all, w_qkv, w_o, bias, normed_all, kv_all, ff_all,
    core_out, core_in, row_out, row_in, wish_out, wish_in, pick_out, pick_in,
    local_sem, recv_sem, right_sem, left_sem, across_sem, gather_recv, gather_row, gather_core,
    core_send, core_recv, row_send, row_recv, wish_send, wish_recv, pick_send, pick_recv,
):
    per, rows, width = states_ref.shape
    groups = lax.axis_size("particle")
    lines = groups // 2
    cells = lax.axis_size("token")
    spans = cells // 2
    units = w_in_all.shape[-1]
    head_count = bias.shape[0] // rows
    head_size = width // head_count
    me = lax.axis_index("particle")
    spot = lax.axis_index("token")
    line, side = me // 2, me % 2
    span, core = spot // 2, spot % 2
    across = (line * 2 + 1 - side, spot)
    above, below = (me + 2, spot), (me - 2, spot)
    other_core = (me, span * 2 + 1 - core)

    def span_peer(step):
        return lax.rem(span + step, spans)

    barrier = pltpu.get_barrier_semaphore()

    def greet(device):
        pl.semaphore_signal(barrier, inc=1, device_id=device, device_id_type=MESH)

    greet(across)
    greet(other_core)
    for step in range(1, spans):
        greet((me, span_peer(step) * 2 + core))

    @pl.when(line > 0)
    def _():
        greet(below)

    @pl.when(line < lines - 1)
    def _():
        greet(above)

    first = pl.multiple_of(spot * units, 128)
    locals_ = [
        pltpu.make_async_copy(states_ref, states_all.at[pl.ds(me * per, per)], local_sem.at[0]),
        pltpu.make_async_copy(
            w_in_hbm.at[:, :, pl.ds(first, units)], w_in_all.at[me], local_sem.at[1]
        ),
        pltpu.make_async_copy(
            w_out_hbm.at[:, pl.ds(first, units)], w_out_all.at[me], local_sem.at[2]
        ),
        pltpu.make_async_copy(w_qkv_hbm, w_qkv, local_sem.at[3]),
        pltpu.make_async_copy(bias_hbm, bias, local_sem.at[4]),
        pltpu.make_async_copy(w_o_hbm, w_o, local_sem.at[5]),
    ]
    for copy in locals_:
        copy.start()
    locals_[0].wait()
    pl.semaphore_wait(
        barrier,
        2 + spans - 1 + jnp.where(line > 0, 1, 0) + jnp.where(line < lines - 1, 1, 0),
    )

    views = (
        lambda k: states_all.at[pl.ds(k * per, per)],
        lambda k: w_in_all.at[k],
        lambda k: w_out_all.at[k],
    )

    def remote(kind, source, sems, device):
        k = source * 2 + side
        return pltpu.make_async_remote_copy(
            src_ref=views[kind](k),
            dst_ref=views[kind](k),
            send_sem=sems.at[kind, source],
            recv_sem=recv_sem.at[kind, k],
            device_id=device,
            device_id_type=MESH,
        )

    def arrived(kind, k):
        pltpu.make_async_remote_copy(
            src_ref=views[kind](k),
            dst_ref=views[kind](k),
            send_sem=across_sem.at[kind, 0],
            recv_sem=recv_sem.at[kind, k],
            device_id=across,
            device_id_type=MESH,
        ).wait_recv()

    def relay(kind, step, along=True, cross=True):
        low, high = line - step, line + step

        @pl.when(low >= 0)
        def _():
            if step > 0:
                arrived(kind, low * 2 + side)

            @pl.when(jnp.logical_and(along, line < lines - 1))
            def _():
                remote(kind, low, right_sem, above).start()

        @pl.when(high < lines)
        def _():
            if step > 0:
                arrived(kind, high * 2 + side)

            @pl.when(jnp.logical_and(along, line > 0))
            def _():
                remote(kind, high, left_sem, below).start()

        if kind == 0 or not cross:
            return

        @pl.when(low >= 0)
        def _():
            remote(kind, low, across_sem, across).start()

        if step > 0:

            @pl.when(high < lines)
            def _():
                remote(kind, high, across_sem, across).start()

    def finish(kind):
        for source in range(lines):
            arrived(kind, source * 2 + 1 - side)

    def drain(kind):
        for source in range(lines):
            if kind > 0:
                remote(kind, source, across_sem, across).wait_send()

            @pl.when(jnp.logical_and(line < lines - 1, source <= line))
            def _():
                remote(kind, source, right_sem, above).wait_send()

            @pl.when(jnp.logical_and(line > 0, source >= line))
            def _():
                remote(kind, source, left_sem, below).wait_send()

    def slot_copy(which, buf, j, slot, send, device):
        return pltpu.make_async_remote_copy(
            src_ref=buf.at[j, slot],
            dst_ref=buf.at[j, slot],
            send_sem=send,
            recv_sem=gather_recv.at[which, j, slot],
            device_id=device,
            device_id_type=MESH,
        )

    sent = []

    def token_sends(which, buf, j):
        for step in range(1, spans):
            device = (me, span_peer(step) * 2 + core)
            sent.append(slot_copy(which, buf, j, spot, gather_row.at[which, j, step], device))
            sent[-1].start()
        sent.append(slot_copy(which, buf, j, spot, gather_core.at[which, j, 0], other_core))
        sent[-1].start()

    def token_forward(which, buf, j):
        for step in range(1, spans):
            slot = span_peer(step) * 2 + core
            copy = slot_copy(which, buf, j, slot, gather_core.at[which, j, step], other_core)
            copy.wait_recv()
            copy.start()
            sent.append(copy)

    def token_finish(which, buf, j):
        for step in range(spans):
            slot = span_peer(step) * 2 + 1 - core
            slot_copy(
                which, buf, j, slot, gather_core.at[which, j, 0], other_core
            ).wait_recv()

    def norm(stream, gain):
        mean = jnp.mean(stream * stream, axis=-1, keepdims=True)
        return (stream * lax.rsqrt(mean + 1e-05) * gain).astype(jnp.bfloat16)

    def dot(a, b):
        return jnp.dot(a, b, preferred_element_type=jnp.float32)

    def dot_t(a, b):
        return lax.dot_general(
            a, b, (((1,), (1,)), ((), ())), preferred_element_type=jnp.float32
        )

    tokens = cells * rows
    last = lines - 1
    for j in range(per):
        wish_out[j] = jnp.full(wish_out.shape[1:], ancestors_ref[j], jnp.int32)

    def to_across(source, target, send, recv):
        return pltpu.make_async_remote_copy(
            src_ref=source,
            dst_ref=target,
            send_sem=send,
            recv_sem=recv,
            device_id=across,
            device_id_type=MESH,
        )

    wish = to_across(wish_out, wish_in, wish_send, wish_recv)
    wish.start()
    relay(0, 0)
    locals_[1].wait()
    relay(1, 0, along=False)
    locals_[2].wait()
    relay(2, 0, along=False)
    wish.wait_recv()

    def pick_from(found, wished, source):
        for i in range(per):
            k = (source * 2 + side) * per + i
            found = jnp.where(wished[:1, :1] == k, states_all[k].astype(jnp.float32), found)
        return found

    nothing = jnp.zeros((rows, width), jnp.float32)
    asked = [pick_from(nothing, wish_in[j], line) for j in range(per)]
    for step in range(1, lines):
        relay(0, step)
        if step == last - 1:
            relay(1, 0, cross=False)
        for source in (jnp.maximum(line - step, 0), jnp.minimum(line + step, last)):
            if step < last:
                asked = [pick_from(asked[j], wish_in[j], source) for j in range(per)]
    picks = []
    for j in range(per):
        if last > 0:
            for source in (0, last):
                asked[j] = pick_from(asked[j], wish_in[j], source)
        pick_out[j] = asked[j].astype(jnp.bfloat16)
        picks.append(to_across(pick_out.at[j], pick_in.at[j], pick_send.at[j], pick_recv.at[j]))
        picks[j].start()
    own = []
    for j in range(per):
        found = nothing
        for source in range(lines):
            found = pick_from(found, wish_out[j], source)
        own.append(found)

    gain = gain_attn_ref[...].reshape(1, width)
    streams, normed = [], []
    for j in range(per):
        picks[j].wait_recv()
        streams.append(own[j] + pick_in[j].astype(jnp.float32))
        normed.append(norm(streams[j], gain))
        normed_all[j, spot] = normed[j]
        token_sends(0, normed_all, j)
    locals_[3].wait()
    scale = 1.0 / math.sqrt(head_size)
    queries = (dot(jnp.concatenate(normed, axis=0), w_qkv[:, :width]) * scale).astype(jnp.bfloat16)
    token_forward(0, normed_all, 0)
    if lines > 1:
        relay(1, 1)

    usable = mask_ref[...].reshape(1, -1) > 0
    half = 8
    strip = half * head_size
    lane = lax.broadcasted_iota(jnp.int32, (half, 1, strip), 2)
    head = lax.broadcasted_iota(jnp.int32, (half, 1, strip), 0)
    mine = jnp.logical_and(lane >= head * head_size, lane < (head + 1) * head_size)
    mine_f = mine.astype(jnp.float32)
    mine_bf = mine_f.astype(jnp.bfloat16)

    def make_keys(j):
        kv_all[j] = dot(normed_all[j].reshape(tokens, width), w_qkv[:, width:]).astype(
            jnp.bfloat16
        )

    def attend(j):
        strips = []
        for part in range(head_count // half):
            low, high = part * strip, (part + 1) * strip
            q = queries[j * rows : (j + 1) * rows, low:high]
            spread = (q[None] * mine_bf).reshape(half * rows, strip)
            scores = dot_t(spread, kv_all[j, :, low:high]) + bias[
                part * half * rows : (part + 1) * half * rows, :
            ].astype(jnp.float32)
            scores = jnp.where(usable, scores, -1e30)
            weights = jnp.exp(scores - jnp.max(scores, axis=1, keepdims=True))
            total = jnp.sum(weights, axis=1, keepdims=True)
            mix = dot(weights.astype(jnp.bfloat16), kv_all[j, :, width + low : width + high])
            mix = mix * (1.0 / total)
            strips.append(jnp.sum(mix.reshape(half, rows, strip) * mine_f, axis=0))
        return jnp.concatenate(strips, axis=1).astype(jnp.bfloat16)

    def close(j, attended):
        streams[j] = streams[j] + dot(attended, w_o[...])
        ff_all[j, spot] = norm(streams[j], gain_ff_ref[...].reshape(1, width))
        token_sends(1, ff_all, j)

    token_finish(0, normed_all, 0)
    make_keys(0)
    for j in range(1, per):
        token_forward(0, normed_all, j)
    for step in range(2, last):
        relay(1, step)
    relay(2, 0, cross=False)
    locals_[4].wait()
    attended = attend(0)
    locals_[5].wait()
    close(0, attended)
    if lines > 2:
        relay(1, last)
    for j in range(1, per):
        token_finish(0, normed_all, j)
        make_keys(j)
        if j == 1 and lines > 1:
            relay(2, 1)
        attended = attend(j)
        token_forward(1, ff_all, j - 1)
        close(j, attended)
    for step in range(2, lines):
        relay(2, step)
    finish(1)

    is_low = core == 0
    kept, cored, rowed = [], [], []

    def to_core(j):
        return pltpu.make_async_remote_copy(
            src_ref=core_out.at[j],
            dst_ref=core_in.at[j],
            send_sem=core_send.at[j],
            recv_sem=core_recv.at[j],
            device_id=other_core,
            device_id_type=MESH,
        )

    def to_row(j, step):
        return pltpu.make_async_remote_copy(
            src_ref=row_out.at[j, span_peer(step)],
            dst_ref=row_in.at[j, step],
            send_sem=row_send.at[j, step],
            recv_sem=row_recv.at[j, step],
            device_id=(me, span_peer(step) * 2 + core),
            device_id_type=MESH,
        )

    def send_rows(j):
        cored[j].wait_recv()
        row_out[j] = (kept[j] + core_in[j].astype(jnp.float32)).astype(jnp.bfloat16)
        for step in range(1, spans):
            rowed.append(to_row(j, step))
            rowed[-1].start()

    for j in range(per):
        token_finish(1, ff_all, j)
        normed_ff = ff_all[j].reshape(tokens, width)
        gate = dot(normed_ff, w_in_all[:, 0].reshape(width, units))
        up = dot(normed_ff, w_in_all[:, 1].reshape(width, units))
        hidden = (gate / (1.0 + jnp.exp(-gate)) * up).astype(jnp.bfloat16)
        if j == 0:
            finish(2)
        if j + 1 == per - 1:
            token_forward(1, ff_all, per - 1)
        if j > 0:
            send_rows(j - 1)
        update = dot_t(hidden, w_out_all[...].reshape(width, units))
        update = update.reshape(spans, 2, rows, width)
        core_out[j] = jnp.where(is_low, update[:, 1], update[:, 0]).astype(jnp.bfloat16)
        cored.append(to_core(j))
        cored[j].start()
        kept.append(jnp.where(is_low, update[:, 0], update[:, 1]))
    send_rows(per - 1)
    for j in range(per):
        stream = streams[j] + row_out[j, span].astype(jnp.float32)
        for step in range(1, spans):
            to_row(j, step).wait_recv()
            stream = stream + row_in[j, step].astype(jnp.float32)
        out_ref[j] = stream.astype(jnp.bfloat16)
    for copy in sent + cored + rowed + [wish] + picks:
        copy.wait_send()
    for kind in range(3):
        drain(kind)


def fused_body(
    states, ancestors, pair_bias, key_mask, gain_attn, w_qkv, w_o, gain_ff, w_in, w_out
):
    per, rows, width = states.shape
    groups, cells = lax.axis_size("particle"), lax.axis_size("token")
    lines, spans = groups // 2, cells // 2
    units = w_out.shape[1] // cells
    depth = w_in.shape[1]
    heads, _, keys = pair_bias.shape
    vmem = pl.BlockSpec(memory_space=pltpu.VMEM)
    smem = pl.BlockSpec(memory_space=pltpu.SMEM)
    hbm = pl.BlockSpec(memory_space=pl.ANY)
    dma = pltpu.SemaphoreType.DMA
    bf16 = jnp.bfloat16
    block = (rows, width)
    return pl.pallas_call(
        block_kernel,
        out_shape=jax.ShapeDtypeStruct(states.shape, bf16),
        in_specs=[vmem, smem, hbm, vmem, vmem, hbm, hbm, vmem, hbm, hbm],
        out_specs=vmem,
        scratch_shapes=[
            pltpu.VMEM((groups * per, rows, width), bf16),
            pltpu.VMEM((groups, 2, depth, units), bf16),
            pltpu.VMEM((groups, depth, units), bf16),
            pltpu.VMEM(w_qkv.shape, bf16),
            pltpu.VMEM(w_o.shape, bf16),
            pltpu.VMEM((heads * rows, keys), bf16),
            pltpu.VMEM((per, cells) + block, bf16),
            pltpu.VMEM((per, cells * rows, 2 * width), bf16),
            pltpu.VMEM((per, cells) + block, bf16),
            pltpu.VMEM((per, spans) + block, bf16),
            pltpu.VMEM((per, spans) + block, bf16),
            pltpu.VMEM((per, spans) + block, bf16),
            pltpu.VMEM((per, spans) + block, bf16),
            pltpu.VMEM((per, 8, 128), jnp.int32),
            pltpu.VMEM((per, 8, 128), jnp.int32),
            pltpu.VMEM((per, rows, width), bf16),
            pltpu.VMEM((per, rows, width), bf16),
            dma((6,)),
            dma((3, groups)),
            dma((3, lines)),
            dma((3, lines)),
            dma((3, lines)),
            dma((2, per, cells)),
            dma((2, per, spans)),
            dma((2, per, spans)),
            dma((per,)),
            dma((per,)),
            dma((per, spans)),
            dma((per, spans)),
            dma,
            dma,
            dma((per,)),
            dma((per,)),
        ],
        compiler_params=pltpu.CompilerParams(
            collective_id=0, has_side_effects=True, vmem_limit_bytes=56 * 1024 * 1024
        ),
    )(
        states,
        ancestors,
        pair_bias.reshape(heads * rows, keys),
        key_mask,
        gain_attn,
        w_qkv,
        w_o,
        gain_ff,
        w_in,
        w_out,
    )


def either_body(states, ancestors, pair_bias, key_mask, gain_attn, w_qkv, w_o, gain_ff, w_in, w_out):
    tiles = w_in.shape[1] % 16 == 0 and (w_out.shape[1] // lax.axis_size("token")) % 128 == 0
    run = fused_body if tiles else body
    return run(
        states, ancestors, pair_bias, key_mask, gain_attn, w_qkv, w_o, gain_ff, w_in, w_out
    )


def solution(mesh):
    placed = (
        P("particle", "token", None),
        P("particle"),
        P(None, "token", None),
        P(),
        P(),
        P(),
        P(),
        P(),
        P(None, "particle", None),
        P("particle", None),
    )
    return jax.shard_map(
        either_body, mesh=mesh, in_specs=placed, out_specs=P("particle", "token", None), check_vma=False
    )
```

```python
import math

import jax
import jax.numpy as jnp
from jax import lax
from jax.experimental import pallas as pl
from jax.experimental.pallas import tpu as pltpu
from jax.sharding import PartitionSpec as P

MESH = pl.DeviceIdType.MESH


def rms_norm(stream, gain_vec):
    return stream * lax.rsqrt(jnp.mean(stream * stream, axis=-1, keepdims=True) + 1e-05) * gain_vec


def attend_portion(running_sum, queries, key_part, value_part, pair_bias, key_mask):
    running, totals, summed = running_sum
    part_count, row_count, model_width = queries.shape
    head_count = pair_bias.shape[0]
    head_size = model_width // head_count
    number = key_part.shape[1]
    query_heads = queries.reshape(part_count, row_count, head_count, head_size)
    key_heads = key_part.reshape(part_count, number, head_count, head_size)
    value_heads = value_part.reshape(part_count, number, head_count, head_size)
    scores = jnp.einsum(
        "prhe,pnhe->phrn", query_heads, key_heads, preferred_element_type=jnp.float32
    )
    bias_part = pair_bias.astype(jnp.float32)
    scores = scores + bias_part[None]
    usable = (key_mask > 0)[None, None, None, :]
    new_max = jnp.maximum(running, jnp.max(jnp.where(usable, scores, -1e30), axis=3))
    weights = jnp.where(usable, jnp.exp(scores - new_max[..., None]), 0.0)
    totals = jnp.sum(weights, axis=3)
    summed = jnp.einsum(
        "phrn,pnhe->phre",
        weights.astype(jnp.bfloat16),
        value_heads,
        preferred_element_type=jnp.float32,
    )
    return (new_max, totals, summed)


def run_block(states, pair_bias, key_mask, gain_attn, w_qkv, w_o, gain_ff, w_in, w_out):
    part_count, row_count, model_width = states.shape
    head_count = pair_bias.shape[0]
    head_size = model_width // head_count
    score_scale = 1.0 / math.sqrt(head_size)
    stream = states.astype(jnp.float32)
    normed = rms_norm(stream, gain_attn).astype(jnp.bfloat16)
    start_carry = (
        jnp.full((part_count, head_count, row_count), -1e30, jnp.float32),
        jnp.zeros((part_count, head_count, row_count), jnp.float32),
        jnp.zeros((part_count, head_count, row_count, head_size), jnp.float32),
    )
    queries = (
        jnp.einsum(
            "prd,de->pre", normed, w_qkv[:, :model_width], preferred_element_type=jnp.float32
        )
        * score_scale
    ).astype(jnp.bfloat16)
    normed_all = lax.all_gather(normed, "token", axis=1, tiled=True)
    projected = jnp.einsum(
        "prd,de->pre", normed_all, w_qkv[:, model_width:], preferred_element_type=jnp.float32
    ).astype(jnp.bfloat16)
    portion = (projected[..., :model_width], projected[..., model_width:])
    running, totals, summed = attend_portion(
        start_carry, queries, portion[0], portion[1], pair_bias, key_mask
    )
    attended = (
        (summed / totals[..., None])
        .transpose(0, 2, 1, 3)
        .reshape(part_count, row_count, model_width)
        .astype(jnp.bfloat16)
    )
    stream = stream + jnp.einsum("prd,de->pre", attended, w_o, preferred_element_type=jnp.float32)
    normed_ff = rms_norm(stream, gain_ff).astype(jnp.bfloat16)
    normed_ff = lax.all_gather(normed_ff, "token", axis=1, tiled=True)
    gate_sum = jnp.einsum("prd,df->prf", normed_ff, w_in[0], preferred_element_type=jnp.float32)
    up_sum = jnp.einsum("prd,df->prf", normed_ff, w_in[1], preferred_element_type=jnp.float32)
    hidden = (jax.nn.silu(gate_sum) * up_sum).astype(jnp.bfloat16)
    update = jnp.einsum(
        "prf,nf->prn", hidden, w_out, preferred_element_type=jnp.float32
    ).astype(jnp.bfloat16)
    update = lax.psum_scatter(update, "token", scatter_dimension=1, tiled=True)
    return (stream + update.astype(jnp.float32)).astype(jnp.bfloat16)


def select_rows(ancestors, portion):
    number = portion.shape[0]
    indices = lax.iota(jnp.int32, number)
    onehot = (ancestors[:, None] == indices[None, :]).astype(jnp.bfloat16)
    return jnp.einsum("jp,prd->jrd", onehot, portion, preferred_element_type=jnp.float32)


def body(states, ancestors, pair_bias, key_mask, gain_attn, w_qkv, w_o, gain_ff, w_in, w_out):
    chosen = select_rows(ancestors, lax.all_gather(states, "particle", axis=0, tiled=True)).astype(
        jnp.bfloat16
    )
    units = w_out.shape[1] // lax.axis_size("token")
    first = lax.axis_index("token") * units
    w_in = lax.all_gather(
        lax.dynamic_slice_in_dim(w_in, first, units, 2), "particle", axis=1, tiled=True
    )
    w_out = lax.all_gather(
        lax.dynamic_slice_in_dim(w_out, first, units, 1), "particle", axis=0, tiled=True
    )
    return run_block(chosen, pair_bias, key_mask, gain_attn, w_qkv, w_o, gain_ff, w_in, w_out)


def block_kernel(
    states_ref, ancestors_ref, bias_hbm, mask_ref, gain_attn_ref, w_qkv_hbm, w_o_hbm, gain_ff_ref,
    w_in_hbm, w_out_hbm, out_ref,
    states_all, w_in_all, w_out_all, w_qkv, w_o, bias, normed_all, kv_all, ff_all,
    core_out, core_in, row_out, row_in, wish_out, wish_in, pick_out, pick_in,
    local_sem, recv_sem, right_sem, left_sem, across_sem, gather_recv, gather_row, gather_core,
    core_send, core_recv, row_send, row_recv, wish_send, wish_recv, pick_send, pick_recv,
):
    per, rows, width = states_ref.shape
    groups = lax.axis_size("particle")
    lines = groups // 2
    cells = lax.axis_size("token")
    spans = cells // 2
    units = w_in_all.shape[-1]
    head_count = bias.shape[0] // rows
    head_size = width // head_count
    me = lax.axis_index("particle")
    spot = lax.axis_index("token")
    line, side = me // 2, me % 2
    span, core = spot // 2, spot % 2
    across = (line * 2 + 1 - side, spot)
    above, below = (me + 2, spot), (me - 2, spot)
    other_core = (me, span * 2 + 1 - core)

    def span_peer(step):
        return lax.rem(span + step, spans)

    barrier = pltpu.get_barrier_semaphore()

    def greet(device):
        pl.semaphore_signal(barrier, inc=1, device_id=device, device_id_type=MESH)

    greet(across)
    greet(other_core)
    for step in range(1, spans):
        greet((me, span_peer(step) * 2 + core))

    @pl.when(line > 0)
    def _():
        greet(below)

    @pl.when(line < lines - 1)
    def _():
        greet(above)

    first = pl.multiple_of(spot * units, 128)
    locals_ = [
        pltpu.make_async_copy(states_ref, states_all.at[pl.ds(me * per, per)], local_sem.at[0]),
        pltpu.make_async_copy(
            w_in_hbm.at[:, :, pl.ds(first, units)], w_in_all.at[me], local_sem.at[1]
        ),
        pltpu.make_async_copy(
            w_out_hbm.at[:, pl.ds(first, units)], w_out_all.at[me], local_sem.at[2]
        ),
        pltpu.make_async_copy(w_qkv_hbm, w_qkv, local_sem.at[3]),
        pltpu.make_async_copy(bias_hbm, bias, local_sem.at[4]),
        pltpu.make_async_copy(w_o_hbm, w_o, local_sem.at[5]),
    ]
    for copy in locals_:
        copy.start()
    locals_[0].wait()
    pl.semaphore_wait(
        barrier,
        2 + spans - 1 + jnp.where(line > 0, 1, 0) + jnp.where(line < lines - 1, 1, 0),
    )

    views = (
        lambda k: states_all.at[pl.ds(k * per, per)],
        lambda k: w_in_all.at[k],
        lambda k: w_out_all.at[k],
    )

    def remote(kind, source, sems, device):
        k = source * 2 + side
        return pltpu.make_async_remote_copy(
            src_ref=views[kind](k),
            dst_ref=views[kind](k),
            send_sem=sems.at[kind, source],
            recv_sem=recv_sem.at[kind, k],
            device_id=device,
            device_id_type=MESH,
        )

    def arrived(kind, k):
        pltpu.make_async_remote_copy(
            src_ref=views[kind](k),
            dst_ref=views[kind](k),
            send_sem=across_sem.at[kind, 0],
            recv_sem=recv_sem.at[kind, k],
            device_id=across,
            device_id_type=MESH,
        ).wait_recv()

    def relay(kind, step, along=True, cross=True):
        low, high = line - step, line + step

        @pl.when(low >= 0)
        def _():
            if step > 0:
                arrived(kind, low * 2 + side)

            @pl.when(jnp.logical_and(along, line < lines - 1))
            def _():
                remote(kind, low, right_sem, above).start()

        @pl.when(high < lines)
        def _():
            if step > 0:
                arrived(kind, high * 2 + side)

            @pl.when(jnp.logical_and(along, line > 0))
            def _():
                remote(kind, high, left_sem, below).start()

        if kind == 0 or not cross:
            return

        @pl.when(low >= 0)
        def _():
            remote(kind, low, across_sem, across).start()

        if step > 0:

            @pl.when(high < lines)
            def _():
                remote(kind, high, across_sem, across).start()

    def finish(kind):
        for source in range(lines):
            arrived(kind, source * 2 + 1 - side)

    def drain(kind):
        for source in range(lines):
            if kind > 0:
                remote(kind, source, across_sem, across).wait_send()

            @pl.when(jnp.logical_and(line < lines - 1, source <= line))
            def _():
                remote(kind, source, right_sem, above).wait_send()

            @pl.when(jnp.logical_and(line > 0, source >= line))
            def _():
                remote(kind, source, left_sem, below).wait_send()

    def slot_copy(which, buf, j, slot, send, device):
        return pltpu.make_async_remote_copy(
            src_ref=buf.at[j, slot],
            dst_ref=buf.at[j, slot],
            send_sem=send,
            recv_sem=gather_recv.at[which, j, slot],
            device_id=device,
            device_id_type=MESH,
        )

    sent = []

    def token_sends(which, buf, j):
        for step in range(1, spans):
            device = (me, span_peer(step) * 2 + core)
            sent.append(slot_copy(which, buf, j, spot, gather_row.at[which, j, step], device))
            sent[-1].start()
        sent.append(slot_copy(which, buf, j, spot, gather_core.at[which, j, 0], other_core))
        sent[-1].start()

    def token_forward(which, buf, j):
        for step in range(1, spans):
            slot = span_peer(step) * 2 + core
            copy = slot_copy(which, buf, j, slot, gather_core.at[which, j, step], other_core)
            copy.wait_recv()
            copy.start()
            sent.append(copy)

    def token_finish(which, buf, j):
        for step in range(spans):
            slot = span_peer(step) * 2 + 1 - core
            slot_copy(
                which, buf, j, slot, gather_core.at[which, j, 0], other_core
            ).wait_recv()

    def norm(stream, gain):
        mean = jnp.mean(stream * stream, axis=-1, keepdims=True)
        return (stream * lax.rsqrt(mean + 1e-05) * gain).astype(jnp.bfloat16)

    def dot(a, b):
        return jnp.dot(a, b, preferred_element_type=jnp.float32)

    def dot_t(a, b):
        return lax.dot_general(
            a, b, (((1,), (1,)), ((), ())), preferred_element_type=jnp.float32
        )

    tokens = cells * rows
    last = lines - 1
    for j in range(per):
        wish_out[j] = jnp.full(wish_out.shape[1:], ancestors_ref[j], jnp.int32)

    def to_across(source, target, send, recv):
        return pltpu.make_async_remote_copy(
            src_ref=source,
            dst_ref=target,
            send_sem=send,
            recv_sem=recv,
            device_id=across,
            device_id_type=MESH,
        )

    def own_weights_along(step):
        @pl.when(jnp.logical_and(line == step, line < last))
        def _():
            remote(1, line, right_sem, above).start()

        @pl.when(jnp.logical_and(line == last - step, line > 0))
        def _():
            remote(1, line, left_sem, below).start()

    wish = to_across(wish_out, wish_in, wish_send, wish_recv)
    wish.start()
    relay(0, 0)
    locals_[1].wait()
    relay(1, 0, along=False)
    locals_[2].wait()
    relay(2, 0, along=False)
    own_weights_along(0)
    wish.wait_recv()

    def pick_from(found, wished, source):
        for i in range(per):
            k = (source * 2 + side) * per + i
            found = jnp.where(wished[:1, :1] == k, states_all[k].astype(jnp.float32), found)
        return found

    nothing = jnp.zeros((rows, width), jnp.float32)
    asked = [pick_from(nothing, wish_in[j], line) for j in range(per)]
    for step in range(1, lines):
        relay(0, step)
        own_weights_along(step)
        for source in (jnp.maximum(line - step, 0), jnp.minimum(line + step, last)):
            if step < last:
                asked = [pick_from(asked[j], wish_in[j], source) for j in range(per)]
    picks = []
    for j in range(per):
        if last > 0:
            for source in (0, last):
                asked[j] = pick_from(asked[j], wish_in[j], source)
        pick_out[j] = asked[j].astype(jnp.bfloat16)
        picks.append(to_across(pick_out.at[j], pick_in.at[j], pick_send.at[j], pick_recv.at[j]))
        picks[j].start()
    own = []
    for j in range(per):
        found = nothing
        for source in range(lines):
            found = pick_from(found, wish_out[j], source)
        own.append(found)
    if lines > 1:
        relay(1, 1)

    gain = gain_attn_ref[...].reshape(1, width)
    streams, normed = [], []
    for j in range(per):
        picks[j].wait_recv()
        streams.append(own[j] + pick_in[j].astype(jnp.float32))
        normed.append(norm(streams[j], gain))
        normed_all[j, spot] = normed[j]
        token_sends(0, normed_all, j)
    locals_[3].wait()
    scale = 1.0 / math.sqrt(head_size)
    queries = (dot(jnp.concatenate(normed, axis=0), w_qkv[:, :width]) * scale).astype(jnp.bfloat16)
    token_forward(0, normed_all, 0)
    for step in range(2, last):
        relay(1, step)
    relay(2, 0, cross=False)

    usable = mask_ref[...].reshape(1, -1) > 0
    half = 8
    strip = half * head_size
    lane = lax.broadcasted_iota(jnp.int32, (half, 1, strip), 2)
    head = lax.broadcasted_iota(jnp.int32, (half, 1, strip), 0)
    mine = jnp.logical_and(lane >= head * head_size, lane < (head + 1) * head_size)
    mine_f = mine.astype(jnp.float32)
    mine_bf = mine_f.astype(jnp.bfloat16)

    def make_keys(j):
        kv_all[j] = dot(normed_all[j].reshape(tokens, width), w_qkv[:, width:]).astype(
            jnp.bfloat16
        )

    def attend(j):
        strips = []
        for part in range(head_count // half):
            low, high = part * strip, (part + 1) * strip
            q = queries[j * rows : (j + 1) * rows, low:high]
            spread = (q[None] * mine_bf).reshape(half * rows, strip)
            scores = dot_t(spread, kv_all[j, :, low:high]) + bias[
                part * half * rows : (part + 1) * half * rows, :
            ].astype(jnp.float32)
            scores = jnp.where(usable, scores, -1e30)
            weights = jnp.exp(scores - jnp.max(scores, axis=1, keepdims=True))
            total = jnp.sum(weights, axis=1, keepdims=True)
            mix = dot(weights.astype(jnp.bfloat16), kv_all[j, :, width + low : width + high])
            mix = mix * (1.0 / total)
            strips.append(jnp.sum(mix.reshape(half, rows, strip) * mine_f, axis=0))
        return jnp.concatenate(strips, axis=1).astype(jnp.bfloat16)

    def close(j, attended):
        streams[j] = streams[j] + dot(attended, w_o[...])
        ff_all[j, spot] = norm(streams[j], gain_ff_ref[...].reshape(1, width))
        token_sends(1, ff_all, j)

    token_finish(0, normed_all, 0)
    make_keys(0)
    for j in range(1, per):
        token_forward(0, normed_all, j)
    locals_[4].wait()
    attended = attend(0)
    locals_[5].wait()
    close(0, attended)
    if lines > 2:
        relay(1, last)
    if lines > 1:
        relay(2, 1)
    for j in range(1, per):
        token_finish(0, normed_all, j)
        make_keys(j)
        if j == 1:
            for step in range(2, last):
                relay(2, step)
        attended = attend(j)
        token_forward(1, ff_all, j - 1)
        close(j, attended)
    if lines > 2:
        relay(2, last)
    finish(1)

    is_low = core == 0
    kept, cored, rowed = [], [], []

    def to_core(j):
        return pltpu.make_async_remote_copy(
            src_ref=core_out.at[j],
            dst_ref=core_in.at[j],
            send_sem=core_send.at[j],
            recv_sem=core_recv.at[j],
            device_id=other_core,
            device_id_type=MESH,
        )

    def to_row(j, step):
        return pltpu.make_async_remote_copy(
            src_ref=row_out.at[j, span_peer(step)],
            dst_ref=row_in.at[j, step],
            send_sem=row_send.at[j, step],
            recv_sem=row_recv.at[j, step],
            device_id=(me, span_peer(step) * 2 + core),
            device_id_type=MESH,
        )

    def send_rows(j):
        cored[j].wait_recv()
        row_out[j] = (kept[j] + core_in[j].astype(jnp.float32)).astype(jnp.bfloat16)
        for step in range(1, spans):
            rowed.append(to_row(j, step))
            rowed[-1].start()

    for j in range(per):
        token_finish(1, ff_all, j)
        normed_ff = ff_all[j].reshape(tokens, width)
        gate = dot(normed_ff, w_in_all[:, 0].reshape(width, units))
        up = dot(normed_ff, w_in_all[:, 1].reshape(width, units))
        hidden = (gate / (1.0 + jnp.exp(-gate)) * up).astype(jnp.bfloat16)
        if j == 0:
            finish(2)
        if j + 1 == per - 1:
            token_forward(1, ff_all, per - 1)
        if j > 0:
            send_rows(j - 1)
        update = dot_t(hidden, w_out_all[...].reshape(width, units))
        update = update.reshape(spans, 2, rows, width)
        core_out[j] = jnp.where(is_low, update[:, 1], update[:, 0]).astype(jnp.bfloat16)
        cored.append(to_core(j))
        cored[j].start()
        kept.append(jnp.where(is_low, update[:, 0], update[:, 1]))
    send_rows(per - 1)
    for j in range(per):
        stream = streams[j] + row_out[j, span].astype(jnp.float32)
        for step in range(1, spans):
            to_row(j, step).wait_recv()
            stream = stream + row_in[j, step].astype(jnp.float32)
        out_ref[j] = stream.astype(jnp.bfloat16)
    for copy in sent + cored + rowed + [wish] + picks:
        copy.wait_send()
    for kind in range(3):
        drain(kind)


def fused_body(
    states, ancestors, pair_bias, key_mask, gain_attn, w_qkv, w_o, gain_ff, w_in, w_out
):
    per, rows, width = states.shape
    groups, cells = lax.axis_size("particle"), lax.axis_size("token")
    lines, spans = groups // 2, cells // 2
    units = w_out.shape[1] // cells
    depth = w_in.shape[1]
    heads, _, keys = pair_bias.shape
    vmem = pl.BlockSpec(memory_space=pltpu.VMEM)
    smem = pl.BlockSpec(memory_space=pltpu.SMEM)
    hbm = pl.BlockSpec(memory_space=pl.ANY)
    dma = pltpu.SemaphoreType.DMA
    bf16 = jnp.bfloat16
    block = (rows, width)
    return pl.pallas_call(
        block_kernel,
        out_shape=jax.ShapeDtypeStruct(states.shape, bf16),
        in_specs=[vmem, smem, hbm, vmem, vmem, hbm, hbm, vmem, hbm, hbm],
        out_specs=vmem,
        scratch_shapes=[
            pltpu.VMEM((groups * per, rows, width), bf16),
            pltpu.VMEM((groups, 2, depth, units), bf16),
            pltpu.VMEM((groups, depth, units), bf16),
            pltpu.VMEM(w_qkv.shape, bf16),
            pltpu.VMEM(w_o.shape, bf16),
            pltpu.VMEM((heads * rows, keys), bf16),
            pltpu.VMEM((per, cells) + block, bf16),
            pltpu.VMEM((per, cells * rows, 2 * width), bf16),
            pltpu.VMEM((per, cells) + block, bf16),
            pltpu.VMEM((per, spans) + block, bf16),
            pltpu.VMEM((per, spans) + block, bf16),
            pltpu.VMEM((per, spans) + block, bf16),
            pltpu.VMEM((per, spans) + block, bf16),
            pltpu.VMEM((per, 8, 128), jnp.int32),
            pltpu.VMEM((per, 8, 128), jnp.int32),
            pltpu.VMEM((per, rows, width), bf16),
            pltpu.VMEM((per, rows, width), bf16),
            dma((6,)),
            dma((3, groups)),
            dma((3, lines)),
            dma((3, lines)),
            dma((3, lines)),
            dma((2, per, cells)),
            dma((2, per, spans)),
            dma((2, per, spans)),
            dma((per,)),
            dma((per,)),
            dma((per, spans)),
            dma((per, spans)),
            dma,
            dma,
            dma((per,)),
            dma((per,)),
        ],
        compiler_params=pltpu.CompilerParams(
            collective_id=0, has_side_effects=True, vmem_limit_bytes=56 * 1024 * 1024
        ),
    )(
        states,
        ancestors,
        pair_bias.reshape(heads * rows, keys),
        key_mask,
        gain_attn,
        w_qkv,
        w_o,
        gain_ff,
        w_in,
        w_out,
    )


def either_body(states, ancestors, pair_bias, key_mask, gain_attn, w_qkv, w_o, gain_ff, w_in, w_out):
    tiles = w_in.shape[1] % 16 == 0 and (w_out.shape[1] // lax.axis_size("token")) % 128 == 0
    run = fused_body if tiles else body
    return run(
        states, ancestors, pair_bias, key_mask, gain_attn, w_qkv, w_o, gain_ff, w_in, w_out
    )


def solution(mesh):
    placed = (
        P("particle", "token", None),
        P("particle"),
        P(None, "token", None),
        P(),
        P(),
        P(),
        P(),
        P(),
        P(None, "particle", None),
        P("particle", None),
    )
    return jax.shard_map(
        either_body, mesh=mesh, in_specs=placed, out_specs=P("particle", "token", None), check_vma=False
    )
```

```python
import math

import jax
import jax.numpy as jnp
from jax import lax
from jax.experimental import pallas as pl
from jax.experimental.pallas import tpu as pltpu
from jax.sharding import PartitionSpec as P

MESH = pl.DeviceIdType.MESH


def rms_norm(stream, gain_vec):
    return stream * lax.rsqrt(jnp.mean(stream * stream, axis=-1, keepdims=True) + 1e-05) * gain_vec


def attend_portion(running_sum, queries, key_part, value_part, pair_bias, key_mask):
    running, totals, summed = running_sum
    part_count, row_count, model_width = queries.shape
    head_count = pair_bias.shape[0]
    head_size = model_width // head_count
    number = key_part.shape[1]
    query_heads = queries.reshape(part_count, row_count, head_count, head_size)
    key_heads = key_part.reshape(part_count, number, head_count, head_size)
    value_heads = value_part.reshape(part_count, number, head_count, head_size)
    scores = jnp.einsum(
        "prhe,pnhe->phrn", query_heads, key_heads, preferred_element_type=jnp.float32
    )
    bias_part = pair_bias.astype(jnp.float32)
    scores = scores + bias_part[None]
    usable = (key_mask > 0)[None, None, None, :]
    new_max = jnp.maximum(running, jnp.max(jnp.where(usable, scores, -1e30), axis=3))
    weights = jnp.where(usable, jnp.exp(scores - new_max[..., None]), 0.0)
    totals = jnp.sum(weights, axis=3)
    summed = jnp.einsum(
        "phrn,pnhe->phre",
        weights.astype(jnp.bfloat16),
        value_heads,
        preferred_element_type=jnp.float32,
    )
    return (new_max, totals, summed)


def run_block(states, pair_bias, key_mask, gain_attn, w_qkv, w_o, gain_ff, w_in, w_out):
    part_count, row_count, model_width = states.shape
    head_count = pair_bias.shape[0]
    head_size = model_width // head_count
    score_scale = 1.0 / math.sqrt(head_size)
    stream = states.astype(jnp.float32)
    normed = rms_norm(stream, gain_attn).astype(jnp.bfloat16)
    start_carry = (
        jnp.full((part_count, head_count, row_count), -1e30, jnp.float32),
        jnp.zeros((part_count, head_count, row_count), jnp.float32),
        jnp.zeros((part_count, head_count, row_count, head_size), jnp.float32),
    )
    queries = (
        jnp.einsum(
            "prd,de->pre", normed, w_qkv[:, :model_width], preferred_element_type=jnp.float32
        )
        * score_scale
    ).astype(jnp.bfloat16)
    normed_all = lax.all_gather(normed, "token", axis=1, tiled=True)
    projected = jnp.einsum(
        "prd,de->pre", normed_all, w_qkv[:, model_width:], preferred_element_type=jnp.float32
    ).astype(jnp.bfloat16)
    portion = (projected[..., :model_width], projected[..., model_width:])
    running, totals, summed = attend_portion(
        start_carry, queries, portion[0], portion[1], pair_bias, key_mask
    )
    attended = (
        (summed / totals[..., None])
        .transpose(0, 2, 1, 3)
        .reshape(part_count, row_count, model_width)
        .astype(jnp.bfloat16)
    )
    stream = stream + jnp.einsum("prd,de->pre", attended, w_o, preferred_element_type=jnp.float32)
    normed_ff = rms_norm(stream, gain_ff).astype(jnp.bfloat16)
    normed_ff = lax.all_gather(normed_ff, "token", axis=1, tiled=True)
    gate_sum = jnp.einsum("prd,df->prf", normed_ff, w_in[0], preferred_element_type=jnp.float32)
    up_sum = jnp.einsum("prd,df->prf", normed_ff, w_in[1], preferred_element_type=jnp.float32)
    hidden = (jax.nn.silu(gate_sum) * up_sum).astype(jnp.bfloat16)
    update = jnp.einsum(
        "prf,nf->prn", hidden, w_out, preferred_element_type=jnp.float32
    ).astype(jnp.bfloat16)
    update = lax.psum_scatter(update, "token", scatter_dimension=1, tiled=True)
    return (stream + update.astype(jnp.float32)).astype(jnp.bfloat16)


def select_rows(ancestors, portion):
    number = portion.shape[0]
    indices = lax.iota(jnp.int32, number)
    onehot = (ancestors[:, None] == indices[None, :]).astype(jnp.bfloat16)
    return jnp.einsum("jp,prd->jrd", onehot, portion, preferred_element_type=jnp.float32)


def body(states, ancestors, pair_bias, key_mask, gain_attn, w_qkv, w_o, gain_ff, w_in, w_out):
    chosen = select_rows(ancestors, lax.all_gather(states, "particle", axis=0, tiled=True)).astype(
        jnp.bfloat16
    )
    units = w_out.shape[1] // lax.axis_size("token")
    first = lax.axis_index("token") * units
    w_in = lax.all_gather(
        lax.dynamic_slice_in_dim(w_in, first, units, 2), "particle", axis=1, tiled=True
    )
    w_out = lax.all_gather(
        lax.dynamic_slice_in_dim(w_out, first, units, 1), "particle", axis=0, tiled=True
    )
    return run_block(chosen, pair_bias, key_mask, gain_attn, w_qkv, w_o, gain_ff, w_in, w_out)


def block_kernel(
    states_ref, ancestors_ref, bias_hbm, mask_ref, gain_attn_ref, w_qkv_hbm, w_o_hbm, gain_ff_ref,
    w_in_hbm, w_out_hbm, out_ref,
    states_all, w_in_all, w_out_all, w_qkv, w_o, bias, normed_all, kv_all, ff_all,
    core_out, core_in, row_out, row_in, wish_out, wish_in, pick_out, pick_in,
    local_sem, recv_sem, right_sem, left_sem, across_sem, gather_recv, gather_row, gather_core,
    core_send, core_recv, row_send, row_recv, wish_send, wish_recv, pick_send, pick_recv,
):
    per, rows, width = states_ref.shape
    groups = lax.axis_size("particle")
    lines = groups // 2
    cells = lax.axis_size("token")
    spans = cells // 2
    units = w_in_all.shape[-1]
    head_count = bias.shape[0] // rows
    head_size = width // head_count
    me = lax.axis_index("particle")
    spot = lax.axis_index("token")
    line, side = me // 2, me % 2
    span, core = spot // 2, spot % 2
    across = (line * 2 + 1 - side, spot)
    above, below = (me + 2, spot), (me - 2, spot)
    other_core = (me, span * 2 + 1 - core)

    def span_peer(step):
        return lax.rem(span + step, spans)

    barrier = pltpu.get_barrier_semaphore()

    def greet(device):
        pl.semaphore_signal(barrier, inc=1, device_id=device, device_id_type=MESH)

    greet(across)
    greet(other_core)
    for step in range(1, spans):
        greet((me, span_peer(step) * 2 + core))

    @pl.when(line > 0)
    def _():
        greet(below)

    @pl.when(line < lines - 1)
    def _():
        greet(above)

    first = pl.multiple_of(spot * units, 128)
    locals_ = [
        pltpu.make_async_copy(states_ref, states_all.at[pl.ds(me * per, per)], local_sem.at[0]),
        pltpu.make_async_copy(
            w_in_hbm.at[:, :, pl.ds(first, units)], w_in_all.at[me], local_sem.at[1]
        ),
        pltpu.make_async_copy(
            w_out_hbm.at[:, pl.ds(first, units)], w_out_all.at[me], local_sem.at[2]
        ),
        pltpu.make_async_copy(w_qkv_hbm, w_qkv, local_sem.at[3]),
        pltpu.make_async_copy(bias_hbm, bias, local_sem.at[4]),
        pltpu.make_async_copy(w_o_hbm, w_o, local_sem.at[5]),
    ]
    for copy in locals_:
        copy.start()
    locals_[0].wait()
    pl.semaphore_wait(
        barrier,
        2 + spans - 1 + jnp.where(line > 0, 1, 0) + jnp.where(line < lines - 1, 1, 0),
    )

    views = (
        lambda k: states_all.at[pl.ds(k * per, per)],
        lambda k: w_in_all.at[k],
        lambda k: w_out_all.at[k],
    )

    def remote(kind, source, sems, device):
        k = source * 2 + side
        return pltpu.make_async_remote_copy(
            src_ref=views[kind](k),
            dst_ref=views[kind](k),
            send_sem=sems.at[kind, source],
            recv_sem=recv_sem.at[kind, k],
            device_id=device,
            device_id_type=MESH,
        )

    def arrived(kind, k):
        pltpu.make_async_remote_copy(
            src_ref=views[kind](k),
            dst_ref=views[kind](k),
            send_sem=across_sem.at[kind, 0],
            recv_sem=recv_sem.at[kind, k],
            device_id=across,
            device_id_type=MESH,
        ).wait_recv()

    def relay(kind, step, along=True, cross=True):
        low, high = line - step, line + step

        @pl.when(low >= 0)
        def _():
            if step > 0:
                arrived(kind, low * 2 + side)

            @pl.when(jnp.logical_and(along, line < lines - 1))
            def _():
                remote(kind, low, right_sem, above).start()

        @pl.when(high < lines)
        def _():
            if step > 0:
                arrived(kind, high * 2 + side)

            @pl.when(jnp.logical_and(along, line > 0))
            def _():
                remote(kind, high, left_sem, below).start()

        if kind == 0 or not cross:
            return

        @pl.when(low >= 0)
        def _():
            remote(kind, low, across_sem, across).start()

        if step > 0:

            @pl.when(high < lines)
            def _():
                remote(kind, high, across_sem, across).start()

    def finish(kind):
        for source in range(lines):
            arrived(kind, source * 2 + 1 - side)

    def drain(kind):
        for source in range(lines):
            if kind > 0:
                remote(kind, source, across_sem, across).wait_send()

            @pl.when(jnp.logical_and(line < lines - 1, source <= line))
            def _():
                remote(kind, source, right_sem, above).wait_send()

            @pl.when(jnp.logical_and(line > 0, source >= line))
            def _():
                remote(kind, source, left_sem, below).wait_send()

    def slot_copy(which, buf, j, slot, send, device):
        return pltpu.make_async_remote_copy(
            src_ref=buf.at[j, slot],
            dst_ref=buf.at[j, slot],
            send_sem=send,
            recv_sem=gather_recv.at[which, j, slot],
            device_id=device,
            device_id_type=MESH,
        )

    sent = []

    def token_sends(which, buf, j):
        for step in range(1, spans):
            device = (me, span_peer(step) * 2 + core)
            sent.append(slot_copy(which, buf, j, spot, gather_row.at[which, j, step], device))
            sent[-1].start()
        sent.append(slot_copy(which, buf, j, spot, gather_core.at[which, j, 0], other_core))
        sent[-1].start()

    def token_forward(which, buf, j):
        for step in range(1, spans):
            slot = span_peer(step) * 2 + core
            copy = slot_copy(which, buf, j, slot, gather_core.at[which, j, step], other_core)
            copy.wait_recv()
            copy.start()
            sent.append(copy)

    def token_finish(which, buf, j, steps=range(spans)):
        for step in steps:
            slot = span_peer(step) * 2 + 1 - core
            slot_copy(
                which, buf, j, slot, gather_core.at[which, j, 0], other_core
            ).wait_recv()

    def norm(stream, gain):
        mean = jnp.mean(stream * stream, axis=-1, keepdims=True)
        return (stream * lax.rsqrt(mean + 1e-05) * gain).astype(jnp.bfloat16)

    def dot(a, b):
        return jnp.dot(a, b, preferred_element_type=jnp.float32)

    def dot_t(a, b):
        return lax.dot_general(
            a, b, (((1,), (1,)), ((), ())), preferred_element_type=jnp.float32
        )

    tokens = cells * rows
    last = lines - 1
    for j in range(per):
        wish_out[j] = jnp.full(wish_out.shape[1:], ancestors_ref[j], jnp.int32)

    def to_across(source, target, send, recv):
        return pltpu.make_async_remote_copy(
            src_ref=source,
            dst_ref=target,
            send_sem=send,
            recv_sem=recv,
            device_id=across,
            device_id_type=MESH,
        )

    def own_weights_along(step):
        @pl.when(jnp.logical_and(line == step, line < last))
        def _():
            remote(1, line, right_sem, above).start()

        @pl.when(jnp.logical_and(line == last - step, line > 0))
        def _():
            remote(1, line, left_sem, below).start()

    wish = to_across(wish_out, wish_in, wish_send, wish_recv)
    wish.start()
    relay(0, 0)
    locals_[1].wait()
    relay(1, 0, along=False)
    locals_[2].wait()
    relay(2, 0, along=False)
    own_weights_along(0)
    wish.wait_recv()

    def pick_from(found, wished, source):
        for i in range(per):
            k = (source * 2 + side) * per + i
            found = jnp.where(wished[:1, :1] == k, states_all[k].astype(jnp.float32), found)
        return found

    nothing = jnp.zeros((rows, width), jnp.float32)
    asked = [pick_from(nothing, wish_in[j], line) for j in range(per)]
    for step in range(1, lines):
        relay(0, step)
        own_weights_along(step)
        for source in (jnp.maximum(line - step, 0), jnp.minimum(line + step, last)):
            if step < last:
                asked = [pick_from(asked[j], wish_in[j], source) for j in range(per)]
    picks = []
    for j in range(per):
        if last > 0:
            for source in (0, last):
                asked[j] = pick_from(asked[j], wish_in[j], source)
        pick_out[j] = asked[j].astype(jnp.bfloat16)
        picks.append(to_across(pick_out.at[j], pick_in.at[j], pick_send.at[j], pick_recv.at[j]))
        picks[j].start()
    own = []
    for j in range(per):
        found = nothing
        for source in range(lines):
            found = pick_from(found, wish_out[j], source)
        own.append(found)
    if lines > 1:
        relay(1, 1)

    gain = gain_attn_ref[...].reshape(1, width)
    streams, normed = [], []
    for j in range(per):
        picks[j].wait_recv()
        streams.append(own[j] + pick_in[j].astype(jnp.float32))
        normed.append(norm(streams[j], gain))
        normed_all[j, spot] = normed[j]
        token_sends(0, normed_all, j)
    locals_[3].wait()

    def make_span_keys(j, step):
        start = span_peer(step) * 2
        kv_all[j, pl.ds(pl.multiple_of(start * rows, 2 * rows), 2 * rows)] = dot(
            normed_all[j, pl.ds(start, 2)].reshape(2 * rows, width), w_qkv[:, width:]
        ).astype(jnp.bfloat16)

    scale = 1.0 / math.sqrt(head_size)
    queries = (dot(jnp.concatenate(normed, axis=0), w_qkv[:, :width]) * scale).astype(jnp.bfloat16)
    token_finish(0, normed_all, 0, range(1))
    make_span_keys(0, 0)
    token_forward(0, normed_all, 0)
    for step in range(2, last):
        relay(1, step)
    relay(2, 0, cross=False)

    usable = mask_ref[...].reshape(1, -1) > 0
    half = 8
    strip = half * head_size
    lane = lax.broadcasted_iota(jnp.int32, (half, 1, strip), 2)
    head = lax.broadcasted_iota(jnp.int32, (half, 1, strip), 0)
    mine = jnp.logical_and(lane >= head * head_size, lane < (head + 1) * head_size)
    mine_f = mine.astype(jnp.float32)
    mine_bf = mine_f.astype(jnp.bfloat16)

    def make_keys(j):
        kv_all[j] = dot(normed_all[j].reshape(tokens, width), w_qkv[:, width:]).astype(
            jnp.bfloat16
        )

    def attend(j):
        strips = []
        for part in range(head_count // half):
            low, high = part * strip, (part + 1) * strip
            q = queries[j * rows : (j + 1) * rows, low:high]
            spread = (q[None] * mine_bf).reshape(half * rows, strip)
            scores = dot_t(spread, kv_all[j, :, low:high]) + bias[
                part * half * rows : (part + 1) * half * rows, :
            ].astype(jnp.float32)
            scores = jnp.where(usable, scores, -1e30)
            weights = jnp.exp(scores - jnp.max(scores, axis=1, keepdims=True))
            total = jnp.sum(weights, axis=1, keepdims=True)
            mix = dot(weights.astype(jnp.bfloat16), kv_all[j, :, width + low : width + high])
            mix = mix * (1.0 / total)
            strips.append(jnp.sum(mix.reshape(half, rows, strip) * mine_f, axis=0))
        return jnp.concatenate(strips, axis=1).astype(jnp.bfloat16)

    def close(j, attended):
        streams[j] = streams[j] + dot(attended, w_o[...])
        ff_all[j, spot] = norm(streams[j], gain_ff_ref[...].reshape(1, width))
        token_sends(1, ff_all, j)

    token_finish(0, normed_all, 0, range(1, spans))
    for step in range(1, spans):
        make_span_keys(0, step)
    for j in range(1, per):
        token_forward(0, normed_all, j)
    locals_[4].wait()
    attended = attend(0)
    locals_[5].wait()
    close(0, attended)
    if lines > 2:
        relay(1, last)
    if lines > 1:
        relay(2, 1)
    for j in range(1, per):
        token_finish(0, normed_all, j)
        make_keys(j)
        if j == 1:
            for step in range(2, last):
                relay(2, step)
        attended = attend(j)
        token_forward(1, ff_all, j - 1)
        close(j, attended)
    finish(1)

    is_low = core == 0
    kept, cored, rowed = [], [], []

    def to_core(j):
        return pltpu.make_async_remote_copy(
            src_ref=core_out.at[j],
            dst_ref=core_in.at[j],
            send_sem=core_send.at[j],
            recv_sem=core_recv.at[j],
            device_id=other_core,
            device_id_type=MESH,
        )

    def to_row(j, step):
        return pltpu.make_async_remote_copy(
            src_ref=row_out.at[j, span_peer(step)],
            dst_ref=row_in.at[j, step],
            send_sem=row_send.at[j, step],
            recv_sem=row_recv.at[j, step],
            device_id=(me, span_peer(step) * 2 + core),
            device_id_type=MESH,
        )

    def send_rows(j):
        cored[j].wait_recv()
        row_out[j] = (kept[j] + core_in[j].astype(jnp.float32)).astype(jnp.bfloat16)
        for step in range(1, spans):
            rowed.append(to_row(j, step))
            rowed[-1].start()

    for j in range(per):
        token_finish(1, ff_all, j)
        normed_ff = ff_all[j].reshape(tokens, width)
        gate = dot(normed_ff, w_in_all[:, 0].reshape(width, units))
        up = dot(normed_ff, w_in_all[:, 1].reshape(width, units))
        hidden = (gate / (1.0 + jnp.exp(-gate)) * up).astype(jnp.bfloat16)
        if j == 0:
            if lines > 2:
                relay(2, last)
            finish(2)
        if j + 1 == per - 1:
            token_forward(1, ff_all, per - 1)
        if j > 0:
            send_rows(j - 1)
        update = dot_t(hidden, w_out_all[...].reshape(width, units))
        update = update.reshape(spans, 2, rows, width)
        core_out[j] = jnp.where(is_low, update[:, 1], update[:, 0]).astype(jnp.bfloat16)
        cored.append(to_core(j))
        cored[j].start()
        kept.append(jnp.where(is_low, update[:, 0], update[:, 1]))
    send_rows(per - 1)
    for j in range(per):
        stream = streams[j] + row_out[j, span].astype(jnp.float32)
        for step in range(1, spans):
            to_row(j, step).wait_recv()
            stream = stream + row_in[j, step].astype(jnp.float32)
        out_ref[j] = stream.astype(jnp.bfloat16)
    for copy in sent + cored + rowed + [wish] + picks:
        copy.wait_send()
    for kind in range(3):
        drain(kind)


def fused_body(
    states, ancestors, pair_bias, key_mask, gain_attn, w_qkv, w_o, gain_ff, w_in, w_out
):
    per, rows, width = states.shape
    groups, cells = lax.axis_size("particle"), lax.axis_size("token")
    lines, spans = groups // 2, cells // 2
    units = w_out.shape[1] // cells
    depth = w_in.shape[1]
    heads, _, keys = pair_bias.shape
    vmem = pl.BlockSpec(memory_space=pltpu.VMEM)
    smem = pl.BlockSpec(memory_space=pltpu.SMEM)
    hbm = pl.BlockSpec(memory_space=pl.ANY)
    dma = pltpu.SemaphoreType.DMA
    bf16 = jnp.bfloat16
    block = (rows, width)
    return pl.pallas_call(
        block_kernel,
        out_shape=jax.ShapeDtypeStruct(states.shape, bf16),
        in_specs=[vmem, smem, hbm, vmem, vmem, hbm, hbm, vmem, hbm, hbm],
        out_specs=vmem,
        scratch_shapes=[
            pltpu.VMEM((groups * per, rows, width), bf16),
            pltpu.VMEM((groups, 2, depth, units), bf16),
            pltpu.VMEM((groups, depth, units), bf16),
            pltpu.VMEM(w_qkv.shape, bf16),
            pltpu.VMEM(w_o.shape, bf16),
            pltpu.VMEM((heads * rows, keys), bf16),
            pltpu.VMEM((per, cells) + block, bf16),
            pltpu.VMEM((per, cells * rows, 2 * width), bf16),
            pltpu.VMEM((per, cells) + block, bf16),
            pltpu.VMEM((per, spans) + block, bf16),
            pltpu.VMEM((per, spans) + block, bf16),
            pltpu.VMEM((per, spans) + block, bf16),
            pltpu.VMEM((per, spans) + block, bf16),
            pltpu.VMEM((per, 8, 128), jnp.int32),
            pltpu.VMEM((per, 8, 128), jnp.int32),
            pltpu.VMEM((per, rows, width), bf16),
            pltpu.VMEM((per, rows, width), bf16),
            dma((6,)),
            dma((3, groups)),
            dma((3, lines)),
            dma((3, lines)),
            dma((3, lines)),
            dma((2, per, cells)),
            dma((2, per, spans)),
            dma((2, per, spans)),
            dma((per,)),
            dma((per,)),
            dma((per, spans)),
            dma((per, spans)),
            dma,
            dma,
            dma((per,)),
            dma((per,)),
        ],
        compiler_params=pltpu.CompilerParams(
            collective_id=0, has_side_effects=True, vmem_limit_bytes=56 * 1024 * 1024
        ),
    )(
        states,
        ancestors,
        pair_bias.reshape(heads * rows, keys),
        key_mask,
        gain_attn,
        w_qkv,
        w_o,
        gain_ff,
        w_in,
        w_out,
    )


def either_body(states, ancestors, pair_bias, key_mask, gain_attn, w_qkv, w_o, gain_ff, w_in, w_out):
    tiles = w_in.shape[1] % 16 == 0 and (w_out.shape[1] // lax.axis_size("token")) % 128 == 0
    run = fused_body if tiles else body
    return run(
        states, ancestors, pair_bias, key_mask, gain_attn, w_qkv, w_o, gain_ff, w_in, w_out
    )


def solution(mesh):
    placed = (
        P("particle", "token", None),
        P("particle"),
        P(None, "token", None),
        P(),
        P(),
        P(),
        P(),
        P(),
        P(None, "particle", None),
        P("particle", None),
    )
    return jax.shard_map(
        either_body, mesh=mesh, in_specs=placed, out_specs=P("particle", "token", None), check_vma=False
    )
```

```python
import math

import jax
import jax.numpy as jnp
from jax import lax
from jax.experimental import pallas as pl
from jax.experimental.pallas import tpu as pltpu
from jax.sharding import PartitionSpec as P

MESH = pl.DeviceIdType.MESH


def rms_norm(stream, gain_vec):
    return stream * lax.rsqrt(jnp.mean(stream * stream, axis=-1, keepdims=True) + 1e-05) * gain_vec


def attend_portion(running_sum, queries, key_part, value_part, pair_bias, key_mask):
    running, totals, summed = running_sum
    part_count, row_count, model_width = queries.shape
    head_count = pair_bias.shape[0]
    head_size = model_width // head_count
    number = key_part.shape[1]
    query_heads = queries.reshape(part_count, row_count, head_count, head_size)
    key_heads = key_part.reshape(part_count, number, head_count, head_size)
    value_heads = value_part.reshape(part_count, number, head_count, head_size)
    scores = jnp.einsum(
        "prhe,pnhe->phrn", query_heads, key_heads, preferred_element_type=jnp.float32
    )
    bias_part = pair_bias.astype(jnp.float32)
    scores = scores + bias_part[None]
    usable = (key_mask > 0)[None, None, None, :]
    new_max = jnp.maximum(running, jnp.max(jnp.where(usable, scores, -1e30), axis=3))
    weights = jnp.where(usable, jnp.exp(scores - new_max[..., None]), 0.0)
    totals = jnp.sum(weights, axis=3)
    summed = jnp.einsum(
        "phrn,pnhe->phre",
        weights.astype(jnp.bfloat16),
        value_heads,
        preferred_element_type=jnp.float32,
    )
    return (new_max, totals, summed)


def run_block(states, pair_bias, key_mask, gain_attn, w_qkv, w_o, gain_ff, w_in, w_out):
    part_count, row_count, model_width = states.shape
    head_count = pair_bias.shape[0]
    head_size = model_width // head_count
    score_scale = 1.0 / math.sqrt(head_size)
    stream = states.astype(jnp.float32)
    normed = rms_norm(stream, gain_attn).astype(jnp.bfloat16)
    start_carry = (
        jnp.full((part_count, head_count, row_count), -1e30, jnp.float32),
        jnp.zeros((part_count, head_count, row_count), jnp.float32),
        jnp.zeros((part_count, head_count, row_count, head_size), jnp.float32),
    )
    queries = (
        jnp.einsum(
            "prd,de->pre", normed, w_qkv[:, :model_width], preferred_element_type=jnp.float32
        )
        * score_scale
    ).astype(jnp.bfloat16)
    normed_all = lax.all_gather(normed, "token", axis=1, tiled=True)
    projected = jnp.einsum(
        "prd,de->pre", normed_all, w_qkv[:, model_width:], preferred_element_type=jnp.float32
    ).astype(jnp.bfloat16)
    portion = (projected[..., :model_width], projected[..., model_width:])
    running, totals, summed = attend_portion(
        start_carry, queries, portion[0], portion[1], pair_bias, key_mask
    )
    attended = (
        (summed / totals[..., None])
        .transpose(0, 2, 1, 3)
        .reshape(part_count, row_count, model_width)
        .astype(jnp.bfloat16)
    )
    stream = stream + jnp.einsum("prd,de->pre", attended, w_o, preferred_element_type=jnp.float32)
    normed_ff = rms_norm(stream, gain_ff).astype(jnp.bfloat16)
    normed_ff = lax.all_gather(normed_ff, "token", axis=1, tiled=True)
    gate_sum = jnp.einsum("prd,df->prf", normed_ff, w_in[0], preferred_element_type=jnp.float32)
    up_sum = jnp.einsum("prd,df->prf", normed_ff, w_in[1], preferred_element_type=jnp.float32)
    hidden = (jax.nn.silu(gate_sum) * up_sum).astype(jnp.bfloat16)
    update = jnp.einsum(
        "prf,nf->prn", hidden, w_out, preferred_element_type=jnp.float32
    ).astype(jnp.bfloat16)
    update = lax.psum_scatter(update, "token", scatter_dimension=1, tiled=True)
    return (stream + update.astype(jnp.float32)).astype(jnp.bfloat16)


def select_rows(ancestors, portion):
    number = portion.shape[0]
    indices = lax.iota(jnp.int32, number)
    onehot = (ancestors[:, None] == indices[None, :]).astype(jnp.bfloat16)
    return jnp.einsum("jp,prd->jrd", onehot, portion, preferred_element_type=jnp.float32)


def body(states, ancestors, pair_bias, key_mask, gain_attn, w_qkv, w_o, gain_ff, w_in, w_out):
    chosen = select_rows(ancestors, lax.all_gather(states, "particle", axis=0, tiled=True)).astype(
        jnp.bfloat16
    )
    units = w_out.shape[1] // lax.axis_size("token")
    first = lax.axis_index("token") * units
    w_in = lax.all_gather(
        lax.dynamic_slice_in_dim(w_in, first, units, 2), "particle", axis=1, tiled=True
    )
    w_out = lax.all_gather(
        lax.dynamic_slice_in_dim(w_out, first, units, 1), "particle", axis=0, tiled=True
    )
    return run_block(chosen, pair_bias, key_mask, gain_attn, w_qkv, w_o, gain_ff, w_in, w_out)


def block_kernel(
    states_ref, ancestors_ref, bias_hbm, mask_ref, gain_attn_ref, w_qkv_hbm, w_o_hbm, gain_ff_ref,
    w_in_hbm, w_out_hbm, out_ref,
    states_all, w_in_all, w_out_all, w_qkv, w_o, bias, normed_all, kv_all, ff_all,
    core_out, core_in, row_out, row_in, wish_out, wish_in, pick_out, pick_in,
    local_sem, recv_sem, right_sem, left_sem, across_sem, gather_recv, gather_row, gather_core,
    core_send, core_recv, row_send, row_recv, wish_send, wish_recv, pick_send, pick_recv,
):
    per, rows, width = states_ref.shape
    groups = lax.axis_size("particle")
    lines = groups // 2
    cells = lax.axis_size("token")
    spans = cells // 2
    units = w_in_all.shape[-1]
    head_count = bias.shape[0] // rows
    head_size = width // head_count
    me = lax.axis_index("particle")
    spot = lax.axis_index("token")
    line, side = me // 2, me % 2
    span, core = spot // 2, spot % 2
    across = (line * 2 + 1 - side, spot)
    above, below = (me + 2, spot), (me - 2, spot)
    other_core = (me, span * 2 + 1 - core)

    def span_peer(step):
        return lax.rem(span + step, spans)

    barrier = pltpu.get_barrier_semaphore()

    def greet(device):
        pl.semaphore_signal(barrier, inc=1, device_id=device, device_id_type=MESH)

    greet(across)
    greet(other_core)
    for step in range(1, spans):
        greet((me, span_peer(step) * 2 + core))

    @pl.when(line > 0)
    def _():
        greet(below)

    @pl.when(line < lines - 1)
    def _():
        greet(above)

    first = pl.multiple_of(spot * units, 128)
    locals_ = [
        pltpu.make_async_copy(states_ref, states_all.at[pl.ds(me * per, per)], local_sem.at[0]),
        pltpu.make_async_copy(
            w_in_hbm.at[:, :, pl.ds(first, units)], w_in_all.at[me], local_sem.at[1]
        ),
        pltpu.make_async_copy(
            w_out_hbm.at[:, pl.ds(first, units)], w_out_all.at[me], local_sem.at[2]
        ),
        pltpu.make_async_copy(w_qkv_hbm, w_qkv, local_sem.at[3]),
        pltpu.make_async_copy(bias_hbm, bias, local_sem.at[4]),
        pltpu.make_async_copy(w_o_hbm, w_o, local_sem.at[5]),
    ]
    for copy in locals_:
        copy.start()
    locals_[0].wait()
    pl.semaphore_wait(
        barrier,
        2 + spans - 1 + jnp.where(line > 0, 1, 0) + jnp.where(line < lines - 1, 1, 0),
    )

    views = (
        lambda k: states_all.at[pl.ds(k * per, per)],
        lambda k: w_in_all.at[k],
        lambda k: w_out_all.at[k],
    )

    def remote(kind, source, sems, device):
        k = source * 2 + side
        return pltpu.make_async_remote_copy(
            src_ref=views[kind](k),
            dst_ref=views[kind](k),
            send_sem=sems.at[kind, source],
            recv_sem=recv_sem.at[kind, k],
            device_id=device,
            device_id_type=MESH,
        )

    def arrived(kind, k):
        pltpu.make_async_remote_copy(
            src_ref=views[kind](k),
            dst_ref=views[kind](k),
            send_sem=across_sem.at[kind, 0],
            recv_sem=recv_sem.at[kind, k],
            device_id=across,
            device_id_type=MESH,
        ).wait_recv()

    def relay(kind, step, along=True, cross=True):
        low, high = line - step, line + step

        @pl.when(low >= 0)
        def _():
            if step > 0:
                arrived(kind, low * 2 + side)

            @pl.when(jnp.logical_and(along, line < lines - 1))
            def _():
                remote(kind, low, right_sem, above).start()

        @pl.when(high < lines)
        def _():
            if step > 0:
                arrived(kind, high * 2 + side)

            @pl.when(jnp.logical_and(along, line > 0))
            def _():
                remote(kind, high, left_sem, below).start()

        if kind == 0 or not cross:
            return

        @pl.when(low >= 0)
        def _():
            remote(kind, low, across_sem, across).start()

        if step > 0:

            @pl.when(high < lines)
            def _():
                remote(kind, high, across_sem, across).start()

    def finish(kind):
        for source in range(lines):
            arrived(kind, source * 2 + 1 - side)

    def drain(kind):
        for source in range(lines):
            if kind > 0:
                remote(kind, source, across_sem, across).wait_send()

            @pl.when(jnp.logical_and(line < lines - 1, source <= line))
            def _():
                remote(kind, source, right_sem, above).wait_send()

            @pl.when(jnp.logical_and(line > 0, source >= line))
            def _():
                remote(kind, source, left_sem, below).wait_send()

    def slot_copy(which, buf, j, slot, send, device):
        return pltpu.make_async_remote_copy(
            src_ref=buf.at[j, slot],
            dst_ref=buf.at[j, slot],
            send_sem=send,
            recv_sem=gather_recv.at[which, j, slot],
            device_id=device,
            device_id_type=MESH,
        )

    sent = []

    def token_sends(which, buf, j):
        for step in range(1, spans):
            device = (me, span_peer(step) * 2 + core)
            sent.append(slot_copy(which, buf, j, spot, gather_row.at[which, j, step], device))
            sent[-1].start()
        sent.append(slot_copy(which, buf, j, spot, gather_core.at[which, j, 0], other_core))
        sent[-1].start()

    def token_forward(which, buf, j):
        for step in range(1, spans):
            slot = span_peer(step) * 2 + core
            copy = slot_copy(which, buf, j, slot, gather_core.at[which, j, step], other_core)
            copy.wait_recv()
            copy.start()
            sent.append(copy)

    def token_finish(which, buf, j, steps=range(spans)):
        for step in steps:
            slot = span_peer(step) * 2 + 1 - core
            slot_copy(
                which, buf, j, slot, gather_core.at[which, j, 0], other_core
            ).wait_recv()

    def norm(stream, gain):
        mean = jnp.mean(stream * stream, axis=-1, keepdims=True)
        return (stream * lax.rsqrt(mean + 1e-05) * gain).astype(jnp.bfloat16)

    def dot(a, b):
        return jnp.dot(a, b, preferred_element_type=jnp.float32)

    def dot_t(a, b):
        return lax.dot_general(
            a, b, (((1,), (1,)), ((), ())), preferred_element_type=jnp.float32
        )

    tokens = cells * rows
    last = lines - 1
    for j in range(per):
        wish_out[j] = jnp.full(wish_out.shape[1:], ancestors_ref[j], jnp.int32)

    def to_across(source, target, send, recv):
        return pltpu.make_async_remote_copy(
            src_ref=source,
            dst_ref=target,
            send_sem=send,
            recv_sem=recv,
            device_id=across,
            device_id_type=MESH,
        )

    def own_weights_along(step):
        @pl.when(jnp.logical_and(line == step, line < last))
        def _():
            remote(1, line, right_sem, above).start()

        @pl.when(jnp.logical_and(line == last - step, line > 0))
        def _():
            remote(1, line, left_sem, below).start()

    wish = to_across(wish_out, wish_in, wish_send, wish_recv)
    wish.start()
    relay(0, 0)
    locals_[1].wait()
    relay(1, 0, along=False)
    locals_[2].wait()
    relay(2, 0, along=False)
    own_weights_along(0)
    wish.wait_recv()

    def pick_from(found, wished, source):
        for i in range(per):
            k = (source * 2 + side) * per + i
            found = jnp.where(wished[:1, :1] == k, states_all[k].astype(jnp.float32), found)
        return found

    nothing = jnp.zeros((rows, width), jnp.float32)
    asked = [pick_from(nothing, wish_in[j], line) for j in range(per)]
    for step in range(1, lines):
        relay(0, step)
        own_weights_along(step)
        for source in (jnp.maximum(line - step, 0), jnp.minimum(line + step, last)):
            if step < last:
                asked = [pick_from(asked[j], wish_in[j], source) for j in range(per)]
    picks = []
    for j in range(per):
        if last > 0:
            for source in (0, last):
                asked[j] = pick_from(asked[j], wish_in[j], source)
        pick_out[j] = asked[j].astype(jnp.bfloat16)
        picks.append(to_across(pick_out.at[j], pick_in.at[j], pick_send.at[j], pick_recv.at[j]))
        picks[j].start()
    own = []
    for j in range(per):
        found = nothing
        for source in range(lines):
            found = pick_from(found, wish_out[j], source)
        own.append(found)
    if lines > 1:
        relay(1, 1)

    gain = gain_attn_ref[...].reshape(1, width)
    streams, normed = [], []
    for j in range(per):
        picks[j].wait_recv()
        streams.append(own[j] + pick_in[j].astype(jnp.float32))
        normed.append(norm(streams[j], gain))
        normed_all[j, spot] = normed[j]
        token_sends(0, normed_all, j)
    locals_[3].wait()

    def make_span_keys(j, step):
        start = span_peer(step) * 2
        kv_all[j, pl.ds(pl.multiple_of(start * rows, 2 * rows), 2 * rows)] = dot(
            normed_all[j, pl.ds(start, 2)].reshape(2 * rows, width), w_qkv[:, width:]
        ).astype(jnp.bfloat16)

    scale = 1.0 / math.sqrt(head_size)
    queries = (dot(jnp.concatenate(normed, axis=0), w_qkv[:, :width]) * scale).astype(jnp.bfloat16)
    token_finish(0, normed_all, 0, range(1))
    make_span_keys(0, 0)
    token_forward(0, normed_all, 0)
    for step in range(2, last):
        relay(1, step)
    relay(2, 0, cross=False)

    usable = mask_ref[...].reshape(1, -1) > 0
    half = 8
    strip = half * head_size
    lane = lax.broadcasted_iota(jnp.int32, (half, 1, strip), 2)
    head = lax.broadcasted_iota(jnp.int32, (half, 1, strip), 0)
    mine = jnp.logical_and(lane >= head * head_size, lane < (head + 1) * head_size)
    mine_f = mine.astype(jnp.float32)
    mine_bf = mine_f.astype(jnp.bfloat16)

    def make_keys(j):
        kv_all[j] = dot(normed_all[j].reshape(tokens, width), w_qkv[:, width:]).astype(
            jnp.bfloat16
        )

    def attend(j):
        strips = []
        for part in range(head_count // half):
            low, high = part * strip, (part + 1) * strip
            q = queries[j * rows : (j + 1) * rows, low:high]
            spread = (q[None] * mine_bf).reshape(half * rows, strip)
            scores = dot_t(spread, kv_all[j, :, low:high]) + bias[
                part * half * rows : (part + 1) * half * rows, :
            ].astype(jnp.float32)
            scores = jnp.where(usable, scores, -1e30)
            weights = jnp.exp(scores - jnp.max(scores, axis=1, keepdims=True))
            total = jnp.sum(weights, axis=1, keepdims=True)
            mix = dot(weights.astype(jnp.bfloat16), kv_all[j, :, width + low : width + high])
            mix = mix * (1.0 / total)
            strips.append(jnp.sum(mix.reshape(half, rows, strip) * mine_f, axis=0))
        return jnp.concatenate(strips, axis=1).astype(jnp.bfloat16)

    def close(j, attended):
        streams[j] = streams[j] + dot(attended, w_o[...])
        ff_all[j, spot] = norm(streams[j], gain_ff_ref[...].reshape(1, width))
        token_sends(1, ff_all, j)

    token_finish(0, normed_all, 0, range(1, spans))
    for step in range(1, spans):
        make_span_keys(0, step)
    for j in range(1, per):
        token_forward(0, normed_all, j)
    locals_[4].wait()
    attended = attend(0)
    locals_[5].wait()
    close(0, attended)
    if lines > 2:
        relay(1, last)
    if lines > 1:
        relay(2, 1)
    for j in range(1, per):
        token_finish(0, normed_all, j)
        make_keys(j)
        if j == 1:
            for step in range(2, last):
                relay(2, step)
        attended = attend(j)
        token_forward(1, ff_all, j - 1)
        close(j, attended)
    finish(1)

    is_low = core == 0
    cored, rowed = [], []

    def to_core(j, spans_of, sem):
        return pltpu.make_async_remote_copy(
            src_ref=core_out.at[j, spans_of],
            dst_ref=core_in.at[j, spans_of],
            send_sem=core_send.at[j, sem],
            recv_sem=core_recv.at[j, sem],
            device_id=other_core,
            device_id_type=MESH,
        )

    def to_row(j, step):
        return pltpu.make_async_remote_copy(
            src_ref=row_out.at[j, span_peer(step)],
            dst_ref=row_in.at[j, step],
            send_sem=row_send.at[j, step],
            recv_sem=row_recv.at[j, step],
            device_id=(me, span_peer(step) * 2 + core),
            device_id_type=MESH,
        )

    def transition_in(normed_ff):
        gate = dot(normed_ff, w_in_all[:, 0].reshape(width, units))
        up = dot(normed_ff, w_in_all[:, 1].reshape(width, units))
        return (gate / (1.0 + jnp.exp(-gate)) * up).astype(jnp.bfloat16)

    def transition_out(j, spans_of, count, sem, hidden):
        update = dot_t(hidden, w_out_all[...].reshape(width, units))
        update = update.reshape(count, 2, rows, width)
        core_out[j, spans_of] = jnp.where(is_low, update[:, 1], update[:, 0]).astype(jnp.bfloat16)
        cored.append(to_core(j, spans_of, sem))
        cored[-1].start()
        return cored[-1], jnp.where(is_low, update[:, 0], update[:, 1])

    def add_core(j, spans_of, copy, kept):
        copy.wait_recv()
        row_out[j, spans_of] = (kept + core_in[j, spans_of].astype(jnp.float32)).astype(
            jnp.bfloat16
        )

    def send_row(j, step):
        rowed.append(to_row(j, step))
        rowed[-1].start()

    def span_transition(j, step):
        at = span_peer(step)
        normed_ff = ff_all[j, pl.ds(at * 2, 2)].reshape(2 * rows, width)
        return transition_out(j, pl.ds(at, 1), 1, step, transition_in(normed_ff))

    whole = pl.ds(0, spans)
    waiting = []
    for j in range(per - 1):
        token_finish(1, ff_all, j)
        hidden = transition_in(ff_all[j].reshape(tokens, width))
        if j == 0:
            if lines > 2:
                relay(2, last)
            finish(2)
        waiting.append(transition_out(j, whole, spans, 0, hidden))
    final = per - 1
    token_finish(1, ff_all, final, range(1))
    near = span_transition(final, 0)
    token_forward(1, ff_all, final)
    for j in range(final):
        add_core(j, whole, *waiting[j])
        for step in range(1, spans):
            send_row(j, step)
    token_finish(1, ff_all, final, range(1, spans))
    far = [span_transition(final, step) for step in range(1, spans)]
    for step, item in enumerate(far, 1):
        add_core(final, pl.ds(span_peer(step), 1), *item)
        send_row(final, step)
    add_core(final, pl.ds(span, 1), *near)
    for j in range(per):
        stream = streams[j] + row_out[j, span].astype(jnp.float32)
        for step in range(1, spans):
            to_row(j, step).wait_recv()
            stream = stream + row_in[j, step].astype(jnp.float32)
        out_ref[j] = stream.astype(jnp.bfloat16)
    for copy in sent + cored + rowed + [wish] + picks:
        copy.wait_send()
    for kind in range(3):
        drain(kind)


def fused_body(
    states, ancestors, pair_bias, key_mask, gain_attn, w_qkv, w_o, gain_ff, w_in, w_out
):
    per, rows, width = states.shape
    groups, cells = lax.axis_size("particle"), lax.axis_size("token")
    lines, spans = groups // 2, cells // 2
    units = w_out.shape[1] // cells
    depth = w_in.shape[1]
    heads, _, keys = pair_bias.shape
    vmem = pl.BlockSpec(memory_space=pltpu.VMEM)
    smem = pl.BlockSpec(memory_space=pltpu.SMEM)
    hbm = pl.BlockSpec(memory_space=pl.ANY)
    dma = pltpu.SemaphoreType.DMA
    bf16 = jnp.bfloat16
    block = (rows, width)
    return pl.pallas_call(
        block_kernel,
        out_shape=jax.ShapeDtypeStruct(states.shape, bf16),
        in_specs=[vmem, smem, hbm, vmem, vmem, hbm, hbm, vmem, hbm, hbm],
        out_specs=vmem,
        scratch_shapes=[
            pltpu.VMEM((groups * per, rows, width), bf16),
            pltpu.VMEM((groups, 2, depth, units), bf16),
            pltpu.VMEM((groups, depth, units), bf16),
            pltpu.VMEM(w_qkv.shape, bf16),
            pltpu.VMEM(w_o.shape, bf16),
            pltpu.VMEM((heads * rows, keys), bf16),
            pltpu.VMEM((per, cells) + block, bf16),
            pltpu.VMEM((per, cells * rows, 2 * width), bf16),
            pltpu.VMEM((per, cells) + block, bf16),
            pltpu.VMEM((per, spans) + block, bf16),
            pltpu.VMEM((per, spans) + block, bf16),
            pltpu.VMEM((per, spans) + block, bf16),
            pltpu.VMEM((per, spans) + block, bf16),
            pltpu.VMEM((per, 8, 128), jnp.int32),
            pltpu.VMEM((per, 8, 128), jnp.int32),
            pltpu.VMEM((per, rows, width), bf16),
            pltpu.VMEM((per, rows, width), bf16),
            dma((6,)),
            dma((3, groups)),
            dma((3, lines)),
            dma((3, lines)),
            dma((3, lines)),
            dma((2, per, cells)),
            dma((2, per, spans)),
            dma((2, per, spans)),
            dma((per, spans)),
            dma((per, spans)),
            dma((per, spans)),
            dma((per, spans)),
            dma,
            dma,
            dma((per,)),
            dma((per,)),
        ],
        compiler_params=pltpu.CompilerParams(
            collective_id=0, has_side_effects=True, vmem_limit_bytes=56 * 1024 * 1024
        ),
    )(
        states,
        ancestors,
        pair_bias.reshape(heads * rows, keys),
        key_mask,
        gain_attn,
        w_qkv,
        w_o,
        gain_ff,
        w_in,
        w_out,
    )


def either_body(states, ancestors, pair_bias, key_mask, gain_attn, w_qkv, w_o, gain_ff, w_in, w_out):
    tiles = w_in.shape[1] % 16 == 0 and (w_out.shape[1] // lax.axis_size("token")) % 128 == 0
    run = fused_body if tiles else body
    return run(
        states, ancestors, pair_bias, key_mask, gain_attn, w_qkv, w_o, gain_ff, w_in, w_out
    )


def solution(mesh):
    placed = (
        P("particle", "token", None),
        P("particle"),
        P(None, "token", None),
        P(),
        P(),
        P(),
        P(),
        P(),
        P(None, "particle", None),
        P("particle", None),
    )
    return jax.shard_map(
        either_body, mesh=mesh, in_specs=placed, out_specs=P("particle", "token", None), check_vma=False
    )
```

```python
import math

import jax
import jax.numpy as jnp
from jax import lax
from jax.experimental import pallas as pl
from jax.experimental.pallas import tpu as pltpu
from jax.sharding import PartitionSpec as P

MESH = pl.DeviceIdType.MESH


def rms_norm(stream, gain_vec):
    return stream * lax.rsqrt(jnp.mean(stream * stream, axis=-1, keepdims=True) + 1e-05) * gain_vec


def attend_portion(running_sum, queries, key_part, value_part, pair_bias, key_mask):
    running, totals, summed = running_sum
    part_count, row_count, model_width = queries.shape
    head_count = pair_bias.shape[0]
    head_size = model_width // head_count
    number = key_part.shape[1]
    query_heads = queries.reshape(part_count, row_count, head_count, head_size)
    key_heads = key_part.reshape(part_count, number, head_count, head_size)
    value_heads = value_part.reshape(part_count, number, head_count, head_size)
    scores = jnp.einsum(
        "prhe,pnhe->phrn", query_heads, key_heads, preferred_element_type=jnp.float32
    )
    bias_part = pair_bias.astype(jnp.float32)
    scores = scores + bias_part[None]
    usable = (key_mask > 0)[None, None, None, :]
    new_max = jnp.maximum(running, jnp.max(jnp.where(usable, scores, -1e30), axis=3))
    weights = jnp.where(usable, jnp.exp(scores - new_max[..., None]), 0.0)
    totals = jnp.sum(weights, axis=3)
    summed = jnp.einsum(
        "phrn,pnhe->phre",
        weights.astype(jnp.bfloat16),
        value_heads,
        preferred_element_type=jnp.float32,
    )
    return (new_max, totals, summed)


def run_block(states, pair_bias, key_mask, gain_attn, w_qkv, w_o, gain_ff, w_in, w_out):
    part_count, row_count, model_width = states.shape
    head_count = pair_bias.shape[0]
    head_size = model_width // head_count
    score_scale = 1.0 / math.sqrt(head_size)
    stream = states.astype(jnp.float32)
    normed = rms_norm(stream, gain_attn).astype(jnp.bfloat16)
    start_carry = (
        jnp.full((part_count, head_count, row_count), -1e30, jnp.float32),
        jnp.zeros((part_count, head_count, row_count), jnp.float32),
        jnp.zeros((part_count, head_count, row_count, head_size), jnp.float32),
    )
    queries = (
        jnp.einsum(
            "prd,de->pre", normed, w_qkv[:, :model_width], preferred_element_type=jnp.float32
        )
        * score_scale
    ).astype(jnp.bfloat16)
    normed_all = lax.all_gather(normed, "token", axis=1, tiled=True)
    projected = jnp.einsum(
        "prd,de->pre", normed_all, w_qkv[:, model_width:], preferred_element_type=jnp.float32
    ).astype(jnp.bfloat16)
    portion = (projected[..., :model_width], projected[..., model_width:])
    running, totals, summed = attend_portion(
        start_carry, queries, portion[0], portion[1], pair_bias, key_mask
    )
    attended = (
        (summed / totals[..., None])
        .transpose(0, 2, 1, 3)
        .reshape(part_count, row_count, model_width)
        .astype(jnp.bfloat16)
    )
    stream = stream + jnp.einsum("prd,de->pre", attended, w_o, preferred_element_type=jnp.float32)
    normed_ff = rms_norm(stream, gain_ff).astype(jnp.bfloat16)
    normed_ff = lax.all_gather(normed_ff, "token", axis=1, tiled=True)
    gate_sum = jnp.einsum("prd,df->prf", normed_ff, w_in[0], preferred_element_type=jnp.float32)
    up_sum = jnp.einsum("prd,df->prf", normed_ff, w_in[1], preferred_element_type=jnp.float32)
    hidden = (jax.nn.silu(gate_sum) * up_sum).astype(jnp.bfloat16)
    update = jnp.einsum(
        "prf,nf->prn", hidden, w_out, preferred_element_type=jnp.float32
    ).astype(jnp.bfloat16)
    update = lax.psum_scatter(update, "token", scatter_dimension=1, tiled=True)
    return (stream + update.astype(jnp.float32)).astype(jnp.bfloat16)


def select_rows(ancestors, portion):
    number = portion.shape[0]
    indices = lax.iota(jnp.int32, number)
    onehot = (ancestors[:, None] == indices[None, :]).astype(jnp.bfloat16)
    return jnp.einsum("jp,prd->jrd", onehot, portion, preferred_element_type=jnp.float32)


def body(states, ancestors, pair_bias, key_mask, gain_attn, w_qkv, w_o, gain_ff, w_in, w_out):
    chosen = select_rows(ancestors, lax.all_gather(states, "particle", axis=0, tiled=True)).astype(
        jnp.bfloat16
    )
    units = w_out.shape[1] // lax.axis_size("token")
    first = lax.axis_index("token") * units
    w_in = lax.all_gather(
        lax.dynamic_slice_in_dim(w_in, first, units, 2), "particle", axis=1, tiled=True
    )
    w_out = lax.all_gather(
        lax.dynamic_slice_in_dim(w_out, first, units, 1), "particle", axis=0, tiled=True
    )
    return run_block(chosen, pair_bias, key_mask, gain_attn, w_qkv, w_o, gain_ff, w_in, w_out)


def block_kernel(
    states_ref, ancestors_ref, bias_hbm, mask_ref, gain_attn_ref, w_qkv_hbm, w_o_hbm, gain_ff_ref,
    w_in_hbm, w_out_hbm, out_ref,
    states_all, w_in_all, w_out_all, w_qkv, w_o, bias, normed_all, kv_all, ff_all,
    core_out, core_in, row_out, row_in, wish_out, wish_in, pick_out, pick_in,
    local_sem, recv_sem, right_sem, left_sem, across_sem, gather_recv, gather_row, gather_core,
    core_send, core_recv, row_send, row_recv, wish_send, wish_recv, pick_send, pick_recv,
):
    per, rows, width = states_ref.shape
    groups = lax.axis_size("particle")
    lines = groups // 2
    cells = lax.axis_size("token")
    spans = cells // 2
    units = w_in_all.shape[-1]
    head_count = bias.shape[0] // rows
    head_size = width // head_count
    me = lax.axis_index("particle")
    spot = lax.axis_index("token")
    line, side = me // 2, me % 2
    span, core = spot // 2, spot % 2
    across = (line * 2 + 1 - side, spot)
    above, below = (me + 2, spot), (me - 2, spot)
    other_core = (me, span * 2 + 1 - core)

    def span_peer(step):
        return lax.rem(span + step, spans)

    barrier = pltpu.get_barrier_semaphore()

    def greet(device):
        pl.semaphore_signal(barrier, inc=1, device_id=device, device_id_type=MESH)

    greet(across)
    greet(other_core)
    for step in range(1, spans):
        greet((me, span_peer(step) * 2 + core))

    @pl.when(line > 0)
    def _():
        greet(below)

    @pl.when(line < lines - 1)
    def _():
        greet(above)

    first = pl.multiple_of(spot * units, 128)
    locals_ = [
        pltpu.make_async_copy(states_ref, states_all.at[pl.ds(me * per, per)], local_sem.at[0]),
        pltpu.make_async_copy(
            w_in_hbm.at[:, :, pl.ds(first, units)], w_in_all.at[me], local_sem.at[1]
        ),
        pltpu.make_async_copy(
            w_out_hbm.at[:, pl.ds(first, units)], w_out_all.at[me], local_sem.at[2]
        ),
        pltpu.make_async_copy(w_qkv_hbm, w_qkv, local_sem.at[3]),
        pltpu.make_async_copy(bias_hbm, bias, local_sem.at[4]),
        pltpu.make_async_copy(w_o_hbm, w_o, local_sem.at[5]),
    ]
    for copy in locals_:
        copy.start()
    locals_[0].wait()
    pl.semaphore_wait(
        barrier,
        2 + spans - 1 + jnp.where(line > 0, 1, 0) + jnp.where(line < lines - 1, 1, 0),
    )

    views = (
        lambda k: states_all.at[pl.ds(k * per, per)],
        lambda k: w_in_all.at[k],
        lambda k: w_out_all.at[k],
    )

    def remote(kind, source, sems, device):
        k = source * 2 + side
        return pltpu.make_async_remote_copy(
            src_ref=views[kind](k),
            dst_ref=views[kind](k),
            send_sem=sems.at[kind, source],
            recv_sem=recv_sem.at[kind, k],
            device_id=device,
            device_id_type=MESH,
        )

    def arrived(kind, k):
        pltpu.make_async_remote_copy(
            src_ref=views[kind](k),
            dst_ref=views[kind](k),
            send_sem=across_sem.at[kind, 0],
            recv_sem=recv_sem.at[kind, k],
            device_id=across,
            device_id_type=MESH,
        ).wait_recv()

    def relay(kind, step, along=True, cross=True):
        low, high = line - step, line + step

        @pl.when(low >= 0)
        def _():
            if step > 0:
                arrived(kind, low * 2 + side)

            @pl.when(jnp.logical_and(along, line < lines - 1))
            def _():
                remote(kind, low, right_sem, above).start()

        @pl.when(high < lines)
        def _():
            if step > 0:
                arrived(kind, high * 2 + side)

            @pl.when(jnp.logical_and(along, line > 0))
            def _():
                remote(kind, high, left_sem, below).start()

        if kind == 0 or not cross:
            return

        @pl.when(low >= 0)
        def _():
            remote(kind, low, across_sem, across).start()

        if step > 0:

            @pl.when(high < lines)
            def _():
                remote(kind, high, across_sem, across).start()

    def finish(kind):
        for source in range(lines):
            arrived(kind, source * 2 + 1 - side)

    def drain(kind):
        for source in range(lines):
            if kind > 0:
                remote(kind, source, across_sem, across).wait_send()

            @pl.when(jnp.logical_and(line < lines - 1, source <= line))
            def _():
                remote(kind, source, right_sem, above).wait_send()

            @pl.when(jnp.logical_and(line > 0, source >= line))
            def _():
                remote(kind, source, left_sem, below).wait_send()

    def slot_copy(which, buf, j, slot, send, device):
        return pltpu.make_async_remote_copy(
            src_ref=buf.at[j, slot],
            dst_ref=buf.at[j, slot],
            send_sem=send,
            recv_sem=gather_recv.at[which, j, slot],
            device_id=device,
            device_id_type=MESH,
        )

    sent = []

    def token_sends(which, buf, j):
        for step in range(1, spans):
            device = (me, span_peer(step) * 2 + core)
            sent.append(slot_copy(which, buf, j, spot, gather_row.at[which, j, step], device))
            sent[-1].start()
        sent.append(slot_copy(which, buf, j, spot, gather_core.at[which, j, 0], other_core))
        sent[-1].start()

    def token_forward(which, buf, j):
        for step in range(1, spans):
            slot = span_peer(step) * 2 + core
            copy = slot_copy(which, buf, j, slot, gather_core.at[which, j, step], other_core)
            copy.wait_recv()
            copy.start()
            sent.append(copy)

    def token_finish(which, buf, j, steps=range(spans)):
        for step in steps:
            slot = span_peer(step) * 2 + 1 - core
            slot_copy(
                which, buf, j, slot, gather_core.at[which, j, 0], other_core
            ).wait_recv()

    def norm(stream, gain):
        mean = jnp.mean(stream * stream, axis=-1, keepdims=True)
        return (stream * lax.rsqrt(mean + 1e-05) * gain).astype(jnp.bfloat16)

    def dot(a, b):
        return jnp.dot(a, b, preferred_element_type=jnp.float32)

    def dot_t(a, b):
        return lax.dot_general(
            a, b, (((1,), (1,)), ((), ())), preferred_element_type=jnp.float32
        )

    tokens = cells * rows
    last = lines - 1
    for j in range(per):
        wish_out[j] = jnp.full(wish_out.shape[1:], ancestors_ref[j], jnp.int32)

    def to_across(source, target, send, recv):
        return pltpu.make_async_remote_copy(
            src_ref=source,
            dst_ref=target,
            send_sem=send,
            recv_sem=recv,
            device_id=across,
            device_id_type=MESH,
        )

    def own_weights_along(step):
        @pl.when(jnp.logical_and(line == step, line < last))
        def _():
            remote(1, line, right_sem, above).start()
            remote(2, line, right_sem, above).start()

        @pl.when(jnp.logical_and(line == last - step, line > 0))
        def _():
            remote(1, line, left_sem, below).start()
            remote(2, line, left_sem, below).start()

    wish = to_across(wish_out, wish_in, wish_send, wish_recv)
    wish.start()
    relay(0, 0)
    locals_[1].wait()
    relay(1, 0, along=False)
    locals_[2].wait()
    relay(2, 0, along=False)
    own_weights_along(0)
    wish.wait_recv()

    def pick_from(found, wished, source):
        for i in range(per):
            k = (source * 2 + side) * per + i
            found = jnp.where(wished[:1, :1] == k, states_all[k].astype(jnp.float32), found)
        return found

    nothing = jnp.zeros((rows, width), jnp.float32)
    asked = [pick_from(nothing, wish_in[j], line) for j in range(per)]
    for step in range(1, lines):
        relay(0, step)
        own_weights_along(step)
        for source in (jnp.maximum(line - step, 0), jnp.minimum(line + step, last)):
            if step < last:
                asked = [pick_from(asked[j], wish_in[j], source) for j in range(per)]
    picks = []
    for j in range(per):
        if last > 0:
            for source in (0, last):
                asked[j] = pick_from(asked[j], wish_in[j], source)
        pick_out[j] = asked[j].astype(jnp.bfloat16)
        picks.append(to_across(pick_out.at[j], pick_in.at[j], pick_send.at[j], pick_recv.at[j]))
        picks[j].start()
    own = []
    for j in range(per):
        found = nothing
        for source in range(lines):
            found = pick_from(found, wish_out[j], source)
        own.append(found)
    if lines > 1:
        relay(1, 1)

    gain = gain_attn_ref[...].reshape(1, width)
    streams, normed = [], []
    for j in range(per):
        picks[j].wait_recv()
        streams.append(own[j] + pick_in[j].astype(jnp.float32))
        normed.append(norm(streams[j], gain))
        normed_all[j, spot] = normed[j]
        token_sends(0, normed_all, j)
    locals_[3].wait()

    def make_span_keys(j, step):
        start = span_peer(step) * 2
        kv_all[j, pl.ds(pl.multiple_of(start * rows, 2 * rows), 2 * rows)] = dot(
            normed_all[j, pl.ds(start, 2)].reshape(2 * rows, width), w_qkv[:, width:]
        ).astype(jnp.bfloat16)

    scale = 1.0 / math.sqrt(head_size)
    queries = (dot(jnp.concatenate(normed, axis=0), w_qkv[:, :width]) * scale).astype(jnp.bfloat16)
    token_finish(0, normed_all, 0, range(1))
    make_span_keys(0, 0)
    token_forward(0, normed_all, 0)
    if lines > 1:
        relay(2, 1)
    for step in range(2, last):
        relay(1, step)

    usable = mask_ref[...].reshape(1, -1) > 0
    half = 8
    strip = half * head_size
    lane = lax.broadcasted_iota(jnp.int32, (half, 1, strip), 2)
    head = lax.broadcasted_iota(jnp.int32, (half, 1, strip), 0)
    mine = jnp.logical_and(lane >= head * head_size, lane < (head + 1) * head_size)
    mine_f = mine.astype(jnp.float32)
    mine_bf = mine_f.astype(jnp.bfloat16)

    def make_keys(j):
        kv_all[j] = dot(normed_all[j].reshape(tokens, width), w_qkv[:, width:]).astype(
            jnp.bfloat16
        )

    def attend(j):
        strips = []
        for part in range(head_count // half):
            low, high = part * strip, (part + 1) * strip
            q = queries[j * rows : (j + 1) * rows, low:high]
            spread = (q[None] * mine_bf).reshape(half * rows, strip)
            scores = dot_t(spread, kv_all[j, :, low:high]) + bias[
                part * half * rows : (part + 1) * half * rows, :
            ].astype(jnp.float32)
            scores = jnp.where(usable, scores, -1e30)
            weights = jnp.exp(scores - jnp.max(scores, axis=1, keepdims=True))
            total = jnp.sum(weights, axis=1, keepdims=True)
            mix = dot(weights.astype(jnp.bfloat16), kv_all[j, :, width + low : width + high])
            mix = mix * (1.0 / total)
            strips.append(jnp.sum(mix.reshape(half, rows, strip) * mine_f, axis=0))
        return jnp.concatenate(strips, axis=1).astype(jnp.bfloat16)

    def close(j, attended):
        streams[j] = streams[j] + dot(attended, w_o[...])
        ff_all[j, spot] = norm(streams[j], gain_ff_ref[...].reshape(1, width))
        token_sends(1, ff_all, j)

    token_finish(0, normed_all, 0, range(1, spans))
    for step in range(1, spans):
        make_span_keys(0, step)
    for j in range(1, per):
        token_forward(0, normed_all, j)
    for step in range(2, last):
        relay(2, step)
    locals_[4].wait()
    attended = attend(0)
    locals_[5].wait()
    close(0, attended)
    if lines > 2:
        relay(1, last)
    for j in range(1, per):
        token_finish(0, normed_all, j)
        make_keys(j)
        if j == 1 and lines > 2:
            relay(2, last)
        attended = attend(j)
        token_forward(1, ff_all, j - 1)
        close(j, attended)
    finish(1)

    is_low = core == 0
    kept, cored, rowed = [], [], []

    def to_core(j):
        return pltpu.make_async_remote_copy(
            src_ref=core_out.at[j],
            dst_ref=core_in.at[j],
            send_sem=core_send.at[j],
            recv_sem=core_recv.at[j],
            device_id=other_core,
            device_id_type=MESH,
        )

    def to_row(j, step):
        return pltpu.make_async_remote_copy(
            src_ref=row_out.at[j, span_peer(step)],
            dst_ref=row_in.at[j, step],
            send_sem=row_send.at[j, step],
            recv_sem=row_recv.at[j, step],
            device_id=(me, span_peer(step) * 2 + core),
            device_id_type=MESH,
        )

    def send_rows(j):
        cored[j].wait_recv()
        row_out[j] = (kept[j] + core_in[j].astype(jnp.float32)).astype(jnp.bfloat16)
        for step in range(1, spans):
            rowed.append(to_row(j, step))
            rowed[-1].start()

    for j in range(per):
        token_finish(1, ff_all, j)
        normed_ff = ff_all[j].reshape(tokens, width)
        gate = dot(normed_ff, w_in_all[:, 0].reshape(width, units))
        up = dot(normed_ff, w_in_all[:, 1].reshape(width, units))
        hidden = (gate / (1.0 + jnp.exp(-gate)) * up).astype(jnp.bfloat16)
        if j == 0:
            finish(2)
        if j + 1 == per - 1:
            token_forward(1, ff_all, per - 1)
        if j > 0:
            send_rows(j - 1)
        update = dot_t(hidden, w_out_all[...].reshape(width, units))
        update = update.reshape(spans, 2, rows, width)
        core_out[j] = jnp.where(is_low, update[:, 1], update[:, 0]).astype(jnp.bfloat16)
        cored.append(to_core(j))
        cored[j].start()
        kept.append(jnp.where(is_low, update[:, 0], update[:, 1]))
    send_rows(per - 1)
    for j in range(per):
        stream = streams[j] + row_out[j, span].astype(jnp.float32)
        for step in range(1, spans):
            to_row(j, step).wait_recv()
            stream = stream + row_in[j, step].astype(jnp.float32)
        out_ref[j] = stream.astype(jnp.bfloat16)
    for copy in sent + cored + rowed + [wish] + picks:
        copy.wait_send()
    for kind in range(3):
        drain(kind)


def fused_body(
    states, ancestors, pair_bias, key_mask, gain_attn, w_qkv, w_o, gain_ff, w_in, w_out
):
    per, rows, width = states.shape
    groups, cells = lax.axis_size("particle"), lax.axis_size("token")
    lines, spans = groups // 2, cells // 2
    units = w_out.shape[1] // cells
    depth = w_in.shape[1]
    heads, _, keys = pair_bias.shape
    vmem = pl.BlockSpec(memory_space=pltpu.VMEM)
    smem = pl.BlockSpec(memory_space=pltpu.SMEM)
    hbm = pl.BlockSpec(memory_space=pl.ANY)
    dma = pltpu.SemaphoreType.DMA
    bf16 = jnp.bfloat16
    block = (rows, width)
    return pl.pallas_call(
        block_kernel,
        out_shape=jax.ShapeDtypeStruct(states.shape, bf16),
        in_specs=[vmem, smem, hbm, vmem, vmem, hbm, hbm, vmem, hbm, hbm],
        out_specs=vmem,
        scratch_shapes=[
            pltpu.VMEM((groups * per, rows, width), bf16),
            pltpu.VMEM((groups, 2, depth, units), bf16),
            pltpu.VMEM((groups, depth, units), bf16),
            pltpu.VMEM(w_qkv.shape, bf16),
            pltpu.VMEM(w_o.shape, bf16),
            pltpu.VMEM((heads * rows, keys), bf16),
            pltpu.VMEM((per, cells) + block, bf16),
            pltpu.VMEM((per, cells * rows, 2 * width), bf16),
            pltpu.VMEM((per, cells) + block, bf16),
            pltpu.VMEM((per, spans) + block, bf16),
            pltpu.VMEM((per, spans) + block, bf16),
            pltpu.VMEM((per, spans) + block, bf16),
            pltpu.VMEM((per, spans) + block, bf16),
            pltpu.VMEM((per, 8, 128), jnp.int32),
            pltpu.VMEM((per, 8, 128), jnp.int32),
            pltpu.VMEM((per, rows, width), bf16),
            pltpu.VMEM((per, rows, width), bf16),
            dma((6,)),
            dma((3, groups)),
            dma((3, lines)),
            dma((3, lines)),
            dma((3, lines)),
            dma((2, per, cells)),
            dma((2, per, spans)),
            dma((2, per, spans)),
            dma((per,)),
            dma((per,)),
            dma((per, spans)),
            dma((per, spans)),
            dma,
            dma,
            dma((per,)),
            dma((per,)),
        ],
        compiler_params=pltpu.CompilerParams(
            collective_id=0, has_side_effects=True, vmem_limit_bytes=56 * 1024 * 1024
        ),
    )(
        states,
        ancestors,
        pair_bias.reshape(heads * rows, keys),
        key_mask,
        gain_attn,
        w_qkv,
        w_o,
        gain_ff,
        w_in,
        w_out,
    )


def either_body(states, ancestors, pair_bias, key_mask, gain_attn, w_qkv, w_o, gain_ff, w_in, w_out):
    tiles = w_in.shape[1] % 16 == 0 and (w_out.shape[1] // lax.axis_size("token")) % 128 == 0
    run = fused_body if tiles else body
    return run(
        states, ancestors, pair_bias, key_mask, gain_attn, w_qkv, w_o, gain_ff, w_in, w_out
    )


def solution(mesh):
    placed = (
        P("particle", "token", None),
        P("particle"),
        P(None, "token", None),
        P(),
        P(),
        P(),
        P(),
        P(),
        P(None, "particle", None),
        P("particle", None),
    )
    return jax.shard_map(
        either_body, mesh=mesh, in_specs=placed, out_specs=P("particle", "token", None), check_vma=False
    )
```

```python
import math

import jax
import jax.numpy as jnp
from jax import lax
from jax.experimental import pallas as pl
from jax.experimental.pallas import tpu as pltpu
from jax.sharding import PartitionSpec as P

MESH = pl.DeviceIdType.MESH


def rms_norm(stream, gain_vec):
    return stream * lax.rsqrt(jnp.mean(stream * stream, axis=-1, keepdims=True) + 1e-05) * gain_vec


def attend_portion(running_sum, queries, key_part, value_part, pair_bias, key_mask):
    running, totals, summed = running_sum
    part_count, row_count, model_width = queries.shape
    head_count = pair_bias.shape[0]
    head_size = model_width // head_count
    number = key_part.shape[1]
    query_heads = queries.reshape(part_count, row_count, head_count, head_size)
    key_heads = key_part.reshape(part_count, number, head_count, head_size)
    value_heads = value_part.reshape(part_count, number, head_count, head_size)
    scores = jnp.einsum(
        "prhe,pnhe->phrn", query_heads, key_heads, preferred_element_type=jnp.float32
    )
    bias_part = pair_bias.astype(jnp.float32)
    scores = scores + bias_part[None]
    usable = (key_mask > 0)[None, None, None, :]
    new_max = jnp.maximum(running, jnp.max(jnp.where(usable, scores, -1e30), axis=3))
    weights = jnp.where(usable, jnp.exp(scores - new_max[..., None]), 0.0)
    totals = jnp.sum(weights, axis=3)
    summed = jnp.einsum(
        "phrn,pnhe->phre",
        weights.astype(jnp.bfloat16),
        value_heads,
        preferred_element_type=jnp.float32,
    )
    return (new_max, totals, summed)


def run_block(states, pair_bias, key_mask, gain_attn, w_qkv, w_o, gain_ff, w_in, w_out):
    part_count, row_count, model_width = states.shape
    head_count = pair_bias.shape[0]
    head_size = model_width // head_count
    score_scale = 1.0 / math.sqrt(head_size)
    stream = states.astype(jnp.float32)
    normed = rms_norm(stream, gain_attn).astype(jnp.bfloat16)
    start_carry = (
        jnp.full((part_count, head_count, row_count), -1e30, jnp.float32),
        jnp.zeros((part_count, head_count, row_count), jnp.float32),
        jnp.zeros((part_count, head_count, row_count, head_size), jnp.float32),
    )
    queries = (
        jnp.einsum(
            "prd,de->pre", normed, w_qkv[:, :model_width], preferred_element_type=jnp.float32
        )
        * score_scale
    ).astype(jnp.bfloat16)
    normed_all = lax.all_gather(normed, "token", axis=1, tiled=True)
    projected = jnp.einsum(
        "prd,de->pre", normed_all, w_qkv[:, model_width:], preferred_element_type=jnp.float32
    ).astype(jnp.bfloat16)
    portion = (projected[..., :model_width], projected[..., model_width:])
    running, totals, summed = attend_portion(
        start_carry, queries, portion[0], portion[1], pair_bias, key_mask
    )
    attended = (
        (summed / totals[..., None])
        .transpose(0, 2, 1, 3)
        .reshape(part_count, row_count, model_width)
        .astype(jnp.bfloat16)
    )
    stream = stream + jnp.einsum("prd,de->pre", attended, w_o, preferred_element_type=jnp.float32)
    normed_ff = rms_norm(stream, gain_ff).astype(jnp.bfloat16)
    normed_ff = lax.all_gather(normed_ff, "token", axis=1, tiled=True)
    gate_sum = jnp.einsum("prd,df->prf", normed_ff, w_in[0], preferred_element_type=jnp.float32)
    up_sum = jnp.einsum("prd,df->prf", normed_ff, w_in[1], preferred_element_type=jnp.float32)
    hidden = (jax.nn.silu(gate_sum) * up_sum).astype(jnp.bfloat16)
    update = jnp.einsum(
        "prf,nf->prn", hidden, w_out, preferred_element_type=jnp.float32
    ).astype(jnp.bfloat16)
    update = lax.psum_scatter(update, "token", scatter_dimension=1, tiled=True)
    return (stream + update.astype(jnp.float32)).astype(jnp.bfloat16)


def select_rows(ancestors, portion):
    number = portion.shape[0]
    indices = lax.iota(jnp.int32, number)
    onehot = (ancestors[:, None] == indices[None, :]).astype(jnp.bfloat16)
    return jnp.einsum("jp,prd->jrd", onehot, portion, preferred_element_type=jnp.float32)


def body(states, ancestors, pair_bias, key_mask, gain_attn, w_qkv, w_o, gain_ff, w_in, w_out):
    chosen = select_rows(ancestors, lax.all_gather(states, "particle", axis=0, tiled=True)).astype(
        jnp.bfloat16
    )
    units = w_out.shape[1] // lax.axis_size("token")
    first = lax.axis_index("token") * units
    w_in = lax.all_gather(
        lax.dynamic_slice_in_dim(w_in, first, units, 2), "particle", axis=1, tiled=True
    )
    w_out = lax.all_gather(
        lax.dynamic_slice_in_dim(w_out, first, units, 1), "particle", axis=0, tiled=True
    )
    return run_block(chosen, pair_bias, key_mask, gain_attn, w_qkv, w_o, gain_ff, w_in, w_out)


def block_kernel(
    states_ref, ancestors_ref, bias_hbm, mask_ref, gain_attn_ref, w_qkv_hbm, w_o_hbm, gain_ff_ref,
    w_in_hbm, w_out_hbm, out_ref,
    states_all, w_in_all, w_out_all, w_qkv, w_o, bias, normed_all, kv_all, ff_all,
    core_out, core_in, row_out, row_in, wish_out, wish_in, pick_out, pick_in,
    local_sem, recv_sem, right_sem, left_sem, across_sem, gather_recv, gather_row, gather_core,
    core_send, core_recv, row_send, row_recv, wish_send, wish_recv, pick_send, pick_recv,
):
    per, rows, width = states_ref.shape
    groups = lax.axis_size("particle")
    lines = groups // 2
    cells = lax.axis_size("token")
    spans = cells // 2
    units = w_in_all.shape[-1]
    head_count = bias.shape[0] // rows
    head_size = width // head_count
    me = lax.axis_index("particle")
    spot = lax.axis_index("token")
    line, side = me // 2, me % 2
    span, core = spot // 2, spot % 2
    across = (line * 2 + 1 - side, spot)
    above, below = (me + 2, spot), (me - 2, spot)
    other_core = (me, span * 2 + 1 - core)

    def span_peer(step):
        return lax.rem(span + step, spans)

    barrier = pltpu.get_barrier_semaphore()

    def greet(device):
        pl.semaphore_signal(barrier, inc=1, device_id=device, device_id_type=MESH)

    greet(across)
    greet(other_core)
    for step in range(1, spans):
        greet((me, span_peer(step) * 2 + core))

    @pl.when(line > 0)
    def _():
        greet(below)

    @pl.when(line < lines - 1)
    def _():
        greet(above)

    first = pl.multiple_of(spot * units, 128)
    locals_ = [
        pltpu.make_async_copy(states_ref, states_all.at[pl.ds(me * per, per)], local_sem.at[0]),
        pltpu.make_async_copy(
            w_in_hbm.at[:, :, pl.ds(first, units)], w_in_all.at[me], local_sem.at[1]
        ),
        pltpu.make_async_copy(
            w_out_hbm.at[:, pl.ds(first, units)], w_out_all.at[me], local_sem.at[2]
        ),
        pltpu.make_async_copy(w_qkv_hbm, w_qkv, local_sem.at[3]),
        pltpu.make_async_copy(bias_hbm, bias, local_sem.at[4]),
        pltpu.make_async_copy(w_o_hbm, w_o, local_sem.at[5]),
    ]
    for copy in locals_:
        copy.start()
    locals_[0].wait()
    pl.semaphore_wait(
        barrier,
        2 + spans - 1 + jnp.where(line > 0, 1, 0) + jnp.where(line < lines - 1, 1, 0),
    )

    views = (
        lambda k: states_all.at[k * per],
        lambda k: w_in_all.at[k],
        lambda k: w_out_all.at[k],
    ) + tuple(lambda k, i=i: states_all.at[k * per + i] for i in range(1, per))
    state_kinds = (0,) + tuple(range(3, 2 + per))

    def remote(kind, source, sems, device):
        k = source * 2 + side
        return pltpu.make_async_remote_copy(
            src_ref=views[kind](k),
            dst_ref=views[kind](k),
            send_sem=sems.at[kind, source],
            recv_sem=recv_sem.at[kind, k],
            device_id=device,
            device_id_type=MESH,
        )

    def arrived(kind, k):
        pltpu.make_async_remote_copy(
            src_ref=views[kind](k),
            dst_ref=views[kind](k),
            send_sem=across_sem.at[kind, 0],
            recv_sem=recv_sem.at[kind, k],
            device_id=across,
            device_id_type=MESH,
        ).wait_recv()

    def relay(kind, step, along=True, cross=True):
        low, high = line - step, line + step

        @pl.when(low >= 0)
        def _():
            if step > 0:
                arrived(kind, low * 2 + side)

            @pl.when(jnp.logical_and(along, line < lines - 1))
            def _():
                remote(kind, low, right_sem, above).start()

        @pl.when(high < lines)
        def _():
            if step > 0:
                arrived(kind, high * 2 + side)

            @pl.when(jnp.logical_and(along, line > 0))
            def _():
                remote(kind, high, left_sem, below).start()

        if kind in state_kinds or not cross:
            return

        @pl.when(low >= 0)
        def _():
            remote(kind, low, across_sem, across).start()

        if step > 0:

            @pl.when(high < lines)
            def _():
                remote(kind, high, across_sem, across).start()

    def finish(kind):
        for source in range(lines):
            arrived(kind, source * 2 + 1 - side)

    def drain(kind):
        for source in range(lines):
            if kind not in state_kinds:
                remote(kind, source, across_sem, across).wait_send()

            @pl.when(jnp.logical_and(line < lines - 1, source <= line))
            def _():
                remote(kind, source, right_sem, above).wait_send()

            @pl.when(jnp.logical_and(line > 0, source >= line))
            def _():
                remote(kind, source, left_sem, below).wait_send()

    def slot_copy(which, buf, j, slot, send, device):
        return pltpu.make_async_remote_copy(
            src_ref=buf.at[j, slot],
            dst_ref=buf.at[j, slot],
            send_sem=send,
            recv_sem=gather_recv.at[which, j, slot],
            device_id=device,
            device_id_type=MESH,
        )

    sent = []

    def token_sends(which, buf, j):
        for step in range(1, spans):
            device = (me, span_peer(step) * 2 + core)
            sent.append(slot_copy(which, buf, j, spot, gather_row.at[which, j, step], device))
            sent[-1].start()
        sent.append(slot_copy(which, buf, j, spot, gather_core.at[which, j, 0], other_core))
        sent[-1].start()

    def token_forward(which, buf, j):
        for step in range(1, spans):
            slot = span_peer(step) * 2 + core
            copy = slot_copy(which, buf, j, slot, gather_core.at[which, j, step], other_core)
            copy.wait_recv()
            copy.start()
            sent.append(copy)

    def token_finish(which, buf, j, steps=range(spans)):
        for step in steps:
            slot = span_peer(step) * 2 + 1 - core
            slot_copy(
                which, buf, j, slot, gather_core.at[which, j, 0], other_core
            ).wait_recv()

    def norm(stream, gain):
        mean = jnp.mean(stream * stream, axis=-1, keepdims=True)
        return (stream * lax.rsqrt(mean + 1e-05) * gain).astype(jnp.bfloat16)

    def dot(a, b):
        return jnp.dot(a, b, preferred_element_type=jnp.float32)

    def dot_t(a, b):
        return lax.dot_general(
            a, b, (((1,), (1,)), ((), ())), preferred_element_type=jnp.float32
        )

    tokens = cells * rows
    last = lines - 1
    for j in range(per):
        wish_out[j] = jnp.full(wish_out.shape[1:], ancestors_ref[j], jnp.int32)

    def to_across(source, target, send, recv):
        return pltpu.make_async_remote_copy(
            src_ref=source,
            dst_ref=target,
            send_sem=send,
            recv_sem=recv,
            device_id=across,
            device_id_type=MESH,
        )

    def own_weights_along(step):
        @pl.when(jnp.logical_and(line == step, line < last))
        def _():
            remote(1, line, right_sem, above).start()
            remote(2, line, right_sem, above).start()

        @pl.when(jnp.logical_and(line == last - step, line > 0))
        def _():
            remote(1, line, left_sem, below).start()
            remote(2, line, left_sem, below).start()

    wish = to_across(wish_out, wish_in, wish_send, wish_recv)
    wish.start()
    for kind in state_kinds:
        relay(kind, 0)
    locals_[1].wait()
    relay(1, 0, along=False)
    locals_[2].wait()
    relay(2, 0, along=False)
    own_weights_along(0)
    wish.wait_recv()

    def pick_from(found, wished, source):
        for i in range(per):
            k = (source * 2 + side) * per + i
            found = jnp.where(wished[:1, :1] == k, states_all[k].astype(jnp.float32), found)
        return found

    nothing = jnp.zeros((rows, width), jnp.float32)
    asked = [pick_from(nothing, wish_in[j], line) for j in range(per)]
    for step in range(1, lines):
        for kind in state_kinds:
            relay(kind, step)
        own_weights_along(step)
        for source in (jnp.maximum(line - step, 0), jnp.minimum(line + step, last)):
            if step < last:
                asked = [pick_from(asked[j], wish_in[j], source) for j in range(per)]
    picks = []
    for j in range(per):
        if last > 0:
            for source in (0, last):
                asked[j] = pick_from(asked[j], wish_in[j], source)
        pick_out[j] = asked[j].astype(jnp.bfloat16)
        picks.append(to_across(pick_out.at[j], pick_in.at[j], pick_send.at[j], pick_recv.at[j]))
        picks[j].start()
    own = []
    for j in range(per):
        found = nothing
        for source in range(lines):
            found = pick_from(found, wish_out[j], source)
        own.append(found)
    if lines > 1:
        relay(1, 1)

    gain = gain_attn_ref[...].reshape(1, width)
    streams, normed = [], []
    for j in range(per):
        picks[j].wait_recv()
        streams.append(own[j] + pick_in[j].astype(jnp.float32))
        normed.append(norm(streams[j], gain))
        normed_all[j, spot] = normed[j]
        token_sends(0, normed_all, j)
    locals_[3].wait()

    def make_span_keys(j, step):
        start = span_peer(step) * 2
        kv_all[j, pl.ds(pl.multiple_of(start * rows, 2 * rows), 2 * rows)] = dot(
            normed_all[j, pl.ds(start, 2)].reshape(2 * rows, width), w_qkv[:, width:]
        ).astype(jnp.bfloat16)

    scale = 1.0 / math.sqrt(head_size)
    queries = (dot(jnp.concatenate(normed, axis=0), w_qkv[:, :width]) * scale).astype(jnp.bfloat16)
    token_finish(0, normed_all, 0, range(1))
    make_span_keys(0, 0)
    token_forward(0, normed_all, 0)
    if lines > 1:
        relay(2, 1)
    for step in range(2, last):
        relay(1, step)

    usable = mask_ref[...].reshape(1, -1) > 0
    half = 8
    strip = half * head_size
    lane = lax.broadcasted_iota(jnp.int32, (half, 1, strip), 2)
    head = lax.broadcasted_iota(jnp.int32, (half, 1, strip), 0)
    mine = jnp.logical_and(lane >= head * head_size, lane < (head + 1) * head_size)
    mine_f = mine.astype(jnp.float32)
    mine_bf = mine_f.astype(jnp.bfloat16)

    def make_keys(j):
        kv_all[j] = dot(normed_all[j].reshape(tokens, width), w_qkv[:, width:]).astype(
            jnp.bfloat16
        )

    def attend(j):
        strips = []
        for part in range(head_count // half):
            low, high = part * strip, (part + 1) * strip
            q = queries[j * rows : (j + 1) * rows, low:high]
            spread = (q[None] * mine_bf).reshape(half * rows, strip)
            scores = dot_t(spread, kv_all[j, :, low:high]) + bias[
                part * half * rows : (part + 1) * half * rows, :
            ].astype(jnp.float32)
            scores = jnp.where(usable, scores, -1e30)
            weights = jnp.exp(scores - jnp.max(scores, axis=1, keepdims=True))
            total = jnp.sum(weights, axis=1, keepdims=True)
            mix = dot(weights.astype(jnp.bfloat16), kv_all[j, :, width + low : width + high])
            mix = mix * (1.0 / total)
            strips.append(jnp.sum(mix.reshape(half, rows, strip) * mine_f, axis=0))
        return jnp.concatenate(strips, axis=1).astype(jnp.bfloat16)

    def close(j, attended):
        streams[j] = streams[j] + dot(attended, w_o[...])
        ff_all[j, spot] = norm(streams[j], gain_ff_ref[...].reshape(1, width))
        token_sends(1, ff_all, j)

    token_finish(0, normed_all, 0, range(1, spans))
    for step in range(1, spans):
        make_span_keys(0, step)
    for j in range(1, per):
        token_forward(0, normed_all, j)
    for step in range(2, last):
        relay(2, step)
    locals_[4].wait()
    attended = attend(0)
    locals_[5].wait()
    close(0, attended)
    if lines > 2:
        relay(1, last)
    for j in range(1, per):
        token_finish(0, normed_all, j)
        make_keys(j)
        if j == 1 and lines > 2:
            relay(2, last)
        attended = attend(j)
        token_forward(1, ff_all, j - 1)
        close(j, attended)
    finish(1)

    is_low = core == 0
    kept, cored, rowed = [], [], []

    def to_core(j):
        return pltpu.make_async_remote_copy(
            src_ref=core_out.at[j],
            dst_ref=core_in.at[j],
            send_sem=core_send.at[j],
            recv_sem=core_recv.at[j],
            device_id=other_core,
            device_id_type=MESH,
        )

    def to_row(j, step):
        return pltpu.make_async_remote_copy(
            src_ref=row_out.at[j, span_peer(step)],
            dst_ref=row_in.at[j, step],
            send_sem=row_send.at[j, step],
            recv_sem=row_recv.at[j, step],
            device_id=(me, span_peer(step) * 2 + core),
            device_id_type=MESH,
        )

    def send_rows(j):
        cored[j].wait_recv()
        row_out[j] = (kept[j] + core_in[j].astype(jnp.float32)).astype(jnp.bfloat16)
        for step in range(1, spans):
            rowed.append(to_row(j, step))
            rowed[-1].start()

    for j in range(per):
        token_finish(1, ff_all, j)
        normed_ff = ff_all[j].reshape(tokens, width)
        gate = dot(normed_ff, w_in_all[:, 0].reshape(width, units))
        up = dot(normed_ff, w_in_all[:, 1].reshape(width, units))
        hidden = (gate / (1.0 + jnp.exp(-gate)) * up).astype(jnp.bfloat16)
        if j == 0:
            finish(2)
        if j + 1 == per - 1:
            token_forward(1, ff_all, per - 1)
        if j > 0:
            send_rows(j - 1)
        update = dot_t(hidden, w_out_all[...].reshape(width, units))
        update = update.reshape(spans, 2, rows, width)
        core_out[j] = jnp.where(is_low, update[:, 1], update[:, 0]).astype(jnp.bfloat16)
        cored.append(to_core(j))
        cored[j].start()
        kept.append(jnp.where(is_low, update[:, 0], update[:, 1]))
    send_rows(per - 1)
    for j in range(per):
        stream = streams[j] + row_out[j, span].astype(jnp.float32)
        for step in range(1, spans):
            to_row(j, step).wait_recv()
            stream = stream + row_in[j, step].astype(jnp.float32)
        out_ref[j] = stream.astype(jnp.bfloat16)
    for copy in sent + cored + rowed + [wish] + picks:
        copy.wait_send()
    for kind in range(2 + per):
        drain(kind)


def fused_body(
    states, ancestors, pair_bias, key_mask, gain_attn, w_qkv, w_o, gain_ff, w_in, w_out
):
    per, rows, width = states.shape
    groups, cells = lax.axis_size("particle"), lax.axis_size("token")
    lines, spans = groups // 2, cells // 2
    units = w_out.shape[1] // cells
    depth = w_in.shape[1]
    heads, _, keys = pair_bias.shape
    vmem = pl.BlockSpec(memory_space=pltpu.VMEM)
    smem = pl.BlockSpec(memory_space=pltpu.SMEM)
    hbm = pl.BlockSpec(memory_space=pl.ANY)
    dma = pltpu.SemaphoreType.DMA
    bf16 = jnp.bfloat16
    block = (rows, width)
    return pl.pallas_call(
        block_kernel,
        out_shape=jax.ShapeDtypeStruct(states.shape, bf16),
        in_specs=[vmem, smem, hbm, vmem, vmem, hbm, hbm, vmem, hbm, hbm],
        out_specs=vmem,
        scratch_shapes=[
            pltpu.VMEM((groups * per, rows, width), bf16),
            pltpu.VMEM((groups, 2, depth, units), bf16),
            pltpu.VMEM((groups, depth, units), bf16),
            pltpu.VMEM(w_qkv.shape, bf16),
            pltpu.VMEM(w_o.shape, bf16),
            pltpu.VMEM((heads * rows, keys), bf16),
            pltpu.VMEM((per, cells) + block, bf16),
            pltpu.VMEM((per, cells * rows, 2 * width), bf16),
            pltpu.VMEM((per, cells) + block, bf16),
            pltpu.VMEM((per, spans) + block, bf16),
            pltpu.VMEM((per, spans) + block, bf16),
            pltpu.VMEM((per, spans) + block, bf16),
            pltpu.VMEM((per, spans) + block, bf16),
            pltpu.VMEM((per, 8, 128), jnp.int32),
            pltpu.VMEM((per, 8, 128), jnp.int32),
            pltpu.VMEM((per, rows, width), bf16),
            pltpu.VMEM((per, rows, width), bf16),
            dma((6,)),
            dma((2 + per, groups)),
            dma((2 + per, lines)),
            dma((2 + per, lines)),
            dma((2 + per, lines)),
            dma((2, per, cells)),
            dma((2, per, spans)),
            dma((2, per, spans)),
            dma((per,)),
            dma((per,)),
            dma((per, spans)),
            dma((per, spans)),
            dma,
            dma,
            dma((per,)),
            dma((per,)),
        ],
        compiler_params=pltpu.CompilerParams(
            collective_id=0, has_side_effects=True, vmem_limit_bytes=56 * 1024 * 1024
        ),
    )(
        states,
        ancestors,
        pair_bias.reshape(heads * rows, keys),
        key_mask,
        gain_attn,
        w_qkv,
        w_o,
        gain_ff,
        w_in,
        w_out,
    )


def either_body(states, ancestors, pair_bias, key_mask, gain_attn, w_qkv, w_o, gain_ff, w_in, w_out):
    tiles = w_in.shape[1] % 16 == 0 and (w_out.shape[1] // lax.axis_size("token")) % 128 == 0
    run = fused_body if tiles else body
    return run(
        states, ancestors, pair_bias, key_mask, gain_attn, w_qkv, w_o, gain_ff, w_in, w_out
    )


def solution(mesh):
    placed = (
        P("particle", "token", None),
        P("particle"),
        P(None, "token", None),
        P(),
        P(),
        P(),
        P(),
        P(),
        P(None, "particle", None),
        P("particle", None),
    )
    return jax.shard_map(
        either_body, mesh=mesh, in_specs=placed, out_specs=P("particle", "token", None), check_vma=False
    )
```
